512 devices in a mesh: row: 16 (over y, core), col: 32 (over x, z).
Axes of the slice: x: 4, y: 8, z: 8, core: 2. Of those that a mesh axis runs over, the one named last changes fastest.
Arguments:
- start_vector: float32 [100663296], P(('row', 'col')), may hold values from -8 to 8
- tile_blocks: bfloat16 [16, 32, 64, 128, 128], P('row', 'col'), may hold values from -0.5 to 0.5
- row_owner: int32 [16, 32, 64, 1], P('row', 'col'), may hold values from 0 to 31; in each aligned block of 64 rows (0 to 63, 64 to 127, ..., all dimensions but the last counted through in order) at most 4 rows name the same one
- row_block: int32 [16, 32, 64], P('row', 'col'), may hold values from 0 to 1535
- col_owner: int32 [16, 32, 64, 1], P('row', 'col'), may hold values from 0 to 15; in each aligned block of 64 rows (0 to 63, 64 to 127, ..., all dimensions but the last counted through in order) at most 8 rows name the same one
- col_block: int32 [16, 32, 64], P('row', 'col'), may hold values from 0 to 1535
- tile_counts: int32 [16, 32], P('row', 'col'), may hold values from 8 to 64, as said below
Outputs:
- lanczos_basis: float32 [2, 100663296], P(None, ('row', 'col'))
- start_alpha: float32 [1], replicated
- tridiagonal: float32 [3], replicated
The draws below stay inside these ranges and needn't reach their ends.
Inputs may be any that keep to these rules, and one draw needn't show every extreme that they name: `row_owner`: within the 64 slots of one grid position no value is named by more than 4 slots; some grid positions reach 4. `col_owner`: within the 64 slots of one grid position no value is named by more than 8 slots; some grid positions reach 8. `tile_counts`: at least one grid position has exactly 64 live tiles.
All inputs are finite; a program needn't handle non-finite values.
Results may differ from the reference program's by a relative error of at most 0.0023.
Values may be sent and summed in bfloat16 or wider, within the bound.
No kernel may reach another device: no remote copies, remote signals or barrier semaphores. Data moves between devices by JAX's collectives and lax.ppermute only.
A program may use at most 64 MiB of HBM per device.

```python
import math
import jax
import jax.numpy as jnp
import numpy as np
from jax import lax

TILE = 128
PB = 1536
MAXT = 64
ITERS = 2
CAPR = 4
CAPC = 8
NV = 100663296
N_ROW = 16
N_COL = 32


def draw_start_vector(key, part):
    key = jax.random.fold_in(key, 21)
    position = jnp.arange(NV).astype(jnp.float32) / float(NV)
    noise = jnp.clip(jax.random.normal(key, (NV,), jnp.float32), -4.0, 4.0)
    ramp = jnp.exp(0.5493 * position)
    return jnp.clip((1.0 + noise) * ramp, -8.0, 8.0)


def draw_tile_blocks(key, part):
    key = jax.random.fold_in(key, 31)
    shape = (N_ROW, N_COL, MAXT, TILE, TILE)
    noise = jnp.clip(jax.random.normal(key, shape, jnp.float32) * 0.0884, -0.4, 0.4)
    return jnp.clip(0.04 + noise, -0.5, 0.5).astype(jnp.bfloat16)


def draw_tile_counts(key, part):
    key = jax.random.fold_in(key, 11)
    first = jax.random.randint(jax.random.fold_in(key, 1), (N_ROW * N_COL,), 0, 8)
    second = jax.random.randint(jax.random.fold_in(key, 2), (N_ROW * N_COL,), 0, 8)
    third = jax.random.randint(jax.random.fold_in(key, 3), (N_ROW * N_COL,), 0, 8)
    lowest = max(1, MAXT // 8)
    filled = lowest + (MAXT - lowest) * (first * second * third) // 343
    chosen = jax.random.randint(jax.random.fold_in(key, 4), (), 0, N_ROW * N_COL)
    places = jnp.arange(N_ROW * N_COL)
    filled = jnp.where(places == chosen, MAXT, filled)
    return filled.reshape(N_ROW, N_COL).astype(jnp.int32)


def with_ends(values, rng, least, largest):
    spot = [jax.random.randint(jax.random.fold_in(rng, axis), (), 0, length) for axis, length in enumerate(values.shape)]
    widest = values.shape.index(max(values.shape))
    next_to = spot[:widest] + [(spot[widest] + 1) % values.shape[widest]] + spot[widest + 1:]
    return values.at[tuple(spot)].set(least).at[tuple(next_to)].set(largest)


def routed_block(own_key, own, number, rows, count, top, bound, slope):
    order = jax.random.permutation(own_key, count)
    packed, common = portions_of(count, rows * top, bound, slope, True), portions_of(count, rows * top, bound, slope, False)
    places = jnp.arange(count)

    def named(sizes, offset_by):
        used = int((sizes > 0).sum())
        fixed = max(1, used // 4)
        passed = fixed + (places - fixed + offset_by * (used - fixed)) % max(1, count - fixed)
        return jnp.zeros((count,), jnp.int32).at[order[jnp.where(places < fixed, places, passed)]].set(jnp.asarray(sizes, jnp.int32))

    sizes = jnp.where(number % 4 == 0, named(packed, number // 4), named(common, number - number // 4 - 1))
    mixed = jax.random.permutation(jax.random.fold_in(own, 3), count)
    donor, receiver = mixed[0:count // 2 * 2:2], mixed[1:count // 2 * 2:2]
    slack = jnp.minimum(sizes[donor] - 1, bound - sizes[receiver]) // 2
    slack = jnp.where((donor == order[0]) | (receiver == order[0]) | (sizes[receiver] == 0), 0, jnp.maximum(slack, 0))
    passed = jax.random.randint(jax.random.fold_in(own, 4), (count // 2,), 0, 1 << 20) % (slack + 1)
    sizes = sizes.at[donor].add(-passed).at[receiver].add(passed)
    members = jnp.searchsorted(jnp.cumsum(sizes), jnp.arange(rows * top), side="right").astype(jnp.int32)
    listing = members.reshape(top, rows).T
    listing = listing[jax.random.permutation(jax.random.fold_in(own, 1), rows)]
    offset_by = jax.random.randint(jax.random.fold_in(own, 2), (rows, 1), 0, top)
    return jnp.take_along_axis(listing, (jnp.arange(top)[None, :] + offset_by) % top, axis=1)


def portions_of(number_of, total, bound, slope, full):
    loads = [(1 << 20) // math.isqrt(rank ** slope) + 1 for rank in range(1, number_of + 1)]
    largest = bound if full else min(bound, max(-(-total // number_of), total * loads[0] // sum(loads)))
    least = 1 if total - largest >= number_of - 1 else 0
    holding, spare = [largest] + [least] * (number_of - 1), total - largest - least * (number_of - 1)
    while spare > 0:
        free = [i for i in range(1, number_of) if holding[i] < largest] or [i for i in range(1, number_of) if holding[i] < bound]
        whole, budget = sum([loads[i] for i in free]), spare
        for i in free:
            addition = min(bound - holding[i], max(1, budget * loads[i] // whole), spare)
            holding[i] = holding[i] + addition
            spare = spare - addition
    return np.array(holding)


def setup_inputs(seed: int = 0) -> dict:
    arg_keys = jax.random.split(jax.random.key(seed), 8)
    start_vector = draw_start_vector(jax.random.fold_in(arg_keys[7], 71), 0)
    tile_blocks = draw_tile_blocks(jax.random.fold_in(arg_keys[7], 71), 0)
    row_owner_keys = jax.random.split(jax.random.fold_in(arg_keys[2], 1), N_ROW * N_COL * MAXT // MAXT)
    row_owner_turns = jax.random.permutation(jax.random.fold_in(arg_keys[2], 3), N_ROW * N_COL * MAXT // MAXT)
    row_owner = jax.vmap(lambda own, number: routed_block(jax.random.fold_in(arg_keys[2], 2), own, number, MAXT, N_COL, 1, CAPR, 2))(row_owner_keys, row_owner_turns).reshape((N_ROW, N_COL, MAXT, 1))
    row_block = with_ends(jax.random.randint(arg_keys[3], (N_ROW, N_COL, MAXT), 0, PB), jax.random.fold_in(arg_keys[3], 1), 0, PB - 1).astype(jnp.int32)
    col_owner_keys = jax.random.split(jax.random.fold_in(arg_keys[4], 1), N_ROW * N_COL * MAXT // MAXT)
    col_owner_turns = jax.random.permutation(jax.random.fold_in(arg_keys[4], 3), N_ROW * N_COL * MAXT // MAXT)
    col_owner = jax.vmap(lambda own, number: routed_block(jax.random.fold_in(arg_keys[4], 2), own, number, MAXT, N_ROW, 1, CAPC, 2))(col_owner_keys, col_owner_turns).reshape((N_ROW, N_COL, MAXT, 1))
    col_block = with_ends(jax.random.randint(arg_keys[5], (N_ROW, N_COL, MAXT), 0, PB), jax.random.fold_in(arg_keys[5], 1), 0, PB - 1).astype(jnp.int32)
    tile_counts = draw_tile_counts(jax.random.fold_in(arg_keys[7], 71), 0)
    return dict(start_vector=start_vector, tile_blocks=tile_blocks, row_owner=row_owner, row_block=row_block, col_owner=col_owner, col_block=col_block, tile_counts=tile_counts)


def apply_hamiltonian(vector, tile_blocks, grow, gcol, live):
    nblk = vector.shape[0] // TILE
    narrow = vector.astype(jnp.bfloat16).reshape(nblk, TILE)

    def one_row(inputs):
        blocks, rows_here, cols_here, alive = inputs
        wide = blocks.astype(jnp.float32)
        direct = jnp.einsum('cmab,cmb->cma', wide, narrow[cols_here].astype(jnp.float32))
        mirror = jnp.einsum('cmab,cma->cmb', wide, narrow[rows_here].astype(jnp.float32))
        return (direct * alive[..., None], mirror * alive[..., None])
    direct, mirror = lax.map(one_row, (tile_blocks, grow, gcol, live))
    result = jnp.zeros((nblk, TILE), jnp.float32)
    result = result.at[grow.reshape(-1)].add(direct.reshape(-1, TILE))
    result = result.at[gcol.reshape(-1)].add(mirror.reshape(-1, TILE))
    return result.reshape(-1)

def reference(start_vector, tile_blocks, row_owner, row_block, col_owner, col_block, tile_counts):
    total = start_vector.shape[0]
    slots = jnp.arange(MAXT).astype(jnp.int32)
    live = (slots[None, None, :] < tile_counts[:, :, None]).astype(jnp.float32)
    row_index = jnp.arange(N_ROW).astype(jnp.int32)[:, None, None]
    col_index = jnp.arange(N_COL).astype(jnp.int32)[None, :, None]
    grow = ((row_index * N_COL + row_owner[..., 0]) * PB + row_block).astype(jnp.int32)
    gcol = ((col_owner[..., 0] * N_COL + col_index) * PB + col_block).astype(jnp.int32)
    energy = jnp.sum(start_vector * start_vector)
    current = start_vector / jnp.sqrt(energy / total + 1e-06)
    basis = [current]
    alphas = []
    betas = []
    for step in range(ITERS):
        image = apply_hamiltonian(basis[-1], tile_blocks, grow, gcol, live)
        correlations = jnp.stack([jnp.sum(older * image) for older in basis]) / total
        update = image
        for index in range(len(basis)):
            update = update - correlations[index] * basis[index]
        square = jnp.sum(update * update) / total
        norm_value = jnp.sqrt(square + 1e-06)
        basis.append(update / norm_value)
        alphas.append(correlations[-1])
        betas.append(norm_value)
    entries = [betas[0]]
    for index in range(1, ITERS):
        entries.append(alphas[index])
        entries.append(betas[index])
    return (jnp.stack(basis[1:]), jnp.stack([alphas[0]]), jnp.stack(entries))
```

```python
import jax
import jax.numpy as jnp
from jax import lax
from jax.experimental import pallas as pl
from jax.experimental.pallas import tpu as pltpu
from jax.sharding import PartitionSpec as P

TILE = 128
LANE = 8
HALF = 4
SCALE = 1024.0
F32 = jnp.float32
BF16 = jnp.bfloat16
VMEM = pl.BlockSpec(memory_space=pltpu.VMEM)
SMEM = pl.BlockSpec(memory_space=pltpu.SMEM)


def iota(shape, axis):
    return lax.broadcasted_iota(jnp.int32, shape, axis)


def halves(x):
    high = x.astype(BF16)
    low = (x - high.astype(F32)).astype(BF16)
    return high, low


def dot(a, b):
    return jnp.dot(a, b, preferred_element_type=F32)


def exact_dot(select, x):
    high, low = halves(x)
    return dot(select, high) + dot(select, low)


def place_of(owner):
    count = owner.shape[1]
    shape = (count, count)
    down, across = iota(shape, 0), iota(shape, 1)
    column = jnp.sum(jnp.where(down == across, owner, 0.0), axis=1, keepdims=True)
    same = column == owner
    rank_row = jnp.sum(jnp.where(same & (down < across), 1.0, 0.0), axis=0, keepdims=True)
    rank_column = jnp.sum(jnp.where(same & (across < down), 1.0, 0.0), axis=1, keepdims=True)
    return (owner * LANE + rank_row).astype(jnp.int32), (column * LANE + rank_column).astype(jnp.int32)


def request_kernel(own_r, blk_r, own_c, blk_c, filled, ask_row, ask_col, pick_row, put_row, pick_col, put_col):
    count = own_r.shape[1]
    alive = iota((1, count), 1) < filled[...]
    for owner, block, ask, pick, put, shift in (
        (own_c, blk_c, ask_row, pick_row, put_row, 0),
        (own_r, blk_r, ask_col, pick_col, put_col, HALF),
    ):
        width = ask.shape[0]
        across, down = place_of(owner[...].astype(F32))
        value = jnp.where(alive, block[...] + 1, 0).astype(F32)
        spot = iota((width, count), 0)
        there = spot == across
        back = spot == across + shift
        wanted = jnp.sum(jnp.where(there | back, value, 0.0), axis=1, keepdims=True) - 1.0
        ask[...] = jnp.broadcast_to(wanted, (width, TILE)).astype(jnp.int32)
        pick[...] = jnp.where(iota((count, width), 1) == down, 1.0, 0.0).astype(BF16)
        put[...] = jnp.where(back, 1.0, 0.0).astype(BF16)


def gather(asked, vector):
    pieces = vector.shape[0]
    rows = asked.shape[0]
    lanes = iota((rows, TILE), 1)
    select = jnp.concatenate(
        [jnp.where(asked == lanes + k * TILE, 1.0, 0.0).astype(BF16) for k in range(pieces // TILE)], axis=1
    )
    return exact_dot(select, vector)


def gather_kernel(asked, vector, out, energy):
    v = vector[...] * SCALE
    out[...] = gather(asked[...], v)
    energy[...] = jnp.sum((v * v).reshape(-1, 8, TILE), axis=0)


def product_lane(asked_row, asked_col):
    rows = [asked_row[...].astype(F32).T[0:1, :]]
    width = asked_col.shape[0]
    for k in range(width // TILE):
        part = asked_col[k * TILE : (k + 1) * TILE, :].astype(F32).T[0:1, :]
        lane = iota((1, TILE), 1)
        rows.append(jnp.where(lane % LANE >= HALF, part, -2.0))
    return [row.astype(jnp.int32) for row in rows]


def meet_kernel(asked_row, asked_col, vector, out, meet):
    out[...] = gather(asked_col[...], vector[...] * SCALE)
    lanes = product_lane(asked_row, asked_col)
    base = 0
    for asked in (asked_row, asked_col):
        mine = asked[...]
        for k, lane in enumerate(lanes):
            hit = (mine == lane) & (mine >= 0)
            meet[base : base + mine.shape[0], k * TILE : (k + 1) * TILE] = jnp.where(hit, 1.0, 0.0).astype(BF16)
        base += mine.shape[0]


def multiply(x, tiles, across):
    count = x.shape[0]
    dims = (((1,), (1 if across else 0,)), ((), ()))
    row = iota((8, TILE), 0)
    groups = []
    for g in range(count // 8):
        part = x[g * 8 : (g + 1) * 8, :]
        high = part.astype(BF16).astype(F32)
        both = jnp.concatenate([high, part - high], axis=0).astype(BF16)
        total = jnp.zeros((8, TILE), F32)
        for j in range(8):
            y = lax.dot_general(both, tiles[g * 8 + j], dims, preferred_element_type=F32)
            total = jnp.where(row == j, y[0:8] + y[8:16], total)
        groups.append(total)
    return jnp.concatenate(groups, axis=0)


def direct_kernel(got, pick, tiles, put, extra, out):
    y = multiply(exact_dot(pick[...], got[...]), tiles, True)
    forward = iota(extra.shape, 0) % LANE < HALF
    out[...] = exact_dot(put[...], y) + jnp.where(forward, extra[...], 0.0)


def mirror_kernel(got, pick, tiles, put, out):
    y = multiply(exact_dot(pick[...], got[...]), tiles, False)
    out[...] = exact_dot(put[...], y)


def sum_kernel(meet, back_row, back_col, out_row, out_col):
    total = exact_dot(meet[...], jnp.concatenate([back_row[...], back_col[...]], axis=0))
    width = out_row.shape[0]
    out_row[...] = total[:width]
    out_col[...] = total[width:]


def inner_kernel(
    meet, energy, v_row, v_col, i_row, i_col, first_row, first_col, second_row, second_col, out
):
    total = exact_dot(meet[...], jnp.concatenate([second_row[...], second_col[...]], axis=0))
    width = v_row.shape[0]
    returned = iota(v_col.shape, 0) % LANE >= HALF
    first_c = jnp.where(returned, first_col[...], 0.0)
    second_c = jnp.where(returned, second_col[...], 0.0)
    first_r, second_r = first_row[...], second_row[...]

    def inner(a_r, b_r, a_c, b_c):
        rows = jnp.sum(a_r * b_r, axis=0, keepdims=True) + jnp.sum(a_c * b_c, axis=0, keepdims=True)
        return jnp.sum(rows, axis=1, keepdims=True)

    values = [
        jnp.sum(jnp.sum(energy[...], axis=0, keepdims=True), axis=1, keepdims=True),
        inner(v_row[...], first_r, v_col[...], first_c),
        inner(i_row[...], first_r, i_col[...], first_c),
        inner(v_row[...], second_r, v_col[...], second_c),
        inner(i_row[...], second_r, i_col[...], second_c),
        inner(total[:width], second_r, total[width:], second_c),
    ]
    lane = iota((1, TILE), 1)
    packed = jnp.zeros((1, TILE), F32)
    for k, value in enumerate(values):
        packed = jnp.where(lane == k, value, packed)
    out[...] = jnp.broadcast_to(packed, out.shape)


def partial_kernel(got, out):
    total = jnp.sum(got[...], axis=0, keepdims=True) * (1.0 / LANE)
    out[...] = jnp.broadcast_to(total, out.shape)


def spread_kernel(asked_row, asked_col, back_row, back_col, out):
    lanes = jnp.concatenate(product_lane(asked_row, asked_col), axis=1)
    high, low = halves(jnp.concatenate([back_row[...], back_col[...]], axis=0))
    step = 256
    for start in range(0, out.shape[0], step):
        place = iota((step, lanes.shape[1]), 0) + start
        select = jnp.where(place == lanes, 1.0, 0.0).astype(BF16)
        out[start : start + step, :] = dot(select, high) + dot(select, low)


def final_kernel(total, got, vector, image, second, out, alpha, rest):
    sums = jnp.sum(got[...], axis=0, keepdims=True) * (1.0 / LANE)
    lane = iota((1, TILE), 1)

    def value(k):
        return jnp.sum(jnp.where(lane == k, sums, 0.0), axis=1, keepdims=True)

    vv, vi, ii, vw, iw, ww = [value(k) for k in range(6)]
    g = 1.0 / (SCALE * jnp.sqrt(vv / (total * SCALE * SCALE) + 1e-06))
    c0 = g * (g * vi / total)
    square = g * (g * (ii - 2.0 * c0 * vi + c0 * c0 * vv) / total)
    b0 = jnp.sqrt(jnp.maximum(square, 0.0) + 1e-06)
    h = g / b0
    c10 = h * (g * (vw - c0 * vi) / total)
    c11 = h * (h * (iw - c0 * ii - c0 * vw + c0 * c0 * vi) / total)
    a = c0 + c11
    b = c11 * c0 - c10 * b0
    square = h * (h * (ww + a * a * ii + b * b * vv - 2.0 * a * iw + 2.0 * b * vw - 2.0 * a * b * vi) / total)
    b1 = jnp.sqrt(jnp.maximum(square, 0.0) + 1e-06)
    f = h / b1
    pieces = vector.shape[0]
    v, i = vector[...], image[...]
    out[pl.ds(0, pieces, 2), :] = h * i - (h * c0 * SCALE) * v
    out[pl.ds(1, pieces, 2), :] = f * second[...] - (f * a) * i + (f * b * SCALE) * v
    alpha[0] = c0[0, 0]
    rest[0] = b0[0, 0]
    rest[1] = c11[0, 0]
    rest[2] = b1[0, 0]


def shape(*dims, dtype=F32):
    return jax.ShapeDtypeStruct(dims, dtype)


def call(kernel, outs, *args, flops=0):
    many = isinstance(outs, tuple)
    return pl.pallas_call(
        kernel,
        out_shape=outs,
        in_specs=[VMEM] * len(args),
        out_specs=tuple([VMEM] * len(outs)) if many else VMEM,
        compiler_params=pltpu.CompilerParams(vmem_limit_bytes=32 * 1024 * 1024),
    )(*args)


def exchange(x, axis, count):
    sent = x.reshape(count, LANE, TILE)
    got = lax.all_to_all(sent, axis, split_axis=0, concat_axis=0, tiled=True)
    return got.reshape(x.shape)


def per_device(start_vector, tile_blocks, row_owner, row_block, col_owner, col_block, tile_counts):
    tiles = tile_blocks[0, 0]
    count = tiles.shape[0]
    vector = start_vector.reshape(-1, TILE)
    pieces = vector.shape[0]
    n_row, n_col = lax.axis_size("row"), lax.axis_size("col")
    wide_r, wide_c = n_row * LANE, n_col * LANE
    every = wide_r + wide_c
    total = float(pieces * TILE * n_row * n_col)

    def over_row(x):
        return exchange(x, "row", n_row)

    def over_col(x):
        return exchange(x, "col", n_col)

    ask_row, ask_col, pick_row, put_row, pick_col, put_col = call(
        request_kernel,
        (
            shape(wide_r, TILE, dtype=jnp.int32),
            shape(wide_c, TILE, dtype=jnp.int32),
            shape(count, wide_r, dtype=BF16),
            shape(wide_r, count, dtype=BF16),
            shape(count, wide_c, dtype=BF16),
            shape(wide_c, count, dtype=BF16),
        ),
        row_owner.reshape(1, count),
        row_block.reshape(1, count),
        col_owner.reshape(1, count),
        col_block.reshape(1, count),
        tile_counts.reshape(1, 1),
    )
    asked_row = over_row(ask_row)
    asked_col = over_col(ask_col)
    v_row, energy = call(gather_kernel, (shape(wide_r, TILE), shape(8, TILE)), asked_row, vector)
    x_col = over_row(v_row)
    v_col, meet = call(
        meet_kernel, (shape(wide_c, TILE), shape(every, every, dtype=BF16)), asked_row, asked_col, vector
    )
    first_col = over_col(call(direct_kernel, shape(wide_c, TILE), x_col, pick_row, tiles, put_col, v_col))
    first_row = over_row(call(mirror_kernel, shape(wide_r, TILE), first_col, pick_col, tiles, put_row))
    i_row, i_col = call(sum_kernel, (shape(wide_r, TILE), shape(wide_c, TILE)), meet, first_row, first_col)
    x_col = over_row(i_row)
    image = call(spread_kernel, shape(pieces, TILE), asked_row, asked_col, first_row, first_col)
    second_col = over_col(call(direct_kernel, shape(wide_c, TILE), x_col, pick_row, tiles, put_col, i_col))
    second_row = over_row(call(mirror_kernel, shape(wide_r, TILE), second_col, pick_col, tiles, put_row))
    inner = call(
        inner_kernel,
        shape(wide_r, TILE),
        meet,
        energy,
        v_row,
        v_col,
        i_row,
        i_col,
        first_row,
        first_col,
        second_row,
        second_col,
    )
    inner = over_row(inner)
    second = call(spread_kernel, shape(pieces, TILE), asked_row, asked_col, second_row, second_col)
    inner = over_col(call(partial_kernel, shape(wide_c, TILE), inner))

    def finish(*refs):
        final_kernel(total, *refs)

    out, alpha, rest = pl.pallas_call(
        finish,
        out_shape=(shape(2 * pieces, TILE), shape(1), shape(3)),
        in_specs=[VMEM] * 4,
        out_specs=(VMEM, SMEM, SMEM),
        compiler_params=pltpu.CompilerParams(vmem_limit_bytes=32 * 1024 * 1024),
    )(inner, vector, image, second)
    basis = out.reshape(pieces, 2, TILE).transpose(1, 0, 2).reshape(2, pieces * TILE)
    return (basis, alpha, rest)


def solution(mesh):
    return jax.shard_map(
        per_device,
        mesh=mesh,
        in_specs=(
            P(("row", "col")),
            P("row", "col", None, None, None),
            P("row", "col", None, None),
            P("row", "col", None),
            P("row", "col", None, None),
            P("row", "col", None),
            P("row", "col"),
        ),
        out_specs=(P(None, ("row", "col")), P(), P()),
        check_vma=False,
    )
```

```python
import jax
import jax.numpy as jnp
from jax import lax
from jax.experimental import pallas as pl
from jax.experimental.pallas import tpu as pltpu
from jax.sharding import PartitionSpec as P

TILE = 128
LANE = 8
HALF = 4
SCALE = 1024.0
F32 = jnp.float32
BF16 = jnp.bfloat16
VMEM = pl.BlockSpec(memory_space=pltpu.VMEM)
SMEM = pl.BlockSpec(memory_space=pltpu.SMEM)
HBM = pl.BlockSpec(memory_space=pltpu.HBM)


def iota(shape, axis):
    return lax.broadcasted_iota(jnp.int32, shape, axis)


def halves(x):
    high = x.astype(BF16)
    low = (x - high.astype(F32)).astype(BF16)
    return high, low


def dot(a, b):
    return jnp.dot(a, b, preferred_element_type=F32)


def exact_dot(select, x):
    high, low = halves(x)
    return dot(select, high) + dot(select, low)


def place_of(owner):
    count = owner.shape[1]
    shape = (count, count)
    down, across = iota(shape, 0), iota(shape, 1)
    column = jnp.sum(jnp.where(down == across, owner, 0.0), axis=1, keepdims=True)
    same = column == owner
    rank_row = jnp.sum(jnp.where(same & (down < across), 1.0, 0.0), axis=0, keepdims=True)
    rank_column = jnp.sum(jnp.where(same & (across < down), 1.0, 0.0), axis=1, keepdims=True)
    return (owner * LANE + rank_row).astype(jnp.int32), (column * LANE + rank_column).astype(jnp.int32)


def request_kernel(*refs):
    far, outs, near, sems = refs[:5], refs[5:11], refs[11:16], refs[16]
    copies = [pltpu.make_async_copy(a, b, sems.at[k]) for k, (a, b) in enumerate(zip(far, near))]
    for copy in copies:
        copy.start()
    for copy in copies:
        copy.wait()
    own_r, blk_r, own_c, blk_c, filled = near
    ask_row, ask_col, pick_row, put_row, pick_col, put_col = outs
    count = own_r.shape[1]
    alive = iota((1, count), 1) < filled[...]
    for owner, block, ask, pick, put, shift in (
        (own_c, blk_c, ask_row, pick_row, put_row, 0),
        (own_r, blk_r, ask_col, pick_col, put_col, HALF),
    ):
        width = ask.shape[0]
        across, down = place_of(owner[...].astype(F32))
        value = jnp.where(alive, block[...] + 1, 0).astype(F32)
        spot = iota((width, count), 0)
        there = spot == across
        back = spot == across + shift
        wanted = jnp.sum(jnp.where(there | back, value, 0.0), axis=1, keepdims=True) - 1.0
        ask[...] = jnp.broadcast_to(wanted, (width, TILE)).astype(jnp.int32)
        pick[...] = jnp.where(iota((count, width), 1) == down, 1.0, 0.0).astype(BF16)
        put[...] = jnp.where(back, 1.0, 0.0).astype(BF16)


def gather(asked, vector):
    pieces = vector.shape[0]
    rows = asked.shape[0]
    lanes = iota((rows, TILE), 1)
    select = jnp.concatenate(
        [jnp.where(asked == lanes + k * TILE, 1.0, 0.0).astype(BF16) for k in range(pieces // TILE)], axis=1
    )
    return exact_dot(select, vector)


def gather_kernel(asked, vector, tiles, out, energy, turned):
    v = vector[...] * SCALE
    out[...] = gather(asked[...], v)
    energy[...] = jnp.sum((v * v).reshape(-1, 8, TILE), axis=0)
    for t in range(tiles.shape[0]):
        turned[t] = tiles[t].T


def product_lane(asked_row, asked_col):
    rows = [asked_row[...].astype(F32).T[0:1, :]]
    width = asked_col.shape[0]
    for k in range(width // TILE):
        part = asked_col[k * TILE : (k + 1) * TILE, :].astype(F32).T[0:1, :]
        lane = iota((1, TILE), 1)
        rows.append(jnp.where(lane % LANE >= HALF, part, -2.0))
    return [row.astype(jnp.int32) for row in rows]


def meet_kernel(asked_row, asked_col, vector, out, meet):
    out[...] = gather(asked_col[...], vector[...] * SCALE)
    lanes = product_lane(asked_row, asked_col)
    base = 0
    for asked in (asked_row, asked_col):
        mine = asked[...]
        for k, lane in enumerate(lanes):
            hit = (mine == lane) & (mine >= 0)
            meet[base : base + mine.shape[0], k * TILE : (k + 1) * TILE] = jnp.where(hit, 1.0, 0.0).astype(BF16)
        base += mine.shape[0]


def multiply(x, tiles):
    count = x.shape[0]
    row = iota((8, TILE), 0)
    groups = []
    for g in range(count // 8):
        part = x[g * 8 : (g + 1) * 8, :]
        high = part.astype(BF16).astype(F32)
        both = jnp.concatenate([high, part - high], axis=0).astype(BF16)
        total = jnp.zeros((8, TILE), F32)
        for j in range(8):
            y = dot(both, tiles[g * 8 + j])
            total = jnp.where(row == j, y[0:8] + y[8:16], total)
        groups.append(total)
    return jnp.concatenate(groups, axis=0)


def direct_kernel(got, pick, turned, put, extra, out):
    y = multiply(exact_dot(pick[...], got[...]), turned)
    forward = iota(extra.shape, 0) % LANE < HALF
    out[...] = exact_dot(put[...], y) + jnp.where(forward, extra[...], 0.0)


def mirror_kernel(got, pick, tiles, put, out):
    y = multiply(exact_dot(pick[...], got[...]), tiles)
    out[...] = exact_dot(put[...], y)


def sum_kernel(meet, back_row, back_col, out_row, out_col):
    total = exact_dot(meet[...], jnp.concatenate([back_row[...], back_col[...]], axis=0))
    width = out_row.shape[0]
    out_row[...] = total[:width]
    out_col[...] = total[width:]


def inner_kernel(
    meet, energy, v_row, v_col, i_row, i_col, first_row, first_col, second_row, second_col, out
):
    total = exact_dot(meet[...], jnp.concatenate([second_row[...], second_col[...]], axis=0))
    width = v_row.shape[0]
    returned = iota(v_col.shape, 0) % LANE >= HALF
    first_c = jnp.where(returned, first_col[...], 0.0)
    second_c = jnp.where(returned, second_col[...], 0.0)
    first_r, second_r = first_row[...], second_row[...]

    def inner(a_r, b_r, a_c, b_c):
        return jnp.sum(a_r * b_r, axis=0, keepdims=True) + jnp.sum(a_c * b_c, axis=0, keepdims=True)

    values = [
        jnp.sum(energy[...], axis=0, keepdims=True),
        inner(v_row[...], first_r, v_col[...], first_c),
        inner(i_row[...], first_r, i_col[...], first_c),
        inner(v_row[...], second_r, v_col[...], second_c),
        inner(i_row[...], second_r, i_col[...], second_c),
        inner(total[:width], second_r, total[width:], second_c),
    ]
    packed = jnp.concatenate(values + [jnp.zeros((2, TILE), F32)], axis=0)
    for k in range(out.shape[0]):
        out[k] = packed


def partial_kernel(got, out):
    total = jnp.sum(got[...], axis=0)
    sums = jnp.sum(total, axis=1, keepdims=True)
    packed = jnp.sum(jnp.where(iota(total.shape, 0) == iota(total.shape, 1), sums, 0.0), axis=0, keepdims=True)
    out[...] = jnp.broadcast_to(packed, out.shape)


def spread_kernel(asked_row, asked_col, back_row, back_col, out):
    lanes = jnp.concatenate(product_lane(asked_row, asked_col), axis=1)
    high, low = halves(jnp.concatenate([back_row[...], back_col[...]], axis=0))
    step = 256
    for start in range(0, out.shape[0], step):
        place = iota((step, lanes.shape[1]), 0) + start
        select = jnp.where(place == lanes, 1.0, 0.0).astype(BF16)
        out[start : start + step, :] = dot(select, high) + dot(select, low)


def final_kernel(total, got, vector, image, second, out, alpha, rest, near, sems):
    sums = jnp.sum(got[...], axis=0, keepdims=True)
    lane = iota((1, TILE), 1)

    def value(k):
        return jnp.sum(jnp.where(lane == k, sums, 0.0), axis=1, keepdims=True)

    vv, vi, ii, vw, iw, ww = [value(k) for k in range(6)]
    g = 1.0 / (SCALE * jnp.sqrt(vv / (total * SCALE * SCALE) + 1e-06))
    c0 = g * (g * vi / total)
    square = g * (g * (ii - 2.0 * c0 * vi + c0 * c0 * vv) / total)
    b0 = jnp.sqrt(jnp.maximum(square, 0.0) + 1e-06)
    h = g / b0
    c10 = h * (g * (vw - c0 * vi) / total)
    c11 = h * (h * (iw - c0 * ii - c0 * vw + c0 * c0 * vi) / total)
    a = c0 + c11
    b = c11 * c0 - c10 * b0
    square = h * (h * (ww + a * a * ii + b * b * vv - 2.0 * a * iw + 2.0 * b * vw - 2.0 * a * b * vi) / total)
    b1 = jnp.sqrt(jnp.maximum(square, 0.0) + 1e-06)
    f = h / b1
    parts = sems.shape[0]
    step = vector.shape[0] // parts
    copies = []
    for k in range(parts):
        rows = pl.ds(k * step, step)
        v, i = vector[rows, :], image[rows, :]
        near[pl.ds(2 * k * step, step, 2), :] = h * i - (h * c0 * SCALE) * v
        near[pl.ds(2 * k * step + 1, step, 2), :] = f * second[rows, :] - (f * a) * i + (f * b * SCALE) * v
        done = pl.ds(2 * k * step, 2 * step)
        copies.append(pltpu.make_async_copy(near.at[done], out.at[done], sems.at[k]))
        copies[-1].start()
    alpha[0] = c0[0, 0]
    rest[0] = b0[0, 0]
    rest[1] = c11[0, 0]
    rest[2] = b1[0, 0]
    for copy in copies:
        copy.wait()


def shape(*dims, dtype=F32):
    return jax.ShapeDtypeStruct(dims, dtype)


def call(kernel, outs, *args, ins=VMEM, out_specs=VMEM, scratch=(), limit=32):
    if isinstance(outs, tuple) and not isinstance(out_specs, tuple):
        out_specs = tuple([out_specs] * len(outs))
    return pl.pallas_call(
        kernel,
        out_shape=outs,
        in_specs=[ins] * len(args),
        out_specs=out_specs,
        scratch_shapes=scratch,
        compiler_params=pltpu.CompilerParams(vmem_limit_bytes=limit * 1024 * 1024),
    )(*args)


def exchange(x, axis, count):
    sent = x.reshape(count, -1, TILE)
    got = lax.all_to_all(sent, axis, split_axis=0, concat_axis=0, tiled=True)
    return got.reshape(x.shape)


def per_device(start_vector, tile_blocks, row_owner, row_block, col_owner, col_block, tile_counts):
    tiles = tile_blocks[0, 0]
    count = tiles.shape[0]
    vector = start_vector.reshape(-1, TILE)
    pieces = vector.shape[0]
    n_row, n_col = lax.axis_size("row"), lax.axis_size("col")
    wide_r, wide_c = n_row * LANE, n_col * LANE
    every = wide_r + wide_c
    total = float(pieces * TILE * n_row * n_col)

    def over_row(x):
        return exchange(x, "row", n_row)

    def over_col(x):
        return exchange(x, "col", n_col)

    ask_row, ask_col, pick_row, put_row, pick_col, put_col = call(
        request_kernel,
        (
            shape(wide_r, TILE, dtype=jnp.int32),
            shape(wide_c, TILE, dtype=jnp.int32),
            shape(count, wide_r, dtype=BF16),
            shape(wide_r, count, dtype=BF16),
            shape(count, wide_c, dtype=BF16),
            shape(wide_c, count, dtype=BF16),
        ),
        row_owner.reshape(1, count),
        row_block.reshape(1, count),
        col_owner.reshape(1, count),
        col_block.reshape(1, count),
        tile_counts.reshape(1, 1),
        ins=HBM,
        limit=63,
        scratch=[pltpu.VMEM((1, count), jnp.int32)] * 4
        + [pltpu.VMEM((1, 1), jnp.int32), pltpu.SemaphoreType.DMA((5,))],
    )
    asked_row = over_row(ask_row)
    asked_col = over_col(ask_col)
    v_row, energy, turned = call(
        gather_kernel,
        (shape(wide_r, TILE), shape(8, TILE), shape(*tiles.shape, dtype=BF16)),
        asked_row,
        vector,
        tiles,
    )
    x_col = over_row(v_row)
    v_col, meet = call(
        meet_kernel, (shape(wide_c, TILE), shape(every, every, dtype=BF16)), asked_row, asked_col, vector
    )
    first_col = over_col(call(direct_kernel, shape(wide_c, TILE), x_col, pick_row, turned, put_col, v_col))
    first_row = over_row(call(mirror_kernel, shape(wide_r, TILE), first_col, pick_col, tiles, put_row))
    i_row, i_col = call(sum_kernel, (shape(wide_r, TILE), shape(wide_c, TILE)), meet, first_row, first_col)
    x_col = over_row(i_row)
    image = call(spread_kernel, shape(pieces, TILE), asked_row, asked_col, first_row, first_col)
    second_col = over_col(call(direct_kernel, shape(wide_c, TILE), x_col, pick_row, turned, put_col, i_col))
    second_row = over_row(call(mirror_kernel, shape(wide_r, TILE), second_col, pick_col, tiles, put_row))
    inner = call(
        inner_kernel,
        shape(n_row, 8, TILE),
        meet,
        energy,
        v_row,
        v_col,
        i_row,
        i_col,
        first_row,
        first_col,
        second_row,
        second_col,
    )
    inner = over_row(inner)
    second = call(spread_kernel, shape(pieces, TILE), asked_row, asked_col, second_row, second_col)
    inner = over_col(call(partial_kernel, shape(n_col, TILE), inner))

    def finish(*refs):
        final_kernel(total, *refs)

    out, alpha, rest = call(
        finish,
        (shape(2 * pieces, TILE), shape(1), shape(3)),
        inner,
        vector,
        image,
        second,
        out_specs=(HBM, SMEM, SMEM),
        scratch=[pltpu.VMEM((2 * pieces, TILE), F32), pltpu.SemaphoreType.DMA((4,))],
    )
    basis = out.reshape(pieces, 2, TILE).transpose(1, 0, 2).reshape(2, pieces * TILE)
    return (basis, alpha, rest)


def solution(mesh):
    return jax.shard_map(
        per_device,
        mesh=mesh,
        in_specs=(
            P(("row", "col")),
            P("row", "col", None, None, None),
            P("row", "col", None, None),
            P("row", "col", None),
            P("row", "col", None, None),
            P("row", "col", None),
            P("row", "col"),
        ),
        out_specs=(P(None, ("row", "col")), P(), P()),
        check_vma=False,
    )
```

```python
import functools

import jax
import jax.numpy as jnp
from jax import lax
from jax.experimental import pallas as pl
from jax.experimental.pallas import tpu as pltpu
from jax.sharding import PartitionSpec as P

TILE = 128
LANE = 8
HALF = 4
SCALE = 1024.0
F32 = jnp.float32
BF16 = jnp.bfloat16
VMEM = pl.BlockSpec(memory_space=pltpu.VMEM)
SMEM = pl.BlockSpec(memory_space=pltpu.SMEM)
HBM = pl.BlockSpec(memory_space=pltpu.HBM)


def iota(shape, axis):
    return lax.broadcasted_iota(jnp.int32, shape, axis)


def halves(x):
    high = x.astype(BF16)
    low = (x - high.astype(F32)).astype(BF16)
    return high, low


def dot(a, b):
    return jnp.dot(a, b, preferred_element_type=F32)


def exact_dot(select, x):
    high, low = halves(x)
    return dot(select, high) + dot(select, low)


def place_of(owner):
    count = owner.shape[1]
    shape = (count, count)
    down, across = iota(shape, 0), iota(shape, 1)
    column = jnp.sum(jnp.where(down == across, owner, 0.0), axis=1, keepdims=True)
    same = column == owner
    rank_row = jnp.sum(jnp.where(same & (down < across), 1.0, 0.0), axis=0, keepdims=True)
    rank_column = jnp.sum(jnp.where(same & (across < down), 1.0, 0.0), axis=1, keepdims=True)
    return (owner * LANE + rank_row).astype(jnp.int32), (column * LANE + rank_column).astype(jnp.int32)


def request_kernel(pieces, slots, ask_row, ask_col, pick_row, put_row, pick_col, put_col, pick_pair, mine):
    own_r, blk_r, own_c, blk_c, filled = [slots[k : k + 1, :] for k in range(5)]
    count = own_r.shape[1]
    alive = iota((1, count), 1) < filled
    for owner, block, ask, pick, put, shift in (
        (own_c, blk_c, ask_row, pick_row, put_row, 0),
        (own_r, blk_r, ask_col, pick_col, put_col, HALF),
    ):
        width = ask.shape[0]
        across, down = place_of(owner.astype(F32))
        value = jnp.where(alive, block + 1, 0).astype(F32)
        spot = iota((width, count), 0)
        there = spot == across
        back = spot == across + shift
        wanted = jnp.sum(jnp.where(there | back, value, 0.0), axis=1, keepdims=True) - 1.0
        ask[...] = jnp.broadcast_to(wanted, (width, TILE)).astype(jnp.int32)
        pick[...] = jnp.where(iota((count, width), 1) == down, 1.0, 0.0).astype(BF16)
        put[...] = jnp.where(back, 1.0, 0.0).astype(BF16)
    ident = jnp.where(alive, own_c * pieces + blk_c, -1)
    width = ask_row.shape[0]
    lane = iota((width, TILE), 1)
    number = iota((width, TILE), 0) // LANE
    ids = jnp.concatenate([ident, ident], axis=1)
    ask_row[...] = jnp.where(lane >= count, ids, jnp.where(lane == count - 1, number, ask_row[...]))
    across = iota((count, count), 0) == iota((count, count), 1)
    down = jnp.sum(jnp.where(across, ident.astype(F32), 0.0), axis=1, keepdims=True).astype(jnp.int32)
    mine[...] = jnp.broadcast_to(jnp.where(down < 0, -2, down), mine.shape)
    place = place_of(own_c.astype(F32))[1]
    high = place + place // LANE * LANE
    lane = iota(pick_pair.shape, 1)
    pick_pair[...] = jnp.where((lane == high) | (lane == high + LANE), 1.0, 0.0).astype(BF16)


def first_lane(asked):
    return jnp.broadcast_to(asked[:, 0:1], asked.shape)


def gather(asked, vector):
    pieces = vector.shape[0]
    rows = asked.shape[0]
    lanes = iota((rows, TILE), 1)
    select = jnp.concatenate(
        [jnp.where(asked == lanes + k * TILE, 1.0, 0.0).astype(BF16) for k in range(pieces // TILE)], axis=1
    )
    return exact_dot(select, vector)


def gather_kernel(asked, vector, tiles, out, energy, turned):
    v = vector[...] * SCALE
    out[...] = gather(first_lane(asked[...]), v)
    energy[...] = jnp.sum((v * v).reshape(-1, 8, TILE), axis=0)
    for t in range(tiles.shape[0]):
        turned[t] = tiles[t].T


def product_lane(asked_row, asked_col):
    rows = [first_lane(asked_row[...]).astype(F32).T[0:1, :]]
    width = asked_col.shape[0]
    for k in range(width // TILE):
        part = asked_col[k * TILE : (k + 1) * TILE, :].astype(F32).T[0:1, :]
        lane = iota((1, TILE), 1)
        rows.append(jnp.where(lane % LANE >= HALF, part, -2.0))
    return [row.astype(jnp.int32) for row in rows]


def meet_kernel(asked_row, asked_col, mine, vector, out, meet, link, link_col):
    out[...] = gather(asked_col[...], vector[...] * SCALE)
    lanes = product_lane(asked_row, asked_col)
    base = 0
    served_row, served_col = first_lane(asked_row[...]), asked_col[...]
    for served in (served_row, served_col):
        for k, lane in enumerate(lanes):
            hit = (served == lane) & (served >= 0)
            meet[base : base + served.shape[0], k * TILE : (k + 1) * TILE] = jnp.where(hit, 1.0, 0.0).astype(BF16)
        base += served.shape[0]
    count = mine.shape[0]
    index = asked_row[0:1, count - 1 : count]
    ident = jnp.where(served_col < 0, -3, served_col + index * vector.shape[0])
    lane = iota((1, TILE), 1)
    for k in range(asked_row.shape[0] // (2 * LANE)):
        even = asked_row[2 * k * LANE : 2 * k * LANE + 1, :]
        odd = asked_row[(2 * k + 1) * LANE : (2 * k + 1) * LANE + 1, :]
        ids = jnp.where(lane < count, pltpu.roll(even, count, 1), odd)
        cols = slice(k * TILE, (k + 1) * TILE)
        link[:, cols] = jnp.where(mine[...] == ids, 1.0, 0.0).astype(BF16)
        link_col[:, cols] = jnp.where(ident == ids, 1.0, 0.0).astype(BF16)


def multiply(x, tiles):
    count = x.shape[0]
    row = iota((8, TILE), 0)
    groups = []
    for g in range(count // 8):
        part = x[g * 8 : (g + 1) * 8, :]
        high = part.astype(BF16).astype(F32)
        both = jnp.concatenate([high, part - high], axis=0).astype(BF16)
        total = jnp.zeros((8, TILE), F32)
        for j in range(8):
            y = dot(both, tiles[g * 8 + j])
            total = jnp.where(row == j, y[0:8] + y[8:16], total)
        groups.append(total)
    return jnp.concatenate(groups, axis=0)


def direct_kernel(got, pick, turned, put, extra, out):
    y = multiply(exact_dot(pick[...], got[...]), turned)
    forward = iota(extra.shape, 0) % LANE < HALF
    out[...] = exact_dot(put[...], y) + jnp.where(forward, extra[...], 0.0)


def mirror_kernel(got, pick, tiles, put, meet, out, first):
    y = multiply(exact_dot(pick[...], got[...]), tiles)
    first[...] = exact_dot(put[...], y)
    width = first.shape[0]
    total = exact_dot(meet[:width, width:], got[...])
    high = total.astype(BF16).astype(F32)
    low = total - high
    count = y.shape[0]
    narrow = y.astype(BF16)
    for k in range(out.shape[0]):
        rows = slice(k * LANE, (k + 1) * LANE)
        out[k, :count, :] = narrow
        out[k, count:, :] = jnp.concatenate([high[rows], low[rows]], axis=0).astype(BF16)


def second_direct_kernel(got, link, link_col, pick, meet, first_col, turned, put, out):
    count = link.shape[0]
    peers = range(got.shape[0])
    mirrors = jnp.concatenate([got[k, :count, :] for k in peers], axis=0)
    sums = jnp.concatenate([got[k, count:, :] for k in peers], axis=0)
    y = multiply(dot(link[...], mirrors) + dot(pick[...], sums), turned)
    width = got.shape[0] * LANE
    image = dot(link_col[...], mirrors) + exact_dot(meet[width:, width:], first_col[...])
    forward = iota(image.shape, 0) % LANE < HALF
    out[...] = exact_dot(put[...], y) + jnp.where(forward, image, 0.0)


def second_mirror_kernel(got, pick, tiles, put, first, out):
    y = exact_dot(put[...], multiply(exact_dot(pick[...], got[...]), tiles))
    out[:, :LANE, :] = y.reshape(-1, LANE, TILE)
    out[:, LANE:, :] = first[...].reshape(-1, LANE, TILE)


def split_rows(got):
    return got[:, LANE:, :].reshape(-1, TILE), got[:, :LANE, :].reshape(-1, TILE)


def inner_kernel(meet, energy, v_row, v_col, got, first_col, second_col, out):
    first_r, second_r = split_rows(got[...])
    first = jnp.concatenate([first_r, first_col[...]], axis=0)
    second = jnp.concatenate([second_r, second_col[...]], axis=0)
    both = exact_dot(meet[...], jnp.concatenate([first, second], axis=1))
    image, total = both[:, :TILE], both[:, TILE:]
    width = v_row.shape[0]
    returned = iota(v_col.shape, 0) % LANE >= HALF
    first_c = jnp.where(returned, first_col[...], 0.0)
    second_c = jnp.where(returned, second_col[...], 0.0)

    def inner(a_r, b_r, a_c, b_c):
        return jnp.sum(a_r * b_r, axis=0, keepdims=True) + jnp.sum(a_c * b_c, axis=0, keepdims=True)

    values = [
        jnp.sum(energy[...], axis=0, keepdims=True),
        inner(v_row[...], first_r, v_col[...], first_c),
        inner(image[:width], first_r, image[width:], first_c),
        inner(v_row[...], second_r, v_col[...], second_c),
        inner(image[:width], second_r, image[width:], second_c),
        inner(total[:width], second_r, total[width:], second_c),
    ]
    packed = jnp.concatenate(values + [jnp.zeros((2, TILE), F32)], axis=0)
    for k in range(out.shape[0]):
        out[k] = packed


def partial_kernel(got, out):
    total = jnp.sum(got[...], axis=0)
    sums = jnp.sum(total, axis=1, keepdims=True)
    packed = jnp.sum(jnp.where(iota(total.shape, 0) == iota(total.shape, 1), sums, 0.0), axis=0, keepdims=True)
    out[...] = jnp.broadcast_to(packed, out.shape)


def spread_kernel(which, asked_row, asked_col, got, back_col, out):
    lanes = jnp.concatenate(product_lane(asked_row, asked_col), axis=1)
    high, low = halves(jnp.concatenate([split_rows(got[...])[which], back_col[...]], axis=0))
    step = 256
    for start in range(0, out.shape[0], step):
        place = iota((step, lanes.shape[1]), 0) + start
        select = jnp.where(place == lanes, 1.0, 0.0).astype(BF16)
        out[start : start + step, :] = dot(select, high) + dot(select, low)


def final_kernel(total, got, vector, image, second, out, alpha, rest, near, sems):
    sums = jnp.sum(got[...], axis=0, keepdims=True)
    lane = iota((1, TILE), 1)

    def value(k):
        return jnp.sum(jnp.where(lane == k, sums, 0.0), axis=1, keepdims=True)

    vv, vi, ii, vw, iw, ww = [value(k) for k in range(6)]
    g = 1.0 / (SCALE * jnp.sqrt(vv / (total * SCALE * SCALE) + 1e-06))
    c0 = g * (g * vi / total)
    square = g * (g * (ii - 2.0 * c0 * vi + c0 * c0 * vv) / total)
    b0 = jnp.sqrt(jnp.maximum(square, 0.0) + 1e-06)
    h = g / b0
    c10 = h * (g * (vw - c0 * vi) / total)
    c11 = h * (h * (iw - c0 * ii - c0 * vw + c0 * c0 * vi) / total)
    a = c0 + c11
    b = c11 * c0 - c10 * b0
    square = h * (h * (ww + a * a * ii + b * b * vv - 2.0 * a * iw + 2.0 * b * vw - 2.0 * a * b * vi) / total)
    b1 = jnp.sqrt(jnp.maximum(square, 0.0) + 1e-06)
    f = h / b1
    parts = sems.shape[0]
    step = vector.shape[0] // parts
    copies = []
    for k in range(parts):
        rows = pl.ds(k * step, step)
        v, i = vector[rows, :], image[rows, :]
        near[pl.ds(2 * k * step, step, 2), :] = h * i - (h * c0 * SCALE) * v
        near[pl.ds(2 * k * step + 1, step, 2), :] = f * second[rows, :] - (f * a) * i + (f * b * SCALE) * v
        done = pl.ds(2 * k * step, 2 * step)
        copies.append(pltpu.make_async_copy(near.at[done], out.at[done], sems.at[k]))
        copies[-1].start()
    alpha[0] = c0[0, 0]
    rest[0] = b0[0, 0]
    rest[1] = c11[0, 0]
    rest[2] = b1[0, 0]
    for copy in copies:
        copy.wait()


def shape(*dims, dtype=F32):
    return jax.ShapeDtypeStruct(dims, dtype)


def call(kernel, outs, *args, ins=VMEM, out_specs=VMEM, scratch=(), limit=16):
    if isinstance(outs, tuple) and not isinstance(out_specs, tuple):
        out_specs = tuple([out_specs] * len(outs))
    return pl.pallas_call(
        kernel,
        out_shape=outs,
        in_specs=[ins] * len(args),
        out_specs=out_specs,
        scratch_shapes=scratch,
        compiler_params=pltpu.CompilerParams(vmem_limit_bytes=limit * 1024 * 1024),
    )(*args)


def exchange(x, axis, count):
    sent = x.reshape(count, -1, TILE)
    got = lax.all_to_all(sent, axis, split_axis=0, concat_axis=0, tiled=True)
    return got.reshape(x.shape)


def per_device(start_vector, tile_blocks, row_owner, row_block, col_owner, col_block, tile_counts):
    tiles = tile_blocks[0, 0]
    count = tiles.shape[0]
    vector = start_vector.reshape(-1, TILE)
    pieces = vector.shape[0]
    n_row, n_col = lax.axis_size("row"), lax.axis_size("col")
    wide_r, wide_c = n_row * LANE, n_col * LANE
    every = wide_r + wide_c
    total = float(pieces * TILE * n_row * n_col)

    def over_row(x):
        return exchange(x, "row", n_row)

    def over_col(x):
        return exchange(x, "col", n_col)

    slots = jnp.concatenate(
        [x.reshape(1, count) for x in (row_owner, row_block, col_owner, col_block)]
        + [jnp.broadcast_to(tile_counts.reshape(1, 1), (1, count))],
        axis=0,
    )
    ask_row, ask_col, pick_row, put_row, pick_col, put_col, pick_pair, mine = call(
        functools.partial(request_kernel, pieces),
        (
            shape(wide_r, TILE, dtype=jnp.int32),
            shape(wide_c, TILE, dtype=jnp.int32),
            shape(count, wide_r, dtype=BF16),
            shape(wide_r, count, dtype=BF16),
            shape(count, wide_c, dtype=BF16),
            shape(wide_c, count, dtype=BF16),
            shape(count, 2 * wide_r, dtype=BF16),
            shape(count, TILE, dtype=jnp.int32),
        ),
        slots,
    )
    asked_row = over_row(ask_row)
    asked_col = over_col(ask_col)
    v_row, energy, turned = call(
        gather_kernel,
        (shape(wide_r, TILE), shape(8, TILE), shape(*tiles.shape, dtype=BF16)),
        asked_row,
        vector,
        tiles,
    )
    x_col = over_row(v_row)
    v_col, meet, link, link_col = call(
        meet_kernel,
        (
            shape(wide_c, TILE),
            shape(every, every, dtype=BF16),
            shape(count, n_row * count, dtype=BF16),
            shape(wide_c, n_row * count, dtype=BF16),
        ),
        asked_row,
        asked_col,
        mine,
        vector,
    )
    first_col = over_col(call(direct_kernel, shape(wide_c, TILE), x_col, pick_row, turned, put_col, v_col))
    packed, first = call(
        mirror_kernel,
        (shape(n_row, count + 2 * LANE, TILE, dtype=BF16), shape(wide_r, TILE)),
        first_col,
        pick_col,
        tiles,
        put_row,
        meet,
    )
    second_col = call(
        second_direct_kernel,
        shape(wide_c, TILE),
        over_row(packed),
        link,
        link_col,
        pick_pair,
        meet,
        first_col,
        turned,
        put_col,
    )
    second_col = over_col(second_col)
    back = call(
        second_mirror_kernel, shape(n_row, 2 * LANE, TILE), second_col, pick_col, tiles, put_row, first
    )
    back = over_row(back)
    inner = call(
        inner_kernel,
        shape(n_row, 8, TILE),
        meet,
        energy,
        v_row,
        v_col,
        back,
        first_col,
        second_col,
    )
    inner = over_row(inner)
    image, second = [
        call(functools.partial(spread_kernel, k), shape(pieces, TILE), asked_row, asked_col, back, column)
        for k, column in enumerate((first_col, second_col))
    ]
    inner = over_col(call(partial_kernel, shape(n_col, TILE), inner))

    def finish(*refs):
        final_kernel(total, *refs)

    out, alpha, rest = call(
        finish,
        (shape(2 * pieces, TILE), shape(1), shape(3)),
        inner,
        vector,
        image,
        second,
        out_specs=(HBM, SMEM, SMEM),
        scratch=[pltpu.VMEM((2 * pieces, TILE), F32), pltpu.SemaphoreType.DMA((4,))],
    )
    basis = out.reshape(pieces, 2, TILE).transpose(1, 0, 2).reshape(2, pieces * TILE)
    return (basis, alpha, rest)


def solution(mesh):
    return jax.shard_map(
        per_device,
        mesh=mesh,
        in_specs=(
            P(("row", "col")),
            P("row", "col", None, None, None),
            P("row", "col", None, None),
            P("row", "col", None),
            P("row", "col", None, None),
            P("row", "col", None),
            P("row", "col"),
        ),
        out_specs=(P(None, ("row", "col")), P(), P()),
        check_vma=False,
    )
```

```python
import functools

import jax
import jax.numpy as jnp
from jax import lax
from jax.experimental import pallas as pl
from jax.experimental.pallas import tpu as pltpu
from jax.sharding import PartitionSpec as P

TILE = 128
LANE = 8
HALF = 4
SCALE = 1024.0
F32 = jnp.float32
BF16 = jnp.bfloat16
VMEM = pl.BlockSpec(memory_space=pltpu.VMEM)
SMEM = pl.BlockSpec(memory_space=pltpu.SMEM)
HBM = pl.BlockSpec(memory_space=pltpu.HBM)


def iota(shape, axis):
    return lax.broadcasted_iota(jnp.int32, shape, axis)


def halves(x):
    high = x.astype(BF16)
    low = (x - high.astype(F32)).astype(BF16)
    return high, low


def dot(a, b):
    return jnp.dot(a, b, preferred_element_type=F32)


def exact_dot(select, x):
    high, low = halves(x)
    return dot(select, high) + dot(select, low)


def place_of(owner):
    count = owner.shape[1]
    shape = (count, count)
    down, across = iota(shape, 0), iota(shape, 1)
    column = jnp.sum(jnp.where(down == across, owner, 0.0), axis=1, keepdims=True)
    same = column == owner
    rank_row = jnp.sum(jnp.where(same & (down < across), 1.0, 0.0), axis=0, keepdims=True)
    rank_column = jnp.sum(jnp.where(same & (across < down), 1.0, 0.0), axis=1, keepdims=True)
    return (owner * LANE + rank_row).astype(jnp.int32), (column * LANE + rank_column).astype(jnp.int32)


def request_kernel(pieces, slots, ask_row, ask_col, pick_row, put_row, pick_col, put_col, pick_pair, mine):
    own_r, blk_r, own_c, blk_c, filled = [slots[k : k + 1, :] for k in range(5)]
    count = own_r.shape[1]
    alive = iota((1, count), 1) < filled
    for owner, block, ask, pick, put, shift in (
        (own_c, blk_c, ask_row, pick_row, put_row, 0),
        (own_r, blk_r, ask_col, pick_col, put_col, HALF),
    ):
        width = ask.shape[0]
        across, down = place_of(owner.astype(F32))
        value = jnp.where(alive, block + 1, 0).astype(F32)
        spot = iota((width, count), 0)
        there = spot == across
        back = spot == across + shift
        wanted = jnp.sum(jnp.where(there | back, value, 0.0), axis=1, keepdims=True) - 1.0
        ask[...] = jnp.broadcast_to(wanted, (width, TILE)).astype(jnp.int32)
        pick[...] = jnp.where(iota((count, width), 1) == down, 1.0, 0.0).astype(BF16)
        put[...] = jnp.where(back, 1.0, 0.0).astype(BF16)
    ident = jnp.where(alive, own_c * pieces + blk_c, -1)
    width = ask_row.shape[0]
    lane = iota((width, TILE), 1)
    number = iota((width, TILE), 0) // LANE
    spot = place_of(own_c.astype(F32))[0]
    ids = jnp.concatenate([ident, ident], axis=1)
    spots = jnp.concatenate([spot, spot], axis=1)
    ids = jnp.where(iota((width, TILE), 0) % 2 == 0, ids, spots)
    ask_row[...] = jnp.where(lane >= count, ids, jnp.where(lane == count - 1, number, ask_row[...]))
    across = iota((count, count), 0) == iota((count, count), 1)
    down = jnp.sum(jnp.where(across, ident.astype(F32), 0.0), axis=1, keepdims=True).astype(jnp.int32)
    mine[...] = jnp.broadcast_to(jnp.where(down < 0, -2, down), mine.shape)
    place = place_of(own_c.astype(F32))[1]
    high = place + place // LANE * LANE
    lane = iota(pick_pair.shape, 1)
    pick_pair[...] = jnp.where(lane == high, 1.0, 0.0).astype(BF16)


def first_lane(asked):
    return jnp.broadcast_to(asked[:, 0:1], asked.shape)


def gather(asked, vector):
    pieces = vector.shape[0]
    rows = asked.shape[0]
    lanes = iota((rows, TILE), 1)
    select = jnp.concatenate(
        [jnp.where(asked == lanes + k * TILE, 1.0, 0.0).astype(BF16) for k in range(pieces // TILE)], axis=1
    )
    return exact_dot(select, vector)


def gather_kernel(asked, vector, out, energy):
    v = vector[...] * SCALE
    out[...] = gather(first_lane(asked[...]), v)
    energy[...] = jnp.sum((v * v).reshape(-1, 8, TILE), axis=0)


def product_lane(asked_row, asked_col):
    rows = [first_lane(asked_row[...]).astype(F32).T[0:1, :]]
    width = asked_col.shape[0]
    for k in range(width // TILE):
        part = asked_col[k * TILE : (k + 1) * TILE, :].astype(F32).T[0:1, :]
        lane = iota((1, TILE), 1)
        rows.append(jnp.where(lane % LANE >= HALF, part, -2.0))
    return [row.astype(jnp.int32) for row in rows]


def meet_tables(asked_row, asked_col, mine, pieces, meet, link, link_col, owned):
    lanes = product_lane(asked_row, asked_col)
    base = 0
    served_row, served_col = first_lane(asked_row[...]), asked_col[...]
    for served in (served_row, served_col):
        for k, lane in enumerate(lanes):
            hit = (served == lane) & (served >= 0)
            meet[base : base + served.shape[0], k * TILE : (k + 1) * TILE] = jnp.where(hit, 1.0, 0.0).astype(BF16)
        base += served.shape[0]
    count = mine.shape[0]
    index = asked_row[0:1, count - 1 : count]
    ident = jnp.where(served_col < 0, -3, served_col + index * pieces)
    lane = iota((1, TILE), 1)
    slot = iota(owned.shape[:1] + (TILE,), 0)
    half = iota(owned.shape[:1] + (TILE,), 1) // count
    for k in range(asked_row.shape[0] // (2 * LANE)):
        start = 2 * k * LANE
        even = [asked_row[start + j : start + j + 1, :] for j in range(2)]
        odd = [asked_row[start + LANE + j : start + LANE + j + 1, :] for j in range(2)]
        ids, spots = [jnp.where(lane < count, pltpu.roll(a, count, 1), b) for a, b in zip(even, odd)]
        cols = slice(k * TILE, (k + 1) * TILE)
        link[:, cols] = jnp.where(mine[...] == ids, 1.0, 0.0).astype(BF16)
        link_col[:, cols] = jnp.where(ident == ids, 1.0, 0.0).astype(BF16)
        sent = (spots == index * LANE + slot % LANE) & (slot // LANE == 2 * k + half)
        owned[:, cols] = jnp.where(sent, 1.0, 0.0).astype(BF16)


def multiply(x, tiles, across):
    count = x.shape[0]
    dims = (((1,), (1 if across else 0,)), ((), ()))
    row = iota((8, TILE), 0)
    groups = []
    for g in range(count // 8):
        part = x[g * 8 : (g + 1) * 8, :]
        high = part.astype(BF16).astype(F32)
        both = jnp.concatenate([high, part - high], axis=0).astype(BF16)
        total = jnp.zeros((8, TILE), F32)
        for j in range(8):
            y = lax.dot_general(both, tiles[g * 8 + j], dims, preferred_element_type=F32)
            total = jnp.where(row == j, y[0:8] + y[8:16], total)
        groups.append(total)
    return jnp.concatenate(groups, axis=0)


def direct_kernel(
    got, pick, tiles, put, asked_row, asked_col, mine, vector, out, v_col, meet, link, link_col, owned
):
    y = multiply(exact_dot(pick[...], got[...]), tiles, True)
    v = gather(asked_col[...], vector[...] * SCALE)
    v_col[...] = v
    forward = iota(v.shape, 0) % LANE < HALF
    out[...] = exact_dot(put[...], y) + jnp.where(forward, v, 0.0)
    meet_tables(asked_row, asked_col, mine, vector.shape[0], meet, link, link_col, owned)


def mirror_kernel(got, pick, tiles, put, meet, out):
    y = multiply(exact_dot(pick[...], got[...]), tiles, False)
    high, low = halves(y)
    width = put.shape[0]
    total = exact_dot(meet[:width, width:], got[...])
    low = dot(put[...], low)
    count = y.shape[0]
    for k in range(out.shape[0]):
        rows = slice(k * LANE, (k + 1) * LANE)
        out[k, :count, :] = high
        out[k, count:, :] = jnp.concatenate([total[rows], low[rows]], axis=0).astype(BF16)


def second_direct_kernel(got, link, link_col, owned, pick, meet, first_col, tiles, put, out, first_row):
    count = link.shape[0]
    peers = range(got.shape[0])
    mirrors = jnp.concatenate([got[k, :count, :] for k in peers], axis=0)
    sums = jnp.concatenate([got[k, count:, :] for k in peers], axis=0)
    y = multiply(dot(link[...], mirrors) + dot(pick[...], sums), tiles, True)
    width = got.shape[0] * LANE
    image = dot(link_col[...], mirrors) + exact_dot(meet[width:, width:], first_col[...])
    forward = iota(image.shape, 0) % LANE < HALF
    out[...] = exact_dot(put[...], y) + jnp.where(forward, image, 0.0)
    slot = iota((width, 2 * width), 0)
    low = iota((width, 2 * width), 1) == slot + slot // LANE * LANE + LANE
    first_row[...] = dot(owned[...], mirrors) + dot(jnp.where(low, 1.0, 0.0).astype(BF16), sums)


def second_mirror_kernel(got, pick, tiles, put, out):
    out[...] = exact_dot(put[...], multiply(exact_dot(pick[...], got[...]), tiles, False))


def inner_kernel(meet, energy, v_row, v_col, first_row, second_row, first_col, second_col, out):
    first_r, second_r = first_row[...], second_row[...]
    first = jnp.concatenate([first_r, first_col[...]], axis=0)
    second = jnp.concatenate([second_r, second_col[...]], axis=0)
    both = exact_dot(meet[...], jnp.concatenate([first, second], axis=1))
    image, total = both[:, :TILE], both[:, TILE:]
    width = v_row.shape[0]
    returned = iota(v_col.shape, 0) % LANE >= HALF
    first_c = jnp.where(returned, first_col[...], 0.0)
    second_c = jnp.where(returned, second_col[...], 0.0)

    def inner(a_r, b_r, a_c, b_c):
        return jnp.sum(a_r * b_r, axis=0, keepdims=True) + jnp.sum(a_c * b_c, axis=0, keepdims=True)

    values = [
        jnp.sum(energy[...], axis=0, keepdims=True),
        inner(v_row[...], first_r, v_col[...], first_c),
        inner(image[:width], first_r, image[width:], first_c),
        inner(v_row[...], second_r, v_col[...], second_c),
        inner(image[:width], second_r, image[width:], second_c),
        inner(total[:width], second_r, total[width:], second_c),
    ]
    packed = jnp.concatenate(values + [jnp.zeros((2, TILE), F32)], axis=0)
    for k in range(out.shape[0]):
        out[k] = packed


def partial_kernel(got, out):
    total = jnp.sum(got[...], axis=0)
    sums = jnp.sum(total, axis=1, keepdims=True)
    packed = jnp.sum(jnp.where(iota(total.shape, 0) == iota(total.shape, 1), sums, 0.0), axis=0, keepdims=True)
    out[...] = jnp.broadcast_to(packed, out.shape)


def spread_kernel(asked_row, asked_col, first_row, second_row, first_col, second_col, image, second):
    lanes = jnp.concatenate(product_lane(asked_row, asked_col), axis=1)
    rows = jnp.concatenate([first_row[...], second_row[...]], axis=1)
    columns = jnp.concatenate([first_col[...], second_col[...]], axis=1)
    high, low = halves(jnp.concatenate([rows, columns], axis=0))
    step = 256
    for start in range(0, image.shape[0], step):
        place = iota((step, lanes.shape[1]), 0) + start
        select = jnp.where(place == lanes, 1.0, 0.0).astype(BF16)
        both = dot(select, high) + dot(select, low)
        image[start : start + step, :] = both[:, :TILE]
        second[start : start + step, :] = both[:, TILE:]


def final_kernel(total, got, vector, image, second, out, alpha, rest, near, sems):
    sums = jnp.sum(got[...], axis=0, keepdims=True)
    lane = iota((1, TILE), 1)

    def value(k):
        return jnp.sum(jnp.where(lane == k, sums, 0.0), axis=1, keepdims=True)

    vv, vi, ii, vw, iw, ww = [value(k) for k in range(6)]
    g = 1.0 / (SCALE * jnp.sqrt(vv / (total * SCALE * SCALE) + 1e-06))
    c0 = g * (g * vi / total)
    square = g * (g * (ii - 2.0 * c0 * vi + c0 * c0 * vv) / total)
    b0 = jnp.sqrt(jnp.maximum(square, 0.0) + 1e-06)
    h = g / b0
    c10 = h * (g * (vw - c0 * vi) / total)
    c11 = h * (h * (iw - c0 * ii - c0 * vw + c0 * c0 * vi) / total)
    a = c0 + c11
    b = c11 * c0 - c10 * b0
    square = h * (h * (ww + a * a * ii + b * b * vv - 2.0 * a * iw + 2.0 * b * vw - 2.0 * a * b * vi) / total)
    b1 = jnp.sqrt(jnp.maximum(square, 0.0) + 1e-06)
    f = h / b1
    parts = sems.shape[0]
    step = vector.shape[0] // parts
    copies = []
    for k in range(parts):
        rows = pl.ds(k * step, step)
        v, i = vector[rows, :], image[rows, :]
        near[pl.ds(2 * k * step, step, 2), :] = h * i - (h * c0 * SCALE) * v
        near[pl.ds(2 * k * step + 1, step, 2), :] = f * second[rows, :] - (f * a) * i + (f * b * SCALE) * v
        done = pl.ds(2 * k * step, 2 * step)
        copies.append(pltpu.make_async_copy(near.at[done], out.at[done], sems.at[k]))
        copies[-1].start()
    alpha[0] = c0[0, 0]
    rest[0] = b0[0, 0]
    rest[1] = c11[0, 0]
    rest[2] = b1[0, 0]
    for copy in copies:
        copy.wait()


def shape(*dims, dtype=F32):
    return jax.ShapeDtypeStruct(dims, dtype)


def call(kernel, outs, *args, ins=VMEM, out_specs=VMEM, scratch=(), limit=16):
    if isinstance(outs, tuple) and not isinstance(out_specs, tuple):
        out_specs = tuple([out_specs] * len(outs))
    return pl.pallas_call(
        kernel,
        out_shape=outs,
        in_specs=[ins] * len(args),
        out_specs=out_specs,
        scratch_shapes=scratch,
        compiler_params=pltpu.CompilerParams(vmem_limit_bytes=limit * 1024 * 1024),
    )(*args)


def exchange(x, axis, count):
    sent = x.reshape(count, -1, TILE)
    got = lax.all_to_all(sent, axis, split_axis=0, concat_axis=0, tiled=True)
    return got.reshape(x.shape)


def per_device(start_vector, tile_blocks, row_owner, row_block, col_owner, col_block, tile_counts):
    tiles = tile_blocks[0, 0]
    count = tiles.shape[0]
    vector = start_vector.reshape(-1, TILE)
    pieces = vector.shape[0]
    n_row, n_col = lax.axis_size("row"), lax.axis_size("col")
    wide_r, wide_c = n_row * LANE, n_col * LANE
    every = wide_r + wide_c
    total = float(pieces * TILE * n_row * n_col)

    def over_row(x):
        return exchange(x, "row", n_row)

    def over_col(x):
        return exchange(x, "col", n_col)

    slots = jnp.concatenate(
        [x.reshape(1, count) for x in (row_owner, row_block, col_owner, col_block)]
        + [jnp.broadcast_to(tile_counts.reshape(1, 1), (1, count))],
        axis=0,
    )
    ask_row, ask_col, pick_row, put_row, pick_col, put_col, pick_pair, mine = call(
        functools.partial(request_kernel, pieces),
        (
            shape(wide_r, TILE, dtype=jnp.int32),
            shape(wide_c, TILE, dtype=jnp.int32),
            shape(count, wide_r, dtype=BF16),
            shape(wide_r, count, dtype=BF16),
            shape(count, wide_c, dtype=BF16),
            shape(wide_c, count, dtype=BF16),
            shape(count, 2 * wide_r, dtype=BF16),
            shape(count, TILE, dtype=jnp.int32),
        ),
        slots,
    )
    asked_row = over_row(ask_row)
    asked_col = over_col(ask_col)
    v_row, energy = call(gather_kernel, (shape(wide_r, TILE), shape(8, TILE)), asked_row, vector)
    x_col = over_row(v_row)
    first_col, v_col, meet, link, link_col, owned = call(
        direct_kernel,
        (
            shape(wide_c, TILE),
            shape(wide_c, TILE),
            shape(every, every, dtype=BF16),
            shape(count, n_row * count, dtype=BF16),
            shape(wide_c, n_row * count, dtype=BF16),
            shape(wide_r, n_row * count, dtype=BF16),
        ),
        x_col,
        pick_row,
        tiles,
        put_col,
        asked_row,
        asked_col,
        mine,
        vector,
    )
    first_col = over_col(first_col)
    packed = call(
        mirror_kernel,
        shape(n_row, count + 2 * LANE, TILE, dtype=BF16),
        first_col,
        pick_col,
        tiles,
        put_row,
        meet,
    )
    second_col, first_row = call(
        second_direct_kernel,
        (shape(wide_c, TILE), shape(wide_r, TILE)),
        over_row(packed),
        link,
        link_col,
        owned,
        pick_pair,
        meet,
        first_col,
        tiles,
        put_col,
    )
    second_col = over_col(second_col)
    second_row = over_row(
        call(second_mirror_kernel, shape(wide_r, TILE), second_col, pick_col, tiles, put_row)
    )
    products = (first_row, second_row, first_col, second_col)
    inner = call(inner_kernel, shape(n_row, 8, TILE), meet, energy, v_row, v_col, *products)
    inner = over_row(inner)
    image, second = call(
        spread_kernel, (shape(pieces, TILE), shape(pieces, TILE)), asked_row, asked_col, *products
    )
    inner = over_col(call(partial_kernel, shape(n_col, TILE), inner))

    def finish(*refs):
        final_kernel(total, *refs)

    out, alpha, rest = call(
        finish,
        (shape(2 * pieces, TILE), shape(1), shape(3)),
        inner,
        vector,
        image,
        second,
        out_specs=(HBM, SMEM, SMEM),
        scratch=[pltpu.VMEM((2 * pieces, TILE), F32), pltpu.SemaphoreType.DMA((4,))],
    )
    basis = out.reshape(pieces, 2, TILE).transpose(1, 0, 2).reshape(2, pieces * TILE)
    return (basis, alpha, rest)


def solution(mesh):
    return jax.shard_map(
        per_device,
        mesh=mesh,
        in_specs=(
            P(("row", "col")),
            P("row", "col", None, None, None),
            P("row", "col", None, None),
            P("row", "col", None),
            P("row", "col", None, None),
            P("row", "col", None),
            P("row", "col"),
        ),
        out_specs=(P(None, ("row", "col")), P(), P()),
        check_vma=False,
    )
```

```python
import functools

import jax
import jax.numpy as jnp
from jax import lax
from jax.experimental import pallas as pl
from jax.experimental.pallas import tpu as pltpu
from jax.sharding import PartitionSpec as P

TILE = 128
LANE = 8
HALF = 4
SCALE = 1024.0
F32 = jnp.float32
BF16 = jnp.bfloat16
VMEM = pl.BlockSpec(memory_space=pltpu.VMEM)
SMEM = pl.BlockSpec(memory_space=pltpu.SMEM)
HBM = pl.BlockSpec(memory_space=pltpu.HBM)


def iota(shape, axis):
    return lax.broadcasted_iota(jnp.int32, shape, axis)


def halves(x):
    high = x.astype(BF16)
    low = (x - high.astype(F32)).astype(BF16)
    return high, low


def dot(a, b):
    return jnp.dot(a, b, preferred_element_type=F32)


def exact_dot(select, x):
    high, low = halves(x)
    return dot(select, high) + dot(select, low)


def place_of(owner):
    count = owner.shape[1]
    shape = (count, count)
    down, across = iota(shape, 0), iota(shape, 1)
    column = jnp.sum(jnp.where(down == across, owner, 0.0), axis=1, keepdims=True)
    same = column == owner
    rank_row = jnp.sum(jnp.where(same & (down < across), 1.0, 0.0), axis=0, keepdims=True)
    rank_column = jnp.sum(jnp.where(same & (across < down), 1.0, 0.0), axis=1, keepdims=True)
    return (owner * LANE + rank_row).astype(jnp.int32), (column * LANE + rank_column).astype(jnp.int32)


def request_kernel(pieces, planes, slots, other, ask):
    n_x, n_z = planes
    me = slots[5:6, 0:1]
    x = slots[6:7, 0:1] // n_z
    count = slots.shape[1]
    width = ask.shape[0]
    spot = iota((width, count), 0)
    col = jnp.zeros((width, 1), F32)
    row = [[None, None], [None, None]]
    riders = []
    for core in range(2):
        these = jnp.where(me % 2 == core, slots[...], other[...])
        own_r, blk_r, own_c, blk_c, filled = [these[k : k + 1, :] for k in range(5)]
        alive = iota((1, count), 1) < filled
        place = place_of(own_r.astype(F32))[0] + HALF * core
        value = jnp.where(alive, blk_r + 1, 0).astype(F32)
        col = col + jnp.sum(jnp.where(spot == place, value, 0.0), axis=1, keepdims=True)
        place = place_of(own_c.astype(F32))[0]
        rank, chip = place % LANE, own_c // 2
        value = jnp.where(alive, blk_c + 1, 0).astype(F32)
        for side in range(2):
            there = (spot == (chip * n_x + x) * LANE + rank) & (own_c % 2 == side)
            row[core][side] = jnp.sum(jnp.where(there, value, 0.0), axis=1, keepdims=True)
        riders.append((alive, own_c, blk_c, place))
    lane = iota((width, TILE), 1)
    down = iota((width, TILE), 0)
    quarter = lane // 16
    values = jnp.broadcast_to(row[0][0], (width, TILE))
    for k in range(1, 4):
        values = jnp.where(quarter == k, row[k // 2][k % 2], values)
    values = values.astype(jnp.int32) - 1
    for core, (alive, own_c, blk_c, place) in enumerate(riders):
        ident = jnp.where(alive, own_c * pieces + blk_c, -1)
        for k, rider in ((core, ident), (2 + core, place)):
            twice = jnp.concatenate([rider, rider], axis=1)
            values = jnp.where((lane >= count) & (down % LANE == k), twice, values)
    values = jnp.where(down // LANE % n_x == x, values, -9)
    ask[...] = jnp.where(me % 2 == 0, jnp.broadcast_to(col, (width, TILE)).astype(jnp.int32) - 1, values)


def local_kernel(pieces, slots, vector, tiles, pick_row, put_row, pick_col, put_col, pick_pair, mine, energy):
    own_r, blk_r, own_c, blk_c, filled = [slots[k : k + 1, :] for k in range(5)]
    count = slots.shape[1]
    for owner, pick, put, shift in ((own_c, pick_row, put_row, 0), (own_r, pick_col, put_col, HALF)):
        width = put.shape[0]
        across, down = place_of(owner.astype(F32))
        pick[...] = jnp.where(iota((count, width), 1) == down, 1.0, 0.0).astype(BF16)
        put[...] = jnp.where(iota((width, count), 0) == across + shift, 1.0, 0.0).astype(BF16)
    ident = jnp.where(iota((1, count), 1) < filled, own_c * pieces + blk_c, -2)
    across = iota((count, count), 0) == iota((count, count), 1)
    down = jnp.sum(jnp.where(across, ident.astype(F32), 0.0), axis=1, keepdims=True).astype(jnp.int32)
    mine[...] = jnp.broadcast_to(down, mine.shape)
    place = place_of(own_c.astype(F32))[1]
    high = place + place // LANE * LANE
    pick_pair[...] = jnp.where(iota(pick_pair.shape, 1) == high, 1.0, 0.0).astype(BF16)
    v = vector[...] * SCALE
    energy[...] = jnp.sum((v * v).reshape(-1, 8, TILE), axis=0)


def first_lane(asked):
    return jnp.broadcast_to(asked[:, 0:1], asked.shape)


def gather(asked, vector):
    pieces = vector.shape[0]
    rows = asked.shape[0]
    lanes = iota((rows, TILE), 1)
    select = jnp.concatenate(
        [jnp.where(asked == lanes + k * TILE, 1.0, 0.0).astype(BF16) for k in range(pieces // TILE)], axis=1
    )
    return exact_dot(select, vector)


def served_kernel(n_x, slots, got, other, vector, asked_row, asked_col, out):
    me = slots[5:6, 0:1]
    first = me % 2 == 0
    width = asked_col.shape[0]
    col = jnp.where(first, got[...], other[...]).reshape(-1, LANE, TILE)
    swapped = jnp.concatenate([col[:, HALF:, :], col[:, :HALF, :]], axis=1)
    lower = iota(col.shape, 1) < HALF
    keep = lower == first.reshape(1, 1, 1)
    asked_col[...] = jnp.where(keep, col, swapped).reshape(width, TILE)
    row = jnp.max(jnp.where(first, other[...], got[...]).reshape(-1, n_x, LANE, TILE), axis=1)
    slot = iota(row.shape, 1)
    lane = iota(row.shape, 2)
    asked, full = [], []
    for core in range(2):
        sides = [jnp.broadcast_to(row[:, :, 16 * k : 16 * k + 1], row.shape) for k in (2 * core, 2 * core + 1)]
        value = jnp.where(first.reshape(1, 1, 1), sides[0], sides[1])
        riders = jnp.where(slot % 2 == 0, row[:, core : core + 1, :], row[:, 2 + core : 3 + core, :])
        count = TILE // 2
        mixed = jnp.where(lane >= count, riders, jnp.where(lane == count - 1, me.reshape(1, 1, 1), value))
        asked.append(value)
        full.append(mixed)
    shape = asked_row.shape
    asked_row[...] = jnp.stack(full, axis=1).reshape(shape)
    out[...] = gather(jnp.stack(asked, axis=1).reshape(shape), vector[...] * SCALE)


def product_lane(asked_row, asked_col):
    rows = [first_lane(asked_row[...]).astype(F32).T[0:1, :]]
    width = asked_col.shape[0]
    for k in range(width // TILE):
        part = asked_col[k * TILE : (k + 1) * TILE, :].astype(F32).T[0:1, :]
        lane = iota((1, TILE), 1)
        rows.append(jnp.where(lane % LANE >= HALF, part, -2.0))
    return [row.astype(jnp.int32) for row in rows]


def meet_tables(asked_row, asked_col, mine, pieces, meet, link, link_col, owned):
    lanes = product_lane(asked_row, asked_col)
    base = 0
    served_row, served_col = first_lane(asked_row[...]), asked_col[...]
    for served in (served_row, served_col):
        for k, lane in enumerate(lanes):
            hit = (served == lane) & (served >= 0)
            meet[base : base + served.shape[0], k * TILE : (k + 1) * TILE] = jnp.where(hit, 1.0, 0.0).astype(BF16)
        base += served.shape[0]
    count = mine.shape[0]
    index = asked_row[0:1, count - 1 : count]
    ident = jnp.where(served_col < 0, -3, served_col + index * pieces)
    lane = iota((1, TILE), 1)
    slot = iota(owned.shape[:1] + (TILE,), 0)
    half = iota(owned.shape[:1] + (TILE,), 1) // count
    for k in range(asked_row.shape[0] // (2 * LANE)):
        start = 2 * k * LANE
        even = [asked_row[start + j : start + j + 1, :] for j in range(2)]
        odd = [asked_row[start + LANE + j : start + LANE + j + 1, :] for j in range(2)]
        ids, spots = [jnp.where(lane < count, pltpu.roll(a, count, 1), b) for a, b in zip(even, odd)]
        cols = slice(k * TILE, (k + 1) * TILE)
        link[:, cols] = jnp.where(mine[...] == ids, 1.0, 0.0).astype(BF16)
        link_col[:, cols] = jnp.where(ident == ids, 1.0, 0.0).astype(BF16)
        sent = (spots == index * LANE + slot % LANE) & (slot // LANE == 2 * k + half)
        owned[:, cols] = jnp.where(sent, 1.0, 0.0).astype(BF16)


def multiply(x, tiles, across):
    count = x.shape[0]
    dims = (((1,), (1 if across else 0,)), ((), ()))
    row = iota((8, TILE), 0)
    groups = []
    for g in range(count // 8):
        part = x[g * 8 : (g + 1) * 8, :]
        high = part.astype(BF16).astype(F32)
        both = jnp.concatenate([high, part - high], axis=0).astype(BF16)
        total = jnp.zeros((8, TILE), F32)
        for j in range(8):
            y = lax.dot_general(both, tiles[g * 8 + j], dims, preferred_element_type=F32)
            total = jnp.where(row == j, y[0:8] + y[8:16], total)
        groups.append(total)
    return jnp.concatenate(groups, axis=0)


def direct_kernel(
    got, pick, tiles, put, asked_row, asked_col, mine, vector, out, v_col, meet, link, link_col, owned
):
    y = multiply(exact_dot(pick[...], got[...]), tiles, True)
    v = gather(asked_col[...], vector[...] * SCALE)
    v_col[...] = v
    forward = iota(v.shape, 0) % LANE < HALF
    out[...] = exact_dot(put[...], y) + jnp.where(forward, v, 0.0)
    meet_tables(asked_row, asked_col, mine, vector.shape[0], meet, link, link_col, owned)


def mirror_kernel(got, pick, tiles, put, meet, out):
    y = multiply(exact_dot(pick[...], got[...]), tiles, False)
    high, low = halves(y)
    width = put.shape[0]
    total = exact_dot(meet[:width, width:], got[...])
    low = dot(put[...], low)
    count = y.shape[0]
    for k in range(out.shape[0]):
        rows = slice(k * LANE, (k + 1) * LANE)
        out[k, :count, :] = high
        out[k, count:, :] = jnp.concatenate([total[rows], low[rows]], axis=0).astype(BF16)


def second_direct_kernel(got, link, link_col, owned, pick, meet, first_col, tiles, put, out, first_row):
    count = link.shape[0]
    peers = range(got.shape[0])
    mirrors = jnp.concatenate([got[k, :count, :] for k in peers], axis=0)
    sums = jnp.concatenate([got[k, count:, :] for k in peers], axis=0)
    y = multiply(dot(link[...], mirrors) + dot(pick[...], sums), tiles, True)
    width = got.shape[0] * LANE
    image = dot(link_col[...], mirrors) + exact_dot(meet[width:, width:], first_col[...])
    forward = iota(image.shape, 0) % LANE < HALF
    out[...] = exact_dot(put[...], y) + jnp.where(forward, image, 0.0)
    slot = iota((width, 2 * width), 0)
    low = iota((width, 2 * width), 1) == slot + slot // LANE * LANE + LANE
    first_row[...] = dot(owned[...], mirrors) + dot(jnp.where(low, 1.0, 0.0).astype(BF16), sums)


def second_mirror_kernel(got, pick, tiles, put, out):
    out[...] = exact_dot(put[...], multiply(exact_dot(pick[...], got[...]), tiles, False))


def inner_kernel(meet, energy, v_row, v_col, first_row, second_row, first_col, second_col, out):
    first_r, second_r = first_row[...], second_row[...]
    first = jnp.concatenate([first_r, first_col[...]], axis=0)
    second = jnp.concatenate([second_r, second_col[...]], axis=0)
    both = exact_dot(meet[...], jnp.concatenate([first, second], axis=1))
    image, total = both[:, :TILE], both[:, TILE:]
    width = v_row.shape[0]
    returned = iota(v_col.shape, 0) % LANE >= HALF
    first_c = jnp.where(returned, first_col[...], 0.0)
    second_c = jnp.where(returned, second_col[...], 0.0)

    def inner(a_r, b_r, a_c, b_c):
        return jnp.sum(a_r * b_r, axis=0, keepdims=True) + jnp.sum(a_c * b_c, axis=0, keepdims=True)

    values = [
        jnp.sum(energy[...], axis=0, keepdims=True),
        inner(v_row[...], first_r, v_col[...], first_c),
        inner(image[:width], first_r, image[width:], first_c),
        inner(v_row[...], second_r, v_col[...], second_c),
        inner(image[:width], second_r, image[width:], second_c),
        inner(total[:width], second_r, total[width:], second_c),
    ]
    packed = jnp.concatenate(values + [jnp.zeros((2, TILE), F32)], axis=0)
    for k in range(out.shape[0]):
        out[k] = packed


def partial_kernel(got, out):
    total = jnp.sum(got[...], axis=0)
    sums = jnp.sum(total, axis=1, keepdims=True)
    packed = jnp.sum(jnp.where(iota(total.shape, 0) == iota(total.shape, 1), sums, 0.0), axis=0, keepdims=True)
    out[...] = jnp.broadcast_to(packed, out.shape)


def spread_kernel(asked_row, asked_col, first_row, second_row, first_col, second_col, image, second):
    lanes = jnp.concatenate(product_lane(asked_row, asked_col), axis=1)
    rows = jnp.concatenate([first_row[...], second_row[...]], axis=1)
    columns = jnp.concatenate([first_col[...], second_col[...]], axis=1)
    high, low = halves(jnp.concatenate([rows, columns], axis=0))
    step = 256
    for start in range(0, image.shape[0], step):
        place = iota((step, lanes.shape[1]), 0) + start
        select = jnp.where(place == lanes, 1.0, 0.0).astype(BF16)
        both = dot(select, high) + dot(select, low)
        image[start : start + step, :] = both[:, :TILE]
        second[start : start + step, :] = both[:, TILE:]


def final_kernel(total, got, vector, image, second, out, alpha, rest, near, sems):
    sums = jnp.sum(got[...], axis=0, keepdims=True)
    lane = iota((1, TILE), 1)

    def value(k):
        return jnp.sum(jnp.where(lane == k, sums, 0.0), axis=1, keepdims=True)

    vv, vi, ii, vw, iw, ww = [value(k) for k in range(6)]
    g = 1.0 / (SCALE * jnp.sqrt(vv / (total * SCALE * SCALE) + 1e-06))
    c0 = g * (g * vi / total)
    square = g * (g * (ii - 2.0 * c0 * vi + c0 * c0 * vv) / total)
    b0 = jnp.sqrt(jnp.maximum(square, 0.0) + 1e-06)
    h = g / b0
    c10 = h * (g * (vw - c0 * vi) / total)
    c11 = h * (h * (iw - c0 * ii - c0 * vw + c0 * c0 * vi) / total)
    a = c0 + c11
    b = c11 * c0 - c10 * b0
    square = h * (h * (ww + a * a * ii + b * b * vv - 2.0 * a * iw + 2.0 * b * vw - 2.0 * a * b * vi) / total)
    b1 = jnp.sqrt(jnp.maximum(square, 0.0) + 1e-06)
    f = h / b1
    parts = sems.shape[0]
    step = vector.shape[0] // parts
    copies = []
    for k in range(parts):
        rows = pl.ds(k * step, step)
        v, i = vector[rows, :], image[rows, :]
        near[pl.ds(2 * k * step, step, 2), :] = h * i - (h * c0 * SCALE) * v
        near[pl.ds(2 * k * step + 1, step, 2), :] = f * second[rows, :] - (f * a) * i + (f * b * SCALE) * v
        done = pl.ds(2 * k * step, 2 * step)
        copies.append(pltpu.make_async_copy(near.at[done], out.at[done], sems.at[k]))
        copies[-1].start()
    alpha[0] = c0[0, 0]
    rest[0] = b0[0, 0]
    rest[1] = c11[0, 0]
    rest[2] = b1[0, 0]
    for copy in copies:
        copy.wait()


def shape(*dims, dtype=F32):
    return jax.ShapeDtypeStruct(dims, dtype)


def call(kernel, outs, *args, ins=VMEM, out_specs=VMEM, scratch=(), limit=16):
    if isinstance(outs, tuple) and not isinstance(out_specs, tuple):
        out_specs = tuple([out_specs] * len(outs))
    return pl.pallas_call(
        kernel,
        out_shape=outs,
        in_specs=[ins] * len(args),
        out_specs=out_specs,
        scratch_shapes=scratch,
        compiler_params=pltpu.CompilerParams(vmem_limit_bytes=limit * 1024 * 1024),
    )(*args)


def exchange(x, axis, count):
    sent = x.reshape(count, -1, TILE)
    got = lax.all_to_all(sent, axis, split_axis=0, concat_axis=0, tiled=True)
    return got.reshape(x.shape)


def per_device(start_vector, tile_blocks, row_owner, row_block, col_owner, col_block, tile_counts):
    tiles = tile_blocks[0, 0]
    count = tiles.shape[0]
    vector = start_vector.reshape(-1, TILE)
    pieces = vector.shape[0]
    n_row, n_col = lax.axis_size("row"), lax.axis_size("col")
    wide_r, wide_c = n_row * LANE, n_col * LANE
    every = wide_r + wide_c
    total = float(pieces * TILE * n_row * n_col)

    def over_row(x):
        return exchange(x, "row", n_row)

    def over_col(x):
        return exchange(x, "col", n_col)

    n_y = n_row // 2
    n_x = n_col // n_y
    n_z = n_col // n_x
    small = [row_owner, row_block, col_owner, col_block, tile_counts]
    small += [lax.axis_index("row"), lax.axis_index("col"), jnp.zeros((), jnp.int32)]
    slots = jnp.concatenate(
        [jnp.broadcast_to(x.reshape(1, -1), (1, count)).astype(jnp.int32) for x in small], axis=0
    )
    planes = [[2 * y * n_col + c for c in range(n_col)] for y in range(n_y)]
    planes += [[(2 * y + 1) * n_col + x * n_z + z for y in range(n_y) for x in range(n_x)] for z in range(n_z)]

    def other_core(x):
        return lax.ppermute(x, "row", [(r, r ^ 1) for r in range(n_row)])

    ask = call(
        functools.partial(request_kernel, pieces, (n_x, n_z)),
        shape(wide_c, TILE, dtype=jnp.int32),
        slots,
        other_core(slots),
    )
    ask = lax.all_to_all(
        ask.reshape(n_col, LANE, TILE),
        ("row", "col"),
        split_axis=0,
        concat_axis=0,
        axis_index_groups=planes,
        tiled=True,
    ).reshape(wide_c, TILE)
    pick_row, put_row, pick_col, put_col, pick_pair, mine, energy = call(
        functools.partial(local_kernel, pieces),
        (
            shape(count, wide_r, dtype=BF16),
            shape(wide_r, count, dtype=BF16),
            shape(count, wide_c, dtype=BF16),
            shape(wide_c, count, dtype=BF16),
            shape(count, 2 * wide_r, dtype=BF16),
            shape(count, TILE, dtype=jnp.int32),
            shape(8, TILE),
        ),
        slots,
        vector,
        tiles,
    )
    asked_row, asked_col, v_row = call(
        functools.partial(served_kernel, n_x),
        (
            shape(wide_r, TILE, dtype=jnp.int32),
            shape(wide_c, TILE, dtype=jnp.int32),
            shape(wide_r, TILE),
        ),
        slots,
        ask,
        other_core(ask),
        vector,
    )
    x_col = over_row(v_row)
    first_col, v_col, meet, link, link_col, owned = call(
        direct_kernel,
        (
            shape(wide_c, TILE),
            shape(wide_c, TILE),
            shape(every, every, dtype=BF16),
            shape(count, n_row * count, dtype=BF16),
            shape(wide_c, n_row * count, dtype=BF16),
            shape(wide_r, n_row * count, dtype=BF16),
        ),
        x_col,
        pick_row,
        tiles,
        put_col,
        asked_row,
        asked_col,
        mine,
        vector,
    )
    first_col = over_col(first_col)
    packed = call(
        mirror_kernel,
        shape(n_row, count + 2 * LANE, TILE, dtype=BF16),
        first_col,
        pick_col,
        tiles,
        put_row,
        meet,
    )
    second_col, first_row = call(
        second_direct_kernel,
        (shape(wide_c, TILE), shape(wide_r, TILE)),
        over_row(packed),
        link,
        link_col,
        owned,
        pick_pair,
        meet,
        first_col,
        tiles,
        put_col,
    )
    second_col = over_col(second_col)
    second_row = over_row(
        call(second_mirror_kernel, shape(wide_r, TILE), second_col, pick_col, tiles, put_row)
    )
    products = (first_row, second_row, first_col, second_col)
    inner = call(inner_kernel, shape(n_row, 8, TILE), meet, energy, v_row, v_col, *products)
    inner = over_row(inner)
    image, second = call(
        spread_kernel, (shape(pieces, TILE), shape(pieces, TILE)), asked_row, asked_col, *products
    )
    inner = over_col(call(partial_kernel, shape(n_col, TILE), inner))

    def finish(*refs):
        final_kernel(total, *refs)

    out, alpha, rest = call(
        finish,
        (shape(2 * pieces, TILE), shape(1), shape(3)),
        inner,
        vector,
        image,
        second,
        out_specs=(HBM, SMEM, SMEM),
        scratch=[pltpu.VMEM((2 * pieces, TILE), F32), pltpu.SemaphoreType.DMA((4,))],
    )
    basis = out.reshape(pieces, 2, TILE).transpose(1, 0, 2).reshape(2, pieces * TILE)
    return (basis, alpha, rest)


def solution(mesh):
    return jax.shard_map(
        per_device,
        mesh=mesh,
        in_specs=(
            P(("row", "col")),
            P("row", "col", None, None, None),
            P("row", "col", None, None),
            P("row", "col", None),
            P("row", "col", None, None),
            P("row", "col", None),
            P("row", "col"),
        ),
        out_specs=(P(None, ("row", "col")), P(), P()),
        check_vma=False,
    )
```

```python
import functools

import jax
import jax.numpy as jnp
from jax import lax
from jax.experimental import pallas as pl
from jax.experimental.pallas import tpu as pltpu
from jax.sharding import PartitionSpec as P

TILE = 128
LANE = 8
HALF = 4
SCALE = 1024.0
F32 = jnp.float32
BF16 = jnp.bfloat16
VMEM = pl.BlockSpec(memory_space=pltpu.VMEM)
SMEM = pl.BlockSpec(memory_space=pltpu.SMEM)
HBM = pl.BlockSpec(memory_space=pltpu.HBM)


def iota(shape, axis):
    return lax.broadcasted_iota(jnp.int32, shape, axis)


def halves(x):
    high = x.astype(BF16)
    low = (x - high.astype(F32)).astype(BF16)
    return high, low


def dot(a, b):
    return jnp.dot(a, b, preferred_element_type=F32)


def exact_dot(select, x):
    high, low = halves(x)
    return dot(select, high) + dot(select, low)


def place_of(owner):
    count = owner.shape[1]
    shape = (count, count)
    down, across = iota(shape, 0), iota(shape, 1)
    column = jnp.sum(jnp.where(down == across, owner, 0.0), axis=1, keepdims=True)
    same = column == owner
    rank_row = jnp.sum(jnp.where(same & (down < across), 1.0, 0.0), axis=0, keepdims=True)
    rank_column = jnp.sum(jnp.where(same & (across < down), 1.0, 0.0), axis=1, keepdims=True)
    return (owner * LANE + rank_row).astype(jnp.int32), (column * LANE + rank_column).astype(jnp.int32)


def request_kernel(pieces, planes, slots, both, ask):
    n_x, n_z = planes
    me = slots[5:6, 0:1]
    x = slots[6:7, 0:1] // n_z
    count = slots.shape[1]
    width = ask.shape[0]
    spot = iota((width, count), 0)
    col = jnp.zeros((width, 1), F32)
    row = [[None, None], [None, None]]
    riders = []
    for core in range(2):
        own_r, blk_r, own_c, blk_c, filled = [both[8 * core + k : 8 * core + k + 1, :] for k in range(5)]
        alive = iota((1, count), 1) < filled
        place = place_of(own_r.astype(F32))[0] + HALF * core
        value = jnp.where(alive, blk_r + 1, 0).astype(F32)
        col = col + jnp.sum(jnp.where(spot == place, value, 0.0), axis=1, keepdims=True)
        place = place_of(own_c.astype(F32))[0]
        rank, chip = place % LANE, own_c // 2
        value = jnp.where(alive, blk_c + 1, 0).astype(F32)
        for side in range(2):
            there = (spot == (chip * n_x + x) * LANE + rank) & (own_c % 2 == side)
            row[core][side] = jnp.sum(jnp.where(there, value, 0.0), axis=1, keepdims=True)
        riders.append((alive, own_c, blk_c, place))
    lane = iota((width, TILE), 1)
    down = iota((width, TILE), 0)
    quarter = lane // 16
    values = jnp.broadcast_to(row[0][0], (width, TILE))
    for k in range(1, 4):
        values = jnp.where(quarter == k, row[k // 2][k % 2], values)
    values = values.astype(jnp.int32) - 1
    for core, (alive, own_c, blk_c, place) in enumerate(riders):
        ident = jnp.where(alive, own_c * pieces + blk_c, -1)
        for k, rider in ((core, ident), (2 + core, place)):
            twice = jnp.concatenate([rider, rider], axis=1)
            values = jnp.where((lane >= count) & (down % LANE == k), twice, values)
    values = jnp.where(down // LANE % n_x == x, values, -9)
    ask[...] = jnp.where(me % 2 == 0, jnp.broadcast_to(col, (width, TILE)).astype(jnp.int32) - 1, values)


def local_kernel(pieces, slots, vector, tiles, pick_row, put_row, pick_col, put_col, pick_pair, mine, energy):
    own_r, blk_r, own_c, blk_c, filled = [slots[k : k + 1, :] for k in range(5)]
    count = slots.shape[1]
    for owner, pick, put, shift in ((own_c, pick_row, put_row, 0), (own_r, pick_col, put_col, HALF)):
        width = put.shape[0]
        across, down = place_of(owner.astype(F32))
        pick[...] = jnp.where(iota((count, width), 1) == down, 1.0, 0.0).astype(BF16)
        put[...] = jnp.where(iota((width, count), 0) == across + shift, 1.0, 0.0).astype(BF16)
    ident = jnp.where(iota((1, count), 1) < filled, own_c * pieces + blk_c, -2)
    across = iota((count, count), 0) == iota((count, count), 1)
    down = jnp.sum(jnp.where(across, ident.astype(F32), 0.0), axis=1, keepdims=True).astype(jnp.int32)
    mine[...] = jnp.broadcast_to(down, mine.shape)
    place = place_of(own_c.astype(F32))[1]
    high = place + place // LANE * LANE
    pick_pair[...] = jnp.where(iota(pick_pair.shape, 1) == high, 1.0, 0.0).astype(BF16)
    v = vector[...] * SCALE
    energy[...] = jnp.sum((v * v).reshape(-1, 8, TILE), axis=0)


def first_lane(asked):
    return jnp.broadcast_to(asked[:, 0:1], asked.shape)


def gather(asked, vector):
    pieces = vector.shape[0]
    rows = asked.shape[0]
    lanes = iota((rows, TILE), 1)
    select = jnp.concatenate(
        [jnp.where(asked == lanes + k * TILE, 1.0, 0.0).astype(BF16) for k in range(pieces // TILE)], axis=1
    )
    return exact_dot(select, vector)


def served_kernel(n_x, slots, pair, vector, squares, asked_row, asked_col, out, energy):
    me = slots[5:6, 0:1]
    first = me % 2 == 0
    width = asked_col.shape[0]
    col = pair[:width, :].reshape(-1, LANE, TILE)
    swapped = jnp.concatenate([col[:, HALF:, :], col[:, :HALF, :]], axis=1)
    lower = iota(col.shape, 1) < HALF
    keep = lower == first.reshape(1, 1, 1)
    asked_col[...] = jnp.where(keep, col, swapped).reshape(width, TILE)
    row = jnp.max(pair[width:, :].reshape(-1, n_x, LANE, TILE), axis=1)
    slot = iota(row.shape, 1)
    lane = iota(row.shape, 2)
    asked, full = [], []
    for core in range(2):
        sides = [jnp.broadcast_to(row[:, :, 16 * k : 16 * k + 1], row.shape) for k in (2 * core, 2 * core + 1)]
        value = jnp.where(first.reshape(1, 1, 1), sides[0], sides[1])
        riders = jnp.where(slot % 2 == 0, row[:, core : core + 1, :], row[:, 2 + core : 3 + core, :])
        count = TILE // 2
        mixed = jnp.where(lane >= count, riders, jnp.where(lane == count - 1, me.reshape(1, 1, 1), value))
        asked.append(value)
        full.append(mixed)
    shape = asked_row.shape
    asked_row[...] = jnp.stack(full, axis=1).reshape(shape)
    out[...] = gather(jnp.stack(asked, axis=1).reshape(shape), vector[...] * SCALE)
    energy[...] = jnp.sum(squares[...], axis=0, keepdims=True)


def product_lane(asked_row, asked_col):
    rows = [first_lane(asked_row[...]).astype(F32).T[0:1, :]]
    width = asked_col.shape[0]
    for k in range(width // TILE):
        part = asked_col[k * TILE : (k + 1) * TILE, :].astype(F32).T[0:1, :]
        lane = iota((1, TILE), 1)
        rows.append(jnp.where(lane % LANE >= HALF, part, -2.0))
    return [row.astype(jnp.int32) for row in rows]


def meet_tables(asked_row, asked_col, mine, pieces, meet, link, link_col, owned):
    lanes = product_lane(asked_row, asked_col)
    base = 0
    served_row, served_col = first_lane(asked_row[...]), asked_col[...]
    for served in (served_row, served_col):
        for k, lane in enumerate(lanes):
            hit = (served == lane) & (served >= 0)
            meet[base : base + served.shape[0], k * TILE : (k + 1) * TILE] = jnp.where(hit, 1.0, 0.0).astype(BF16)
        base += served.shape[0]
    count = mine.shape[0]
    index = asked_row[0:1, count - 1 : count]
    ident = jnp.where(served_col < 0, -3, served_col + index * pieces)
    lane = iota((1, TILE), 1)
    slot = iota(owned.shape[:1] + (TILE,), 0)
    half = iota(owned.shape[:1] + (TILE,), 1) // count
    for k in range(asked_row.shape[0] // (2 * LANE)):
        start = 2 * k * LANE
        even = [asked_row[start + j : start + j + 1, :] for j in range(2)]
        odd = [asked_row[start + LANE + j : start + LANE + j + 1, :] for j in range(2)]
        ids, spots = [jnp.where(lane < count, pltpu.roll(a, count, 1), b) for a, b in zip(even, odd)]
        cols = slice(k * TILE, (k + 1) * TILE)
        link[:, cols] = jnp.where(mine[...] == ids, 1.0, 0.0).astype(BF16)
        link_col[:, cols] = jnp.where(ident == ids, 1.0, 0.0).astype(BF16)
        sent = (spots == index * LANE + slot % LANE) & (slot // LANE == 2 * k + half)
        owned[:, cols] = jnp.where(sent, 1.0, 0.0).astype(BF16)


def multiply(x, tiles, across):
    count = x.shape[0]
    dims = (((1,), (1 if across else 0,)), ((), ()))
    row = iota((8, TILE), 0)
    groups = []
    for g in range(count // 8):
        part = x[g * 8 : (g + 1) * 8, :]
        high = part.astype(BF16).astype(F32)
        both = jnp.concatenate([high, part - high], axis=0).astype(BF16)
        total = jnp.zeros((8, TILE), F32)
        for j in range(8):
            y = lax.dot_general(both, tiles[g * 8 + j], dims, preferred_element_type=F32)
            total = jnp.where(row == j, y[0:8] + y[8:16], total)
        groups.append(total)
    return jnp.concatenate(groups, axis=0)


def direct_kernel(
    got, pick, tiles, put, asked_row, asked_col, mine, vector, out, v_col, meet, link, link_col, owned
):
    y = multiply(exact_dot(pick[...], got[...]), tiles, True)
    v = gather(asked_col[...], vector[...] * SCALE)
    v_col[...] = v
    forward = iota(v.shape, 0) % LANE < HALF
    out[...] = exact_dot(put[...], y) + jnp.where(forward, v, 0.0)
    meet_tables(asked_row, asked_col, mine, vector.shape[0], meet, link, link_col, owned)


def mirror_kernel(got, pick, tiles, put, meet, out):
    y = multiply(exact_dot(pick[...], got[...]), tiles, False)
    high, low = halves(y)
    width = put.shape[0]
    total = exact_dot(meet[:width, width:], got[...])
    low = dot(put[...], low)
    count = y.shape[0]
    for k in range(out.shape[0]):
        rows = slice(k * LANE, (k + 1) * LANE)
        out[k, :count, :] = high
        out[k, count:, :] = jnp.concatenate([total[rows], low[rows]], axis=0).astype(BF16)


def second_direct_kernel(got, link, link_col, owned, pick, meet, first_col, tiles, put, out, first_row):
    count = link.shape[0]
    peers = range(got.shape[0])
    mirrors = jnp.concatenate([got[k, :count, :] for k in peers], axis=0)
    sums = jnp.concatenate([got[k, count:, :] for k in peers], axis=0)
    y = multiply(dot(link[...], mirrors) + dot(pick[...], sums), tiles, True)
    width = got.shape[0] * LANE
    image = dot(link_col[...], mirrors) + exact_dot(meet[width:, width:], first_col[...])
    forward = iota(image.shape, 0) % LANE < HALF
    out[...] = exact_dot(put[...], y) + jnp.where(forward, image, 0.0)
    slot = iota((width, 2 * width), 0)
    low = iota((width, 2 * width), 1) == slot + slot // LANE * LANE + LANE
    first_row[...] = dot(owned[...], mirrors) + dot(jnp.where(low, 1.0, 0.0).astype(BF16), sums)


def second_mirror_kernel(got, pick, tiles, put, out):
    out[...] = exact_dot(put[...], multiply(exact_dot(pick[...], got[...]), tiles, False))


def inner_kernel(meet, energy, v_row, v_col, first_row, second_row, first_col, second_col, out):
    first_r, second_r = first_row[...], second_row[...]
    first = jnp.concatenate([first_r, first_col[...]], axis=0)
    second = jnp.concatenate([second_r, second_col[...]], axis=0)
    both = exact_dot(meet[...], jnp.concatenate([first, second], axis=1))
    image, total = both[:, :TILE], both[:, TILE:]
    width = v_row.shape[0]
    returned = iota(v_col.shape, 0) % LANE >= HALF
    first_c = jnp.where(returned, first_col[...], 0.0)
    second_c = jnp.where(returned, second_col[...], 0.0)

    def inner(a_r, b_r, a_c, b_c):
        return jnp.sum(a_r * b_r, axis=0, keepdims=True) + jnp.sum(a_c * b_c, axis=0, keepdims=True)

    values = [
        energy[...],
        inner(v_row[...], first_r, v_col[...], first_c),
        inner(image[:width], first_r, image[width:], first_c),
        inner(v_row[...], second_r, v_col[...], second_c),
        inner(image[:width], second_r, image[width:], second_c),
        inner(total[:width], second_r, total[width:], second_c),
    ]
    packed = jnp.concatenate(values + [jnp.zeros((2, TILE), F32)], axis=0)
    for k in range(out.shape[0]):
        out[k] = packed


def partial_kernel(got, out):
    total = jnp.sum(got[...], axis=0)
    sums = jnp.sum(total, axis=1, keepdims=True)
    packed = jnp.sum(jnp.where(iota(total.shape, 0) == iota(total.shape, 1), sums, 0.0), axis=0, keepdims=True)
    out[...] = jnp.broadcast_to(packed, out.shape)


def spread_kernel(asked_row, asked_col, first_row, second_row, first_col, second_col, image, second):
    lanes = jnp.concatenate(product_lane(asked_row, asked_col), axis=1)
    rows = jnp.concatenate([first_row[...], second_row[...]], axis=1)
    columns = jnp.concatenate([first_col[...], second_col[...]], axis=1)
    high, low = halves(jnp.concatenate([rows, columns], axis=0))
    step = 256
    for start in range(0, image.shape[0], step):
        place = iota((step, lanes.shape[1]), 0) + start
        select = jnp.where(place == lanes, 1.0, 0.0).astype(BF16)
        both = dot(select, high) + dot(select, low)
        image[start : start + step, :] = both[:, :TILE]
        second[start : start + step, :] = both[:, TILE:]


def final_kernel(total, got, vector, image, second, out, alpha, rest, near, sems):
    sums = jnp.sum(got[...], axis=0, keepdims=True)
    lane = iota((1, TILE), 1)

    def value(k):
        return jnp.sum(jnp.where(lane == k, sums, 0.0), axis=1, keepdims=True)

    vv, vi, ii, vw, iw, ww = [value(k) for k in range(6)]
    g = 1.0 / (SCALE * jnp.sqrt(vv / (total * SCALE * SCALE) + 1e-06))
    c0 = g * (g * vi / total)
    square = g * (g * (ii - 2.0 * c0 * vi + c0 * c0 * vv) / total)
    b0 = jnp.sqrt(jnp.maximum(square, 0.0) + 1e-06)
    h = g / b0
    c10 = h * (g * (vw - c0 * vi) / total)
    c11 = h * (h * (iw - c0 * ii - c0 * vw + c0 * c0 * vi) / total)
    a = c0 + c11
    b = c11 * c0 - c10 * b0
    square = h * (h * (ww + a * a * ii + b * b * vv - 2.0 * a * iw + 2.0 * b * vw - 2.0 * a * b * vi) / total)
    b1 = jnp.sqrt(jnp.maximum(square, 0.0) + 1e-06)
    f = h / b1
    parts = sems.shape[0]
    step = vector.shape[0] // parts
    copies = []
    for k in range(parts):
        rows = pl.ds(k * step, step)
        v, i = vector[rows, :], image[rows, :]
        near[pl.ds(2 * k * step, step, 2), :] = h * i - (h * c0 * SCALE) * v
        near[pl.ds(2 * k * step + 1, step, 2), :] = f * second[rows, :] - (f * a) * i + (f * b * SCALE) * v
        done = pl.ds(2 * k * step, 2 * step)
        copies.append(pltpu.make_async_copy(near.at[done], out.at[done], sems.at[k]))
        copies[-1].start()
    alpha[0] = c0[0, 0]
    rest[0] = b0[0, 0]
    rest[1] = c11[0, 0]
    rest[2] = b1[0, 0]
    for copy in copies:
        copy.wait()


def shape(*dims, dtype=F32):
    return jax.ShapeDtypeStruct(dims, dtype)


def call(kernel, outs, *args, ins=VMEM, out_specs=VMEM, scratch=(), limit=16):
    if isinstance(outs, tuple) and not isinstance(out_specs, tuple):
        out_specs = tuple([out_specs] * len(outs))
    return pl.pallas_call(
        kernel,
        out_shape=outs,
        in_specs=[ins] * len(args),
        out_specs=out_specs,
        scratch_shapes=scratch,
        compiler_params=pltpu.CompilerParams(vmem_limit_bytes=limit * 1024 * 1024),
    )(*args)


def exchange(x, axis, count):
    sent = x.reshape(count, -1, TILE)
    got = lax.all_to_all(sent, axis, split_axis=0, concat_axis=0, tiled=True)
    return got.reshape(x.shape)


def per_device(start_vector, tile_blocks, row_owner, row_block, col_owner, col_block, tile_counts):
    tiles = tile_blocks[0, 0]
    count = tiles.shape[0]
    vector = start_vector.reshape(-1, TILE)
    pieces = vector.shape[0]
    n_row, n_col = lax.axis_size("row"), lax.axis_size("col")
    wide_r, wide_c = n_row * LANE, n_col * LANE
    every = wide_r + wide_c
    total = float(pieces * TILE * n_row * n_col)

    def over_row(x):
        return exchange(x, "row", n_row)

    def over_col(x):
        return exchange(x, "col", n_col)

    n_y = n_row // 2
    n_x = n_col // n_y
    n_z = n_col // n_x
    small = [row_owner, row_block, col_owner, col_block, tile_counts]
    small += [lax.axis_index("row"), lax.axis_index("col"), jnp.zeros((), jnp.int32)]
    slots = jnp.concatenate(
        [jnp.broadcast_to(x.reshape(1, -1), (1, count)).astype(jnp.int32) for x in small], axis=0
    )
    planes = [[2 * y * n_col + c for c in range(n_col)] for y in range(n_y)]
    planes += [[(2 * y + 1) * n_col + x * n_z + z for y in range(n_y) for x in range(n_x)] for z in range(n_z)]

    chips = [[2 * y, 2 * y + 1] for y in range(n_y)]

    def over_chip(x):
        return lax.all_gather(x, "row", axis_index_groups=chips, tiled=True)

    ask = call(
        functools.partial(request_kernel, pieces, (n_x, n_z)),
        shape(wide_c, TILE, dtype=jnp.int32),
        slots,
        over_chip(slots),
    )
    ask = lax.all_to_all(
        ask.reshape(n_col, LANE, TILE),
        ("row", "col"),
        split_axis=0,
        concat_axis=0,
        axis_index_groups=planes,
        tiled=True,
    ).reshape(wide_c, TILE)
    pick_row, put_row, pick_col, put_col, pick_pair, mine, squares = call(
        functools.partial(local_kernel, pieces),
        (
            shape(count, wide_r, dtype=BF16),
            shape(wide_r, count, dtype=BF16),
            shape(count, wide_c, dtype=BF16),
            shape(wide_c, count, dtype=BF16),
            shape(count, 2 * wide_r, dtype=BF16),
            shape(count, TILE, dtype=jnp.int32),
            shape(8, TILE),
        ),
        slots,
        vector,
        tiles,
    )
    asked_row, asked_col, v_row, energy = call(
        functools.partial(served_kernel, n_x),
        (
            shape(wide_r, TILE, dtype=jnp.int32),
            shape(wide_c, TILE, dtype=jnp.int32),
            shape(wide_r, TILE),
            shape(1, TILE),
        ),
        slots,
        over_chip(ask),
        vector,
        squares,
    )
    x_col = over_row(v_row)
    first_col, v_col, meet, link, link_col, owned = call(
        direct_kernel,
        (
            shape(wide_c, TILE),
            shape(wide_c, TILE),
            shape(every, every, dtype=BF16),
            shape(count, n_row * count, dtype=BF16),
            shape(wide_c, n_row * count, dtype=BF16),
            shape(wide_r, n_row * count, dtype=BF16),
        ),
        x_col,
        pick_row,
        tiles,
        put_col,
        asked_row,
        asked_col,
        mine,
        vector,
    )
    first_col = over_col(first_col)
    packed = call(
        mirror_kernel,
        shape(n_row, count + 2 * LANE, TILE, dtype=BF16),
        first_col,
        pick_col,
        tiles,
        put_row,
        meet,
    )
    second_col, first_row = call(
        second_direct_kernel,
        (shape(wide_c, TILE), shape(wide_r, TILE)),
        over_row(packed),
        link,
        link_col,
        owned,
        pick_pair,
        meet,
        first_col,
        tiles,
        put_col,
    )
    second_col = over_col(second_col)
    second_row = over_row(
        call(second_mirror_kernel, shape(wide_r, TILE), second_col, pick_col, tiles, put_row)
    )
    products = (first_row, second_row, first_col, second_col)
    inner = call(inner_kernel, shape(n_row, 8, TILE), meet, energy, v_row, v_col, *products)
    inner = over_row(inner)
    image, second = call(
        spread_kernel, (shape(pieces, TILE), shape(pieces, TILE)), asked_row, asked_col, *products
    )
    inner = over_col(call(partial_kernel, shape(n_col, TILE), inner))

    def finish(*refs):
        final_kernel(total, *refs)

    out, alpha, rest = call(
        finish,
        (shape(2 * pieces, TILE), shape(1), shape(3)),
        inner,
        vector,
        image,
        second,
        out_specs=(HBM, SMEM, SMEM),
        scratch=[pltpu.VMEM((2 * pieces, TILE), F32), pltpu.SemaphoreType.DMA((4,))],
    )
    basis = out.reshape(pieces, 2, TILE).transpose(1, 0, 2).reshape(2, pieces * TILE)
    return (basis, alpha, rest)


def solution(mesh):
    return jax.shard_map(
        per_device,
        mesh=mesh,
        in_specs=(
            P(("row", "col")),
            P("row", "col", None, None, None),
            P("row", "col", None, None),
            P("row", "col", None),
            P("row", "col", None, None),
            P("row", "col", None),
            P("row", "col"),
        ),
        out_specs=(P(None, ("row", "col")), P(), P()),
        check_vma=False,
    )
```

```python
import functools

import jax
import jax.numpy as jnp
from jax import lax
from jax.experimental import pallas as pl
from jax.experimental.pallas import tpu as pltpu
from jax.sharding import PartitionSpec as P

TILE = 128
LANE = 8
LOW = LANE - 1
BITS = 3
HALF = 4
SCALE = 1024.0
F32 = jnp.float32
BF16 = jnp.bfloat16
VMEM = pl.BlockSpec(memory_space=pltpu.VMEM)
SMEM = pl.BlockSpec(memory_space=pltpu.SMEM)
HBM = pl.BlockSpec(memory_space=pltpu.HBM)


def iota(shape, axis):
    return lax.broadcasted_iota(jnp.int32, shape, axis)


def halves(x):
    high = x.astype(BF16)
    low = (x - high.astype(F32)).astype(BF16)
    return high, low


def dot(a, b):
    return jnp.dot(a, b, preferred_element_type=F32)


def exact_dot(select, x):
    high, low = halves(x)
    return dot(select, high) + dot(select, low)


def place_of(owner, column):
    count = owner.shape[1]
    shape = (count, count)
    down, across = iota(shape, 0), iota(shape, 1)
    same = column == owner
    rank_row = jnp.sum(jnp.where(same & (down < across), 1, 0), axis=0, keepdims=True)
    rank_column = jnp.sum(jnp.where(same & (across < down), 1, 0), axis=1, keepdims=True)
    return owner * LANE + rank_row, column * LANE + rank_column


def columns_of(slots):
    twice = jnp.concatenate([slots, slots], axis=1).astype(F32)
    return twice.T[: slots.shape[1], :].astype(jnp.int32)


def request_kernel(pieces, planes, slots, both, ask):
    n_x, n_z = planes
    me = slots[5:6, 0:1]
    x = slots[6:7, 0:1] // n_z
    count = slots.shape[1]
    width = ask.shape[0]
    spot = iota((width, count), 0)
    quarter = iota((TILE, count), 0) >> 4
    col = row = jnp.zeros((width, TILE), F32)
    riders = []

    def spread(there, value):
        there = jnp.where(there, 1.0, 0.0).astype(BF16)
        rest = value & 15
        dims = (((1,), (1,)), ((), ()))
        return sum(
            lax.dot_general(there, part.astype(F32).astype(BF16), dims, preferred_element_type=F32)
            for part in (value - rest, rest)
        )

    columns = columns_of(both[...])
    for core in range(2):
        own_r, blk_r, own_c, blk_c, filled = [both[8 * core + k : 8 * core + k + 1, :] for k in range(5)]
        alive = iota((1, count), 1) < filled
        place = place_of(own_r, columns[:, 8 * core : 8 * core + 1])[0] + HALF * core
        value = jnp.broadcast_to(jnp.where(alive, blk_r + 1, 0), (TILE, count))
        col = col + spread(spot == place, value)
        place = place_of(own_c, columns[:, 8 * core + 2 : 8 * core + 3])[0]
        rank, chip = place & LOW, own_c >> 1
        here = ((quarter >> 1) == core) & ((quarter & 1) == (own_c & 1))
        value = jnp.where(here, jnp.where(alive, blk_c + 1, 0), 0)
        row = row + spread(spot == (chip * n_x + x) * LANE + rank, value)
        riders.append((alive, own_c, blk_c, place))
    lane = iota((width, TILE), 1)
    down = iota((width, TILE), 0)
    values = row.astype(jnp.int32) - 1
    for core, (alive, own_c, blk_c, place) in enumerate(riders):
        ident = jnp.where(alive, own_c * pieces + blk_c, -1)
        for k, rider in ((core, ident), (2 + core, place)):
            twice = jnp.concatenate([rider, rider], axis=1)
            values = jnp.where((lane >= count) & ((down & LOW) == k), twice, values)
    values = jnp.where((down >> BITS) % n_x == x, values, -9)
    ask[...] = jnp.where((me & 1) == 0, col.astype(jnp.int32) - 1, values)


def local_kernel(
    pieces, slots, vector, tiles, pick_row, put_row, pick_col, put_col, pick_pair, mine, energy, turned
):
    own_c = slots[2:3, :]
    count = slots.shape[1]
    columns = columns_of(slots[...])
    for k, pick, put, shift in ((2, pick_row, put_row, 0), (0, pick_col, put_col, HALF)):
        width = put.shape[0]
        across, down = place_of(slots[k : k + 1, :], columns[:, k : k + 1])
        pick[...] = jnp.where(iota((count, width), 1) == down, 1.0, 0.0).astype(BF16)
        put[...] = jnp.where(iota((width, count), 0) == across + shift, 1.0, 0.0).astype(BF16)
    ident = jnp.where(iota((count, 1), 0) < columns[:, 4:5], columns[:, 2:3] * pieces + columns[:, 3:4], -2)
    mine[...] = jnp.broadcast_to(ident, mine.shape)
    place = place_of(own_c, columns[:, 2:3])[1]
    high = place + (place & ~LOW)
    pick_pair[...] = jnp.where(iota(pick_pair.shape, 1) == high, 1.0, 0.0).astype(BF16)
    v = vector[...] * SCALE
    energy[...] = jnp.sum((v * v).reshape(-1, 8, TILE), axis=0)
    for t in range(tiles.shape[0]):
        turned[t] = tiles[t].T


def first_lane(asked):
    return jnp.broadcast_to(asked[:, 0:1], asked.shape)


def gather(asked, vector):
    pieces = vector.shape[0]
    rows = asked.shape[0]
    lanes = iota((rows, TILE), 1)
    select = jnp.concatenate(
        [jnp.where(asked == lanes + k * TILE, 1.0, 0.0).astype(BF16) for k in range(pieces // TILE)], axis=1
    )
    return exact_dot(select, vector)


def served_kernel(n_x, slots, pair, vector, squares, asked_row, asked_col, out, energy):
    me = slots[5:6, 0:1]
    first = (me & 1) == 0
    width = asked_col.shape[0]
    col = pair[:width, :].reshape(-1, LANE, TILE)
    swapped = jnp.concatenate([col[:, HALF:, :], col[:, :HALF, :]], axis=1)
    lower = iota(col.shape, 1) < HALF
    keep = lower == first.reshape(1, 1, 1)
    asked_col[...] = jnp.where(keep, col, swapped).reshape(width, TILE)
    row = jnp.max(pair[width:, :].reshape(-1, n_x, LANE, TILE), axis=1)
    slot = iota(row.shape, 1)
    lane = iota(row.shape, 2)
    asked, full = [], []
    for core in range(2):
        sides = [jnp.broadcast_to(row[:, :, 16 * k : 16 * k + 1], row.shape) for k in (2 * core, 2 * core + 1)]
        value = jnp.where(first.reshape(1, 1, 1), sides[0], sides[1])
        riders = jnp.where((slot & 1) == 0, row[:, core : core + 1, :], row[:, 2 + core : 3 + core, :])
        count = TILE // 2
        mixed = jnp.where(lane >= count, riders, jnp.where(lane == count - 1, me.reshape(1, 1, 1), value))
        asked.append(value)
        full.append(mixed)
    shape = asked_row.shape
    asked_row[...] = jnp.stack(full, axis=1).reshape(shape)
    out[...] = gather(jnp.stack(asked, axis=1).reshape(shape), vector[...] * SCALE)
    energy[...] = jnp.sum(squares[...], axis=0, keepdims=True)


def product_lane(asked_row, asked_col):
    rows = [first_lane(asked_row[...]).astype(F32).T[0:1, :]]
    width = asked_col.shape[0]
    for k in range(width // TILE):
        part = asked_col[k * TILE : (k + 1) * TILE, :].astype(F32).T[0:1, :]
        lane = iota((1, TILE), 1)
        rows.append(jnp.where((lane & LOW) >= HALF, part, -2.0))
    return [row.astype(jnp.int32) for row in rows]


def meet_tables(asked_row, asked_col, mine, pieces, meet, link, link_col, owned):
    lanes = product_lane(asked_row, asked_col)
    base = 0
    served_row, served_col = first_lane(asked_row[...]), asked_col[...]
    for served in (served_row, served_col):
        for k, lane in enumerate(lanes):
            hit = (served == lane) & (served >= 0)
            meet[base : base + served.shape[0], k * TILE : (k + 1) * TILE] = jnp.where(hit, 1.0, 0.0).astype(BF16)
        base += served.shape[0]
    count = mine.shape[0]
    index = asked_row[0:1, count - 1 : count]
    ident = jnp.where(served_col < 0, -3, served_col + index * pieces)
    lane = iota((1, TILE), 1)
    slot = iota(owned.shape[:1] + (TILE,), 0)
    half = jnp.where(iota(owned.shape[:1] + (TILE,), 1) < count, 0, 1)
    for k in range(asked_row.shape[0] // (2 * LANE)):
        start = 2 * k * LANE
        even = [asked_row[start + j : start + j + 1, :] for j in range(2)]
        odd = [asked_row[start + LANE + j : start + LANE + j + 1, :] for j in range(2)]
        ids, spots = [jnp.where(lane < count, pltpu.roll(a, count, 1), b) for a, b in zip(even, odd)]
        cols = slice(k * TILE, (k + 1) * TILE)
        link[:, cols] = jnp.where(mine[...] == ids, 1.0, 0.0).astype(BF16)
        link_col[:, cols] = jnp.where(ident == ids, 1.0, 0.0).astype(BF16)
        sent = (spots == index * LANE + (slot & LOW)) & ((slot >> BITS) == 2 * k + half)
        owned[:, cols] = jnp.where(sent, 1.0, 0.0).astype(BF16)


def multiply(x, tiles):
    count = x.shape[0]
    row = iota((16, TILE), 0) & 7
    groups = []
    for g in range(count // 8):
        part = x[g * 8 : (g + 1) * 8, :]
        high = part.astype(BF16).astype(F32)
        both = jnp.concatenate([high, part - high], axis=0)
        apart = jnp.concatenate([jnp.where(row == j, both, 0.0).astype(BF16) for j in range(8)], axis=1)
        y = dot(apart, tiles[g * 8 : (g + 1) * 8].reshape(8 * TILE, TILE))
        groups.append(y[0:8] + y[8:16])
    return jnp.concatenate(groups, axis=0)


def direct_kernel(
    got, pick, tiles, put, asked_row, asked_col, mine, vector, out, v_col, meet, link, link_col, owned
):
    y = multiply(exact_dot(pick[...], got[...]), tiles)
    v = gather(asked_col[...], vector[...] * SCALE)
    v_col[...] = v
    forward = (iota(v.shape, 0) & LOW) < HALF
    out[...] = exact_dot(put[...], y) + jnp.where(forward, v, 0.0)
    meet_tables(asked_row, asked_col, mine, vector.shape[0], meet, link, link_col, owned)


def mirror_kernel(got, pick, tiles, put, meet, out):
    y = multiply(exact_dot(pick[...], got[...]), tiles)
    high, low = halves(y)
    width = put.shape[0]
    total = exact_dot(meet[:width, width:], got[...])
    low = dot(put[...], low)
    count = y.shape[0]
    for k in range(out.shape[0]):
        rows = slice(k * LANE, (k + 1) * LANE)
        out[k, :count, :] = high
        out[k, count:, :] = jnp.concatenate([total[rows], low[rows]], axis=0).astype(BF16)


def second_direct_kernel(got, link, link_col, owned, pick, meet, first_col, tiles, put, out, first_row):
    count = link.shape[0]
    peers = range(got.shape[0])
    mirrors = jnp.concatenate([got[k, :count, :] for k in peers], axis=0)
    sums = jnp.concatenate([got[k, count:, :] for k in peers], axis=0)
    y = multiply(dot(link[...], mirrors) + dot(pick[...], sums), tiles)
    width = got.shape[0] * LANE
    image = dot(link_col[...], mirrors) + exact_dot(meet[width:, width:], first_col[...])
    forward = (iota(image.shape, 0) & LOW) < HALF
    out[...] = exact_dot(put[...], y) + jnp.where(forward, image, 0.0)
    slot = iota((width, 2 * width), 0)
    low = iota((width, 2 * width), 1) == slot + (slot & ~LOW) + LANE
    first_row[...] = dot(owned[...], mirrors) + dot(jnp.where(low, 1.0, 0.0).astype(BF16), sums)


def second_mirror_kernel(got, pick, tiles, put, out):
    out[...] = exact_dot(put[...], multiply(exact_dot(pick[...], got[...]), tiles))


def inner_kernel(meet, energy, v_row, v_col, first_row, second_row, first_col, second_col, out):
    first_r, second_r = first_row[...], second_row[...]
    first = jnp.concatenate([first_r, first_col[...]], axis=0)
    second = jnp.concatenate([second_r, second_col[...]], axis=0)
    both = exact_dot(meet[...], jnp.concatenate([first, second], axis=1))
    image, total = both[:, :TILE], both[:, TILE:]
    width = v_row.shape[0]
    returned = (iota(v_col.shape, 0) & LOW) >= HALF
    first_c = jnp.where(returned, first_col[...], 0.0)
    second_c = jnp.where(returned, second_col[...], 0.0)

    def inner(a_r, b_r, a_c, b_c):
        return jnp.sum(a_r * b_r, axis=0, keepdims=True) + jnp.sum(a_c * b_c, axis=0, keepdims=True)

    values = [
        energy[...],
        inner(v_row[...], first_r, v_col[...], first_c),
        inner(image[:width], first_r, image[width:], first_c),
        inner(v_row[...], second_r, v_col[...], second_c),
        inner(image[:width], second_r, image[width:], second_c),
        inner(total[:width], second_r, total[width:], second_c),
    ]
    packed = jnp.concatenate(values + [jnp.zeros((2, TILE), F32)], axis=0)
    for k in range(out.shape[0]):
        out[k] = packed


def partial_kernel(got, out):
    total = jnp.sum(got[...], axis=0)
    sums = jnp.sum(total, axis=1, keepdims=True)
    packed = jnp.sum(jnp.where(iota(total.shape, 0) == iota(total.shape, 1), sums, 0.0), axis=0, keepdims=True)
    out[...] = jnp.broadcast_to(packed, out.shape)


def spread_kernel(asked_row, asked_col, first_row, second_row, first_col, second_col, image, second):
    lanes = jnp.concatenate(product_lane(asked_row, asked_col), axis=1)
    rows = jnp.concatenate([first_row[...], second_row[...]], axis=1)
    columns = jnp.concatenate([first_col[...], second_col[...]], axis=1)
    high, low = halves(jnp.concatenate([rows, columns], axis=0))
    step = 256
    for start in range(0, image.shape[0], step):
        place = iota((step, lanes.shape[1]), 0) + start
        select = jnp.where(place == lanes, 1.0, 0.0).astype(BF16)
        both = dot(select, high) + dot(select, low)
        image[start : start + step, :] = both[:, :TILE]
        second[start : start + step, :] = both[:, TILE:]


def final_kernel(total, got, vector, image, second, out, alpha, rest, near, sems):
    sums = jnp.sum(got[...], axis=0, keepdims=True)
    lane = iota((1, TILE), 1)

    def value(k):
        return jnp.sum(jnp.where(lane == k, sums, 0.0), axis=1, keepdims=True)

    vv, vi, ii, vw, iw, ww = [value(k) for k in range(6)]
    share = 1.0 / total
    g = lax.rsqrt(vv * (share / (SCALE * SCALE)) + 1e-06) * (1.0 / SCALE)
    c0 = g * (g * vi * share)
    square = g * (g * (ii - 2.0 * c0 * vi + c0 * c0 * vv) * share)
    square = jnp.maximum(square, 0.0) + 1e-06
    root = lax.rsqrt(square)
    b0 = square * root
    h = g * root
    c10 = h * (g * (vw - c0 * vi) * share)
    c11 = h * (h * (iw - c0 * ii - c0 * vw + c0 * c0 * vi) * share)
    a = c0 + c11
    b = c11 * c0 - c10 * b0
    square = h * (h * (ww + a * a * ii + b * b * vv - 2.0 * a * iw + 2.0 * b * vw - 2.0 * a * b * vi) * share)
    square = jnp.maximum(square, 0.0) + 1e-06
    root = lax.rsqrt(square)
    b1 = square * root
    f = h * root
    parts = sems.shape[0]
    step = vector.shape[0] // parts
    copies = []
    for k in range(parts):
        rows = pl.ds(k * step, step)
        v, i = vector[rows, :], image[rows, :]
        near[pl.ds(2 * k * step, step, 2), :] = h * i - (h * c0 * SCALE) * v
        near[pl.ds(2 * k * step + 1, step, 2), :] = f * second[rows, :] - (f * a) * i + (f * b * SCALE) * v
        done = pl.ds(2 * k * step, 2 * step)
        copies.append(pltpu.make_async_copy(near.at[done], out.at[done], sems.at[k]))
        copies[-1].start()
    alpha[0] = c0[0, 0]
    rest[0] = b0[0, 0]
    rest[1] = c11[0, 0]
    rest[2] = b1[0, 0]
    for copy in copies:
        copy.wait()


def shape(*dims, dtype=F32):
    return jax.ShapeDtypeStruct(dims, dtype)


def call(kernel, outs, *args, ins=VMEM, out_specs=VMEM, scratch=(), limit=16):
    if isinstance(outs, tuple) and not isinstance(out_specs, tuple):
        out_specs = tuple([out_specs] * len(outs))
    return pl.pallas_call(
        kernel,
        out_shape=outs,
        in_specs=[ins] * len(args),
        out_specs=out_specs,
        scratch_shapes=scratch,
        compiler_params=pltpu.CompilerParams(vmem_limit_bytes=limit * 1024 * 1024),
    )(*args)


def exchange(x, axis, count):
    sent = x.reshape(count, -1, TILE)
    got = lax.all_to_all(sent, axis, split_axis=0, concat_axis=0, tiled=True)
    return got.reshape(x.shape)


def per_device(start_vector, tile_blocks, row_owner, row_block, col_owner, col_block, tile_counts):
    tiles = tile_blocks[0, 0]
    count = tiles.shape[0]
    vector = start_vector.reshape(-1, TILE)
    pieces = vector.shape[0]
    n_row, n_col = lax.axis_size("row"), lax.axis_size("col")
    wide_r, wide_c = n_row * LANE, n_col * LANE
    every = wide_r + wide_c
    total = float(pieces * TILE * n_row * n_col)

    def over_row(x):
        return exchange(x, "row", n_row)

    def over_col(x):
        return exchange(x, "col", n_col)

    n_y = n_row // 2
    n_x = n_col // n_y
    n_z = n_col // n_x
    small = [row_owner, row_block, col_owner, col_block, tile_counts]
    small += [lax.axis_index("row"), lax.axis_index("col"), jnp.zeros((), jnp.int32)]
    slots = jnp.concatenate(
        [jnp.broadcast_to(x.reshape(1, -1), (1, count)).astype(jnp.int32) for x in small], axis=0
    )
    planes = [[2 * y * n_col + c for c in range(n_col)] for y in range(n_y)]
    planes += [[(2 * y + 1) * n_col + x * n_z + z for y in range(n_y) for x in range(n_x)] for z in range(n_z)]

    chips = [[2 * y, 2 * y + 1] for y in range(n_y)]

    def over_chip(x):
        return lax.all_gather(x, "row", axis_index_groups=chips, tiled=True)

    ask = call(
        functools.partial(request_kernel, pieces, (n_x, n_z)),
        shape(wide_c, TILE, dtype=jnp.int32),
        slots,
        over_chip(slots),
    )
    ask = lax.all_to_all(
        ask.reshape(n_col, LANE, TILE),
        ("row", "col"),
        split_axis=0,
        concat_axis=0,
        axis_index_groups=planes,
        tiled=True,
    ).reshape(wide_c, TILE)
    pick_row, put_row, pick_col, put_col, pick_pair, mine, squares, turned = call(
        functools.partial(local_kernel, pieces),
        (
            shape(count, wide_r, dtype=BF16),
            shape(wide_r, count, dtype=BF16),
            shape(count, wide_c, dtype=BF16),
            shape(wide_c, count, dtype=BF16),
            shape(count, 2 * wide_r, dtype=BF16),
            shape(count, TILE, dtype=jnp.int32),
            shape(8, TILE),
            shape(*tiles.shape, dtype=BF16),
        ),
        slots,
        vector,
        tiles,
    )
    asked_row, asked_col, v_row, energy = call(
        functools.partial(served_kernel, n_x),
        (
            shape(wide_r, TILE, dtype=jnp.int32),
            shape(wide_c, TILE, dtype=jnp.int32),
            shape(wide_r, TILE),
            shape(1, TILE),
        ),
        slots,
        over_chip(ask),
        vector,
        squares,
    )
    x_col = over_row(v_row)
    first_col, v_col, meet, link, link_col, owned = call(
        direct_kernel,
        (
            shape(wide_c, TILE),
            shape(wide_c, TILE),
            shape(every, every, dtype=BF16),
            shape(count, n_row * count, dtype=BF16),
            shape(wide_c, n_row * count, dtype=BF16),
            shape(wide_r, n_row * count, dtype=BF16),
        ),
        x_col,
        pick_row,
        turned,
        put_col,
        asked_row,
        asked_col,
        mine,
        vector,
    )
    first_col = over_col(first_col)
    packed = call(
        mirror_kernel,
        shape(n_row, count + 2 * LANE, TILE, dtype=BF16),
        first_col,
        pick_col,
        tiles,
        put_row,
        meet,
    )
    second_col, first_row = call(
        second_direct_kernel,
        (shape(wide_c, TILE), shape(wide_r, TILE)),
        over_row(packed),
        link,
        link_col,
        owned,
        pick_pair,
        meet,
        first_col,
        turned,
        put_col,
    )
    second_col = over_col(second_col)
    second_row = over_row(
        call(second_mirror_kernel, shape(wide_r, TILE), second_col, pick_col, tiles, put_row)
    )
    products = (first_row, second_row, first_col, second_col)
    inner = call(inner_kernel, shape(n_row, 8, TILE), meet, energy, v_row, v_col, *products)
    inner = over_row(inner)
    image, second = call(
        spread_kernel, (shape(pieces, TILE), shape(pieces, TILE)), asked_row, asked_col, *products
    )
    inner = over_col(call(partial_kernel, shape(n_col, TILE), inner))

    def finish(*refs):
        final_kernel(total, *refs)

    out, alpha, rest = call(
        finish,
        (shape(2 * pieces, TILE), shape(1), shape(3)),
        inner,
        vector,
        image,
        second,
        out_specs=(HBM, SMEM, SMEM),
        scratch=[pltpu.VMEM((2 * pieces, TILE), F32), pltpu.SemaphoreType.DMA((8,))],
    )
    basis = out.reshape(pieces, 2, TILE).transpose(1, 0, 2).reshape(2, pieces * TILE)
    return (basis, alpha, rest)


def solution(mesh):
    return jax.shard_map(
        per_device,
        mesh=mesh,
        in_specs=(
            P(("row", "col")),
            P("row", "col", None, None, None),
            P("row", "col", None, None),
            P("row", "col", None),
            P("row", "col", None, None),
            P("row", "col", None),
            P("row", "col"),
        ),
        out_specs=(P(None, ("row", "col")), P(), P()),
        check_vma=False,
    )
```

```python
import functools

import jax
import jax.numpy as jnp
from jax import lax
from jax.experimental import pallas as pl
from jax.experimental.pallas import tpu as pltpu
from jax.sharding import PartitionSpec as P

TILE = 128
LANE = 8
LOW = LANE - 1
BITS = 3
HALF = 4
SCALE = 1024.0
F32 = jnp.float32
BF16 = jnp.bfloat16
VMEM = pl.BlockSpec(memory_space=pltpu.VMEM)
SMEM = pl.BlockSpec(memory_space=pltpu.SMEM)
HBM = pl.BlockSpec(memory_space=pltpu.HBM)


def iota(shape, axis):
    return lax.broadcasted_iota(jnp.int32, shape, axis)


def halves(x):
    high = x.astype(BF16)
    low = (x - high.astype(F32)).astype(BF16)
    return high, low


def dot(a, b):
    return jnp.dot(a, b, preferred_element_type=F32)


def exact_dot(select, x):
    high, low = halves(x)
    return dot(select, high) + dot(select, low)


def place_of(owner, column):
    count = owner.shape[1]
    shape = (count, count)
    down, across = iota(shape, 0), iota(shape, 1)
    same = column == owner
    rank_row = jnp.sum(jnp.where(same & (down < across), 1, 0), axis=0, keepdims=True)
    rank_column = jnp.sum(jnp.where(same & (across < down), 1, 0), axis=1, keepdims=True)
    return owner * LANE + rank_row, column * LANE + rank_column


def columns_of(rows):
    rows = rows + [jnp.zeros_like(rows[0])] * (8 - len(rows))
    return jnp.concatenate(rows, axis=0).astype(F32).T.astype(jnp.int32)


def request_kernel(pieces, planes, both, me, col, ask):
    n_x, n_z = planes
    first = (jnp.full((1, 1), me[0], jnp.int32) & 1) == 0
    x = col[0] // n_z
    count = both.shape[1]
    width = ask.shape[0]
    lane = iota((1, TILE), 1)
    core = jnp.where(lane < count, 0, 1)

    owner_r, block_r, owner_c, block_c, filled = [
        jnp.concatenate([both[k : k + 1, :], both[8 + k : 9 + k, :]], axis=1) for k in range(5)
    ]
    alive = lane - core * count < filled
    tags = [owner_r + core * count, owner_c + core * count]
    columns = columns_of(tags)
    earlier = iota((TILE, TILE), 0) < iota((TILE, TILE), 1)
    rank_r, rank_c = [
        jnp.sum(jnp.where((columns[:, k : k + 1] == tag) & earlier, 1, 0), axis=0, keepdims=True)
        for k, tag in enumerate(tags)
    ]
    place = owner_c * LANE + rank_c
    spot = jnp.where(
        first, owner_r * LANE + rank_r + core * HALF, ((owner_c >> 1) * n_x + x) * LANE + rank_c
    )
    quarter = iota((TILE, TILE), 0) >> 4
    here = ((quarter >> 1) == core) & ((quarter & 1) == (owner_c & 1)) & alive
    value = jnp.where(first, jnp.where(alive, block_r + 1, 0), jnp.where(here, block_c + 1, 0))
    there = jnp.where(iota((width, TILE), 0) == spot, 1.0, 0.0).astype(BF16)
    rest = value & 15
    dims = (((1,), (1,)), ((), ()))
    total = sum(
        lax.dot_general(there, part.astype(F32).astype(BF16), dims, preferred_element_type=F32)
        for part in (value - rest, rest)
    )
    total = total.astype(jnp.int32) - 1
    ident = jnp.where(alive, owner_c * pieces + block_c, -1)
    down = iota((width, TILE), 0)
    slot = down & LOW
    ids = jnp.where(slot == 0, pltpu.roll(ident, count, 1), ident)
    places = jnp.where(slot == 2, pltpu.roll(place, count, 1), place)
    riders = jnp.where(slot < 2, ids, places)
    full = jnp.where((lane >= count) & (slot < 4), riders, total)
    full = jnp.where((down >> BITS) % n_x == x, full, -9)
    ask[...] = jnp.where(first, total, full)


def local_kernel(
    pieces, both, me, vector, tiles,
    pick_row, put_row, pick_col, put_col, pick_pair, mine, energy, turned,
):
    first = (jnp.full((1, 1), me[0], jnp.int32) & 1) == 0
    count = both.shape[1]
    slots = [jnp.where(first, both[k : k + 1, :], both[8 + k : 9 + k, :]) for k in (0, 2, 3)]
    live = jnp.where(first, both[4:5, 0:1], both[12:13, 0:1])
    columns = columns_of([jnp.concatenate([row, row], axis=1) for row in slots])[:count, :]
    for k, pick, put, shift in ((1, pick_row, put_row, 0), (0, pick_col, put_col, HALF)):
        width = put.shape[0]
        across, down = place_of(slots[k], columns[:, k : k + 1])
        pick[...] = jnp.where(iota((count, width), 1) == down, 1.0, 0.0).astype(BF16)
        put[...] = jnp.where(iota((width, count), 0) == across + shift, 1.0, 0.0).astype(BF16)
    ident = jnp.where(iota((count, 1), 0) < live, columns[:, 1:2] * pieces + columns[:, 2:3], -2)
    mine[...] = jnp.broadcast_to(ident, mine.shape)
    place = place_of(slots[1], columns[:, 1:2])[1]
    high = place + (place & ~LOW)
    pick_pair[...] = jnp.where(iota(pick_pair.shape, 1) == high, 1.0, 0.0).astype(BF16)
    v = vector[...] * SCALE
    energy[...] = jnp.sum((v * v).reshape(-1, 8, TILE), axis=0)
    for t in range(tiles.shape[0]):
        turned[t] = tiles[t].T


def first_lane(asked):
    return jnp.broadcast_to(asked[:, 0:1], asked.shape)


def gather(asked, vector):
    pieces = vector.shape[0]
    rows = asked.shape[0]
    lanes = iota((rows, TILE), 1)
    select = jnp.concatenate(
        [jnp.where(asked == lanes + k * TILE, 1.0, 0.0).astype(BF16) for k in range(pieces // TILE)], axis=1
    )
    return exact_dot(select, vector)


def served_kernel(n_x, index, pair, vector, squares, asked_row, asked_col, out, energy):
    me = jnp.full((1, 1), index[0], jnp.int32)
    first = (me & 1) == 0
    width = asked_col.shape[0]
    col = pair[:width, :].reshape(-1, LANE, TILE)
    swapped = jnp.concatenate([col[:, HALF:, :], col[:, :HALF, :]], axis=1)
    lower = iota(col.shape, 1) < HALF
    keep = lower == first.reshape(1, 1, 1)
    asked_col[...] = jnp.where(keep, col, swapped).reshape(width, TILE)
    row = jnp.max(pair[width:, :].reshape(-1, n_x, LANE, TILE), axis=1)
    slot = iota(row.shape, 1)
    lane = iota(row.shape, 2)
    asked, full = [], []
    for core in range(2):
        sides = [jnp.broadcast_to(row[:, :, 16 * k : 16 * k + 1], row.shape) for k in (2 * core, 2 * core + 1)]
        value = jnp.where(first.reshape(1, 1, 1), sides[0], sides[1])
        riders = jnp.where((slot & 1) == 0, row[:, core : core + 1, :], row[:, 2 + core : 3 + core, :])
        count = TILE // 2
        mixed = jnp.where(lane >= count, riders, jnp.where(lane == count - 1, me.reshape(1, 1, 1), value))
        asked.append(value)
        full.append(mixed)
    shape = asked_row.shape
    asked_row[...] = jnp.stack(full, axis=1).reshape(shape)
    out[...] = gather(jnp.stack(asked, axis=1).reshape(shape), vector[...] * SCALE)
    energy[...] = jnp.sum(squares[...], axis=0, keepdims=True)


def product_lane(asked_row, asked_col):
    rows = [first_lane(asked_row[...]).astype(F32).T[0:1, :]]
    width = asked_col.shape[0]
    for k in range(width // TILE):
        part = asked_col[k * TILE : (k + 1) * TILE, :].astype(F32).T[0:1, :]
        lane = iota((1, TILE), 1)
        rows.append(jnp.where((lane & LOW) >= HALF, part, -2.0))
    return [row.astype(jnp.int32) for row in rows]


def meet_tables(asked_row, asked_col, mine, pieces, meet, link, link_col, owned):
    lanes = product_lane(asked_row, asked_col)
    base = 0
    served_row, served_col = first_lane(asked_row[...]), asked_col[...]
    for served in (served_row, served_col):
        for k, lane in enumerate(lanes):
            hit = (served == lane) & (served >= 0)
            meet[base : base + served.shape[0], k * TILE : (k + 1) * TILE] = jnp.where(hit, 1.0, 0.0).astype(BF16)
        base += served.shape[0]
    count = mine.shape[0]
    index = asked_row[0:1, count - 1 : count]
    ident = jnp.where(served_col < 0, -3, served_col + index * pieces)
    lane = iota((1, TILE), 1)
    slot = iota(owned.shape[:1] + (TILE,), 0)
    half = jnp.where(iota(owned.shape[:1] + (TILE,), 1) < count, 0, 1)
    for k in range(asked_row.shape[0] // (2 * LANE)):
        start = 2 * k * LANE
        even = [asked_row[start + j : start + j + 1, :] for j in range(2)]
        odd = [asked_row[start + LANE + j : start + LANE + j + 1, :] for j in range(2)]
        ids, spots = [jnp.where(lane < count, pltpu.roll(a, count, 1), b) for a, b in zip(even, odd)]
        cols = slice(k * TILE, (k + 1) * TILE)
        link[:, cols] = jnp.where(mine[...] == ids, 1.0, 0.0).astype(BF16)
        link_col[:, cols] = jnp.where(ident == ids, 1.0, 0.0).astype(BF16)
        sent = (spots == index * LANE + (slot & LOW)) & ((slot >> BITS) == 2 * k + half)
        owned[:, cols] = jnp.where(sent, 1.0, 0.0).astype(BF16)


def multiply(x, tiles):
    count = x.shape[0]
    row = iota((16, TILE), 0) & 7
    groups = []
    for g in range(count // 8):
        part = x[g * 8 : (g + 1) * 8, :]
        high = part.astype(BF16).astype(F32)
        both = jnp.concatenate([high, part - high], axis=0)
        apart = jnp.concatenate([jnp.where(row == j, both, 0.0).astype(BF16) for j in range(8)], axis=1)
        y = dot(apart, tiles[g * 8 : (g + 1) * 8].reshape(8 * TILE, TILE))
        groups.append(y[0:8] + y[8:16])
    return jnp.concatenate(groups, axis=0)


def direct_kernel(
    got, pick, tiles, put, asked_row, asked_col, mine, vector, out, v_col, meet, link, link_col, owned
):
    y = multiply(exact_dot(pick[...], got[...]), tiles)
    v = gather(asked_col[...], vector[...] * SCALE)
    v_col[...] = v
    forward = (iota(v.shape, 0) & LOW) < HALF
    out[...] = exact_dot(put[...], y) + jnp.where(forward, v, 0.0)
    meet_tables(asked_row, asked_col, mine, vector.shape[0], meet, link, link_col, owned)


def mirror_kernel(got, pick, tiles, put, meet, out):
    y = multiply(exact_dot(pick[...], got[...]), tiles)
    high, low = halves(y)
    width = put.shape[0]
    total = exact_dot(meet[:width, width:], got[...])
    low = dot(put[...], low)
    count = y.shape[0]
    for k in range(out.shape[0]):
        rows = slice(k * LANE, (k + 1) * LANE)
        out[k, :count, :] = high
        out[k, count:, :] = jnp.concatenate([total[rows], low[rows]], axis=0).astype(BF16)


def second_direct_kernel(got, link, link_col, owned, pick, meet, first_col, tiles, put, out, first_row):
    count = link.shape[0]
    peers = range(got.shape[0])
    mirrors = jnp.concatenate([got[k, :count, :] for k in peers], axis=0)
    sums = jnp.concatenate([got[k, count:, :] for k in peers], axis=0)
    y = multiply(dot(link[...], mirrors) + dot(pick[...], sums), tiles)
    width = got.shape[0] * LANE
    image = dot(link_col[...], mirrors) + exact_dot(meet[width:, width:], first_col[...])
    forward = (iota(image.shape, 0) & LOW) < HALF
    out[...] = exact_dot(put[...], y) + jnp.where(forward, image, 0.0)
    slot = iota((width, 2 * width), 0)
    low = iota((width, 2 * width), 1) == slot + (slot & ~LOW) + LANE
    first_row[...] = dot(owned[...], mirrors) + dot(jnp.where(low, 1.0, 0.0).astype(BF16), sums)


def second_mirror_kernel(got, pick, tiles, put, out):
    out[...] = exact_dot(put[...], multiply(exact_dot(pick[...], got[...]), tiles))


def inner_kernel(meet, energy, v_row, v_col, first_row, second_row, first_col, second_col, out):
    first_r, second_r = first_row[...], second_row[...]
    first = jnp.concatenate([first_r, first_col[...]], axis=0)
    second = jnp.concatenate([second_r, second_col[...]], axis=0)
    both = exact_dot(meet[...], jnp.concatenate([first, second], axis=1))
    image, total = both[:, :TILE], both[:, TILE:]
    width = v_row.shape[0]
    returned = (iota(v_col.shape, 0) & LOW) >= HALF
    first_c = jnp.where(returned, first_col[...], 0.0)
    second_c = jnp.where(returned, second_col[...], 0.0)

    def inner(a_r, b_r, a_c, b_c):
        return jnp.sum(a_r * b_r, axis=0, keepdims=True) + jnp.sum(a_c * b_c, axis=0, keepdims=True)

    values = [
        energy[...],
        inner(v_row[...], first_r, v_col[...], first_c),
        inner(image[:width], first_r, image[width:], first_c),
        inner(v_row[...], second_r, v_col[...], second_c),
        inner(image[:width], second_r, image[width:], second_c),
        inner(total[:width], second_r, total[width:], second_c),
    ]
    packed = jnp.concatenate(values + [jnp.zeros((2, TILE), F32)], axis=0)
    for k in range(out.shape[0]):
        out[k] = packed


def partial_kernel(got, out):
    total = jnp.sum(got[...], axis=0)
    sums = jnp.sum(total, axis=1, keepdims=True)
    packed = jnp.sum(jnp.where(iota(total.shape, 0) == iota(total.shape, 1), sums, 0.0), axis=0, keepdims=True)
    out[...] = jnp.broadcast_to(packed, out.shape)


def returned_rows(x):
    pairs = x.reshape(-1, 2, LANE, TILE)
    return jnp.concatenate([pairs[:, 0, HALF:, :], pairs[:, 1, HALF:, :]], axis=1).reshape(-1, TILE)


def final_kernel(
    total, got, vector, asked_row, asked_col, first_row, second_row, first_col, second_col,
    out, alpha, rest, near, sems,
):
    sums = jnp.sum(got[...], axis=0, keepdims=True)
    lane = iota((1, TILE), 1)

    def value(k):
        return jnp.sum(jnp.where(lane == k, sums, 0.0), axis=1, keepdims=True)

    vv, vi, ii, vw, iw, ww = [value(k) for k in range(6)]
    share = 1.0 / total
    g = lax.rsqrt(vv * (share / (SCALE * SCALE)) + 1e-06) * (1.0 / SCALE)
    c0 = g * (g * vi * share)
    square = g * (g * (ii - 2.0 * c0 * vi + c0 * c0 * vv) * share)
    square = jnp.maximum(square, 0.0) + 1e-06
    root = lax.rsqrt(square)
    b0 = square * root
    h = g * root
    c10 = h * (g * (vw - c0 * vi) * share)
    c11 = h * (h * (iw - c0 * ii - c0 * vw + c0 * c0 * vi) * share)
    a = c0 + c11
    b = c11 * c0 - c10 * b0
    square = h * (h * (ww + a * a * ii + b * b * vv - 2.0 * a * iw + 2.0 * b * vw - 2.0 * a * b * vi) * share)
    square = jnp.maximum(square, 0.0) + 1e-06
    root = lax.rsqrt(square)
    b1 = square * root
    f = h * root
    parts = sems.shape[0]
    step = vector.shape[0] // parts
    asked = [first_lane(asked_row[...]), returned_rows(asked_col[...])]
    lanes = jnp.concatenate([x.astype(F32).T[0:1, :].astype(jnp.int32) for x in asked], axis=1)
    image = jnp.concatenate([first_row[...], returned_rows(first_col[...])], axis=0)
    second = jnp.concatenate([second_row[...], returned_rows(second_col[...])], axis=0)
    high, low = halves(jnp.concatenate([image, second], axis=1))
    copies = []
    for k in range(parts):
        v = vector[pl.ds(k * step, step), :]
        place = iota((step, lanes.shape[1]), 0) + k * step
        select = jnp.where(place == lanes, 1.0, 0.0).astype(BF16)
        both = dot(select, high) + dot(select, low)
        i, w = both[:, :TILE], both[:, TILE:]
        near[pl.ds(2 * k * step, step, 2), :] = h * i - (h * c0 * SCALE) * v
        near[pl.ds(2 * k * step + 1, step, 2), :] = f * w - (f * a) * i + (f * b * SCALE) * v
        done = pl.ds(2 * k * step, 2 * step)
        copies.append(pltpu.make_async_copy(near.at[done], out.at[done], sems.at[k]))
        copies[-1].start()
    alpha[0] = c0[0, 0]
    rest[0] = b0[0, 0]
    rest[1] = c11[0, 0]
    rest[2] = b1[0, 0]
    for copy in copies:
        copy.wait()


def shape(*dims, dtype=F32):
    return jax.ShapeDtypeStruct(dims, dtype)


def call(kernel, outs, *args, ins=VMEM, out_specs=VMEM, scratch=(), limit=16):
    if isinstance(outs, tuple) and not isinstance(out_specs, tuple):
        out_specs = tuple([out_specs] * len(outs))
    return pl.pallas_call(
        kernel,
        out_shape=outs,
        in_specs=ins if isinstance(ins, list) else [ins] * len(args),
        out_specs=out_specs,
        scratch_shapes=scratch,
        compiler_params=pltpu.CompilerParams(vmem_limit_bytes=limit * 1024 * 1024),
    )(*args)


def exchange(x, axis, count):
    sent = x.reshape(count, -1, TILE)
    got = lax.all_to_all(sent, axis, split_axis=0, concat_axis=0, tiled=True)
    return got.reshape(x.shape)


def per_device(start_vector, tile_blocks, row_owner, row_block, col_owner, col_block, tile_counts):
    tiles = tile_blocks[0, 0]
    count = tiles.shape[0]
    vector = start_vector.reshape(-1, TILE)
    pieces = vector.shape[0]
    n_row, n_col = lax.axis_size("row"), lax.axis_size("col")
    wide_r, wide_c = n_row * LANE, n_col * LANE
    every = wide_r + wide_c
    total = float(pieces * TILE * n_row * n_col)

    def over_row(x):
        return exchange(x, "row", n_row)

    def over_col(x):
        return exchange(x, "col", n_col)

    n_y = n_row // 2
    n_x = n_col // n_y
    n_z = n_col // n_x
    planes = [[2 * y * n_col + c for c in range(n_col)] for y in range(n_y)]
    planes += [[(2 * y + 1) * n_col + x * n_z + z for y in range(n_y) for x in range(n_x)] for z in range(n_z)]
    chips = [[2 * y, 2 * y + 1] for y in range(n_y)]

    def over_chip(x):
        return lax.all_gather(x, "row", axis_index_groups=chips, tiled=True)

    slots = [row_owner, row_block, col_owner, col_block, tile_counts] + [jnp.zeros((), jnp.int32)] * 3
    slots = jnp.concatenate([jnp.broadcast_to(x.reshape(1, -1), (1, count)) for x in slots], axis=0)
    both = over_chip(slots)
    me, col = lax.axis_index("row").reshape(1), lax.axis_index("col").reshape(1)
    ask = call(
        functools.partial(request_kernel, pieces, (n_x, n_z)),
        shape(wide_c, TILE, dtype=jnp.int32),
        both,
        me,
        col,
        ins=[VMEM] + [SMEM] * 2,
    )
    ask = lax.all_to_all(
        ask.reshape(n_col, LANE, TILE),
        ("row", "col"),
        split_axis=0,
        concat_axis=0,
        axis_index_groups=planes,
        tiled=True,
    ).reshape(wide_c, TILE)
    pick_row, put_row, pick_col, put_col, pick_pair, mine, squares, turned = call(
        functools.partial(local_kernel, pieces),
        (
            shape(count, wide_r, dtype=BF16),
            shape(wide_r, count, dtype=BF16),
            shape(count, wide_c, dtype=BF16),
            shape(wide_c, count, dtype=BF16),
            shape(count, 2 * wide_r, dtype=BF16),
            shape(count, TILE, dtype=jnp.int32),
            shape(8, TILE),
            shape(*tiles.shape, dtype=BF16),
        ),
        both,
        me,
        vector,
        tiles,
        ins=[VMEM, SMEM] + [VMEM] * 2,
    )
    asked_row, asked_col, v_row, energy = call(
        functools.partial(served_kernel, n_x),
        (
            shape(wide_r, TILE, dtype=jnp.int32),
            shape(wide_c, TILE, dtype=jnp.int32),
            shape(wide_r, TILE),
            shape(1, TILE),
        ),
        me,
        over_chip(ask),
        vector,
        squares,
        ins=[SMEM] + [VMEM] * 3,
    )
    x_col = over_row(v_row)
    first_col, v_col, meet, link, link_col, owned = call(
        direct_kernel,
        (
            shape(wide_c, TILE),
            shape(wide_c, TILE),
            shape(every, every, dtype=BF16),
            shape(count, n_row * count, dtype=BF16),
            shape(wide_c, n_row * count, dtype=BF16),
            shape(wide_r, n_row * count, dtype=BF16),
        ),
        x_col,
        pick_row,
        turned,
        put_col,
        asked_row,
        asked_col,
        mine,
        vector,
    )
    first_col = over_col(first_col)
    packed = call(
        mirror_kernel,
        shape(n_row, count + 2 * LANE, TILE, dtype=BF16),
        first_col,
        pick_col,
        tiles,
        put_row,
        meet,
    )
    second_col, first_row = call(
        second_direct_kernel,
        (shape(wide_c, TILE), shape(wide_r, TILE)),
        over_row(packed),
        link,
        link_col,
        owned,
        pick_pair,
        meet,
        first_col,
        turned,
        put_col,
    )
    second_col = over_col(second_col)
    second_row = over_row(
        call(second_mirror_kernel, shape(wide_r, TILE), second_col, pick_col, tiles, put_row)
    )
    products = (first_row, second_row, first_col, second_col)
    inner = call(inner_kernel, shape(n_row, 8, TILE), meet, energy, v_row, v_col, *products)
    inner = over_row(inner)
    inner = over_col(call(partial_kernel, shape(n_col, TILE), inner))

    def finish(*refs):
        final_kernel(total, *refs)

    out, alpha, rest = call(
        finish,
        (shape(2 * pieces, TILE), shape(1), shape(3)),
        inner,
        vector,
        asked_row,
        asked_col,
        *products,
        out_specs=(HBM, SMEM, SMEM),
        scratch=[pltpu.VMEM((2 * pieces, TILE), F32), pltpu.SemaphoreType.DMA((8,))],
    )
    basis = out.reshape(pieces, 2, TILE).transpose(1, 0, 2).reshape(2, pieces * TILE)
    return (basis, alpha, rest)


def solution(mesh):
    return jax.shard_map(
        per_device,
        mesh=mesh,
        in_specs=(
            P(("row", "col")),
            P("row", "col", None, None, None),
            P("row", "col", None, None),
            P("row", "col", None),
            P("row", "col", None, None),
            P("row", "col", None),
            P("row", "col"),
        ),
        out_specs=(P(None, ("row", "col")), P(), P()),
        check_vma=False,
    )
```

```python
import functools

import jax
import jax.numpy as jnp
from jax import lax
from jax.experimental import pallas as pl
from jax.experimental.pallas import tpu as pltpu
from jax.sharding import PartitionSpec as P

TILE = 128
LANE = 8
LOW = LANE - 1
BITS = 3
HALF = 4
SCALE = 1024.0
F32 = jnp.float32
BF16 = jnp.bfloat16
VMEM = pl.BlockSpec(memory_space=pltpu.VMEM)
SMEM = pl.BlockSpec(memory_space=pltpu.SMEM)
HBM = pl.BlockSpec(memory_space=pltpu.HBM)


def iota(shape, axis):
    return lax.broadcasted_iota(jnp.int32, shape, axis)


def halves(x):
    high = x.astype(BF16)
    low = (x - high.astype(F32)).astype(BF16)
    return high, low


def dot(a, b):
    return jnp.dot(a, b, preferred_element_type=F32)


def exact_dot(select, x):
    high, low = halves(x)
    return dot(select, high) + dot(select, low)


def place_of(owner, column):
    count = owner.shape[1]
    shape = (count, count)
    down, across = iota(shape, 0), iota(shape, 1)
    same = column == owner
    rank_row = jnp.sum(jnp.where(same & (down < across), 1, 0), axis=0, keepdims=True)
    rank_column = jnp.sum(jnp.where(same & (across < down), 1, 0), axis=1, keepdims=True)
    return owner * LANE + rank_row, column * LANE + rank_column


def columns_of(rows):
    rows = rows + [jnp.zeros_like(rows[0])] * (8 - len(rows))
    return jnp.concatenate(rows, axis=0).astype(F32).T.astype(jnp.int32)


def request_kernel(bits, planes, both, me, col, ask):
    n_x, n_z = planes
    first = (jnp.full((1, 1), me[0], jnp.int32) & 1) == 0
    x = col[0] // n_z
    count = both.shape[1]
    width = ask.shape[0]
    lane = iota((1, TILE), 1)
    core = jnp.where(lane < count, 0, 1)

    owner_r, block_r, owner_c, block_c, filled = [
        jnp.concatenate([both[k : k + 1, :], both[8 + k : 9 + k, :]], axis=1) for k in range(5)
    ]
    alive = lane - core * count < filled
    tags = [owner_r + core * count, owner_c + core * count]
    columns = columns_of(tags)
    earlier = iota((TILE, TILE), 0) < iota((TILE, TILE), 1)
    rank_r, rank_c = [
        jnp.sum(jnp.where((columns[:, k : k + 1] == tag) & earlier, 1, 0), axis=0, keepdims=True)
        for k, tag in enumerate(tags)
    ]
    packed = jnp.where(alive, (((owner_c << bits) + block_c) << BITS) + rank_c, -1)
    down = iota((width, TILE), 0)
    packed = jnp.where(down % n_x == x, packed, -9)
    slot = rank_r + core * HALF
    value = jnp.where((iota((TILE, TILE), 0) >> 4) == slot, jnp.where(alive, block_r + 1, 0), 0)
    there = jnp.where(down == owner_r, 1.0, 0.0).astype(BF16)
    rest = value & 15
    dims = (((1,), (1,)), ((), ()))
    total = sum(
        lax.dot_general(there, part.astype(F32).astype(BF16), dims, preferred_element_type=F32)
        for part in (value - rest, rest)
    )
    ask[...] = jnp.where(first, total.astype(jnp.int32) - 1, packed)


def local_kernel(
    bits, both, me, vector, tiles,
    pick_row, put_row, pick_col, put_col, pick_pair, mine, energy, turned,
):
    first = (jnp.full((1, 1), me[0], jnp.int32) & 1) == 0
    count = both.shape[1]
    slots = [jnp.where(first, both[k : k + 1, :], both[8 + k : 9 + k, :]) for k in (0, 2, 3)]
    live = jnp.where(first, both[4:5, 0:1], both[12:13, 0:1])
    columns = columns_of([jnp.concatenate([row, row], axis=1) for row in slots])[:count, :]
    for k, pick, put, shift in ((1, pick_row, put_row, 0), (0, pick_col, put_col, HALF)):
        width = put.shape[0]
        across, down = place_of(slots[k], columns[:, k : k + 1])
        pick[...] = jnp.where(iota((count, width), 1) == down, 1.0, 0.0).astype(BF16)
        put[...] = jnp.where(iota((width, count), 0) == across + shift, 1.0, 0.0).astype(BF16)
    ident = jnp.where(iota((count, 1), 0) < live, (columns[:, 1:2] << bits) + columns[:, 2:3], -2)
    mine[...] = jnp.broadcast_to(ident, mine.shape)
    place = place_of(slots[1], columns[:, 1:2])[1]
    high = place + (place & ~LOW)
    pick_pair[...] = jnp.where(iota(pick_pair.shape, 1) == high, 1.0, 0.0).astype(BF16)
    v = vector[...] * SCALE
    energy[...] = jnp.sum((v * v).reshape(-1, 8, TILE), axis=0)
    for t in range(tiles.shape[0]):
        turned[t] = tiles[t].T


def gather(asked, vector):
    pieces = vector.shape[0]
    rows = asked.shape[0]
    lanes = iota((rows, TILE), 1)
    select = jnp.concatenate(
        [jnp.where(asked == lanes + k * TILE, 1.0, 0.0).astype(BF16) for k in range(pieces // TILE)], axis=1
    )
    return exact_dot(select, vector)


def served_kernel(n_x, bits, me, pair, vector, squares, asked_row, asked_col, riders, out, energy):
    first = (jnp.full((1, 1), me[0], jnp.int32) & 1) == 0
    peers = pair.shape[0] // 2
    col = pair[:peers, :]
    for k in range(HALF):
        sides = [jnp.broadcast_to(col[:, 16 * j : 16 * j + 1], col.shape) for j in (k, k + HALF)]
        value = jnp.where(first, sides[0], sides[1])
        asked_col[pl.ds(k, peers, LANE), :] = value
        asked_col[pl.ds(k + HALF, peers, LANE), :] = value
    chips = peers // n_x
    row = pair[pl.ds(peers, chips, n_x), :]
    for x in range(1, n_x):
        row = jnp.maximum(row, pair[pl.ds(peers + x, chips, n_x), :])
    riders[...] = row
    down = iota((2 * LANE, TILE), 0)
    side = jnp.where(iota((2 * LANE, TILE), 1) < TILE // 2, 0, 1) == (down >> BITS)
    parts = []
    for k in range(chips):
        rider = row[k : k + 1, :]
        here = ((rider >> (bits + BITS)) == me[0]) & ((rider & LOW) == (down & LOW)) & side
        value = jnp.where(here, ((rider >> BITS) & ((1 << bits) - 1)) + 1, 0).astype(F32)
        parts.append(jnp.sum(value, axis=1, keepdims=True))
    asked = jnp.broadcast_to(jnp.concatenate(parts, axis=0), asked_row.shape).astype(jnp.int32) - 1
    asked_row[...] = asked
    out[...] = gather(asked, vector[...] * SCALE)
    energy[...] = jnp.sum(squares[...], axis=0, keepdims=True)


def product_lane(asked_row, asked_col):
    rows = [asked_row[...].astype(F32).T[0:1, :]]
    width = asked_col.shape[0]
    for k in range(width // TILE):
        part = asked_col[k * TILE : (k + 1) * TILE, :].astype(F32).T[0:1, :]
        lane = iota((1, TILE), 1)
        rows.append(jnp.where((lane & LOW) >= HALF, part, -2.0))
    return [row.astype(jnp.int32) for row in rows]


def meet_tables(bits, asked_row, asked_col, mine, riders, me, meet, link, link_col, owned):
    lanes = product_lane(asked_row, asked_col)
    base = 0
    served_row, served_col = asked_row[...], asked_col[...]
    for served in (served_row, served_col):
        for k, lane in enumerate(lanes):
            hit = (served == lane) & (served >= 0)
            meet[base : base + served.shape[0], k * TILE : (k + 1) * TILE] = jnp.where(hit, 1.0, 0.0).astype(BF16)
        base += served.shape[0]
    ident = jnp.where(served_col < 0, -3, served_col + (me[0] << bits))
    slot = iota(owned.shape[:1] + (TILE,), 0)
    half = jnp.where(iota(owned.shape[:1] + (TILE,), 1) < mine.shape[0], 0, 1)
    for k in range(riders.shape[0]):
        rider = riders[k : k + 1, :]
        ids = rider >> BITS
        cols = slice(k * TILE, (k + 1) * TILE)
        link[:, cols] = jnp.where(mine[...] == ids, 1.0, 0.0).astype(BF16)
        link_col[:, cols] = jnp.where(ident == ids, 1.0, 0.0).astype(BF16)
        sent = ((rider >> (bits + BITS)) == me[0]) & ((rider & LOW) == (slot & LOW))
        sent = sent & ((slot >> BITS) == 2 * k + half)
        owned[:, cols] = jnp.where(sent, 1.0, 0.0).astype(BF16)


def multiply(x, tiles):
    count = x.shape[0]
    row = iota((16, TILE), 0) & 7
    groups = []
    for g in range(count // 8):
        part = x[g * 8 : (g + 1) * 8, :]
        high = part.astype(BF16).astype(F32)
        both = jnp.concatenate([high, part - high], axis=0)
        apart = jnp.concatenate([jnp.where(row == j, both, 0.0).astype(BF16) for j in range(8)], axis=1)
        y = dot(apart, tiles[g * 8 : (g + 1) * 8].reshape(8 * TILE, TILE))
        groups.append(y[0:8] + y[8:16])
    return jnp.concatenate(groups, axis=0)


def direct_kernel(
    bits, me, got, pick, tiles, put, asked_row, asked_col, mine, riders, vector,
    out, v_col, meet, link, link_col, owned,
):
    y = multiply(exact_dot(pick[...], got[...]), tiles)
    v = gather(asked_col[...], vector[...] * SCALE)
    v_col[...] = v
    forward = (iota(v.shape, 0) & LOW) < HALF
    out[...] = exact_dot(put[...], y) + jnp.where(forward, v, 0.0)
    meet_tables(bits, asked_row, asked_col, mine, riders, me, meet, link, link_col, owned)


def mirror_kernel(got, pick, tiles, put, meet, out):
    y = multiply(exact_dot(pick[...], got[...]), tiles)
    high, low = halves(y)
    width = put.shape[0]
    total = exact_dot(meet[:width, width:], got[...])
    low = dot(put[...], low)
    count = y.shape[0]
    for k in range(out.shape[0]):
        rows = slice(k * LANE, (k + 1) * LANE)
        out[k, :count, :] = high
        out[k, count:, :] = jnp.concatenate([total[rows], low[rows]], axis=0).astype(BF16)


def second_direct_kernel(got, link, link_col, owned, pick, meet, first_col, tiles, put, out, first_row):
    count = link.shape[0]
    peers = range(got.shape[0])
    mirrors = jnp.concatenate([got[k, :count, :] for k in peers], axis=0)
    sums = jnp.concatenate([got[k, count:, :] for k in peers], axis=0)
    y = multiply(dot(link[...], mirrors) + dot(pick[...], sums), tiles)
    width = got.shape[0] * LANE
    image = dot(link_col[...], mirrors) + exact_dot(meet[width:, width:], first_col[...])
    forward = (iota(image.shape, 0) & LOW) < HALF
    out[...] = exact_dot(put[...], y) + jnp.where(forward, image, 0.0)
    slot = iota((width, 2 * width), 0)
    low = iota((width, 2 * width), 1) == slot + (slot & ~LOW) + LANE
    first_row[...] = dot(owned[...], mirrors) + dot(jnp.where(low, 1.0, 0.0).astype(BF16), sums)


def second_mirror_kernel(got, pick, tiles, put, out):
    out[...] = exact_dot(put[...], multiply(exact_dot(pick[...], got[...]), tiles))


def inner_kernel(meet, energy, v_row, v_col, first_row, second_row, first_col, second_col, out):
    first_r, second_r = first_row[...], second_row[...]
    first = jnp.concatenate([first_r, first_col[...]], axis=0)
    second = jnp.concatenate([second_r, second_col[...]], axis=0)
    both = exact_dot(meet[...], jnp.concatenate([first, second], axis=1))
    image, total = both[:, :TILE], both[:, TILE:]
    width = v_row.shape[0]
    returned = (iota(v_col.shape, 0) & LOW) >= HALF
    first_c = jnp.where(returned, first_col[...], 0.0)
    second_c = jnp.where(returned, second_col[...], 0.0)

    def inner(a_r, b_r, a_c, b_c):
        return jnp.sum(a_r * b_r, axis=0, keepdims=True) + jnp.sum(a_c * b_c, axis=0, keepdims=True)

    values = [
        energy[...],
        inner(v_row[...], first_r, v_col[...], first_c),
        inner(image[:width], first_r, image[width:], first_c),
        inner(v_row[...], second_r, v_col[...], second_c),
        inner(image[:width], second_r, image[width:], second_c),
        inner(total[:width], second_r, total[width:], second_c),
    ]
    packed = jnp.concatenate(values + [jnp.zeros((2, TILE), F32)], axis=0)
    for k in range(out.shape[0]):
        out[k] = packed


def partial_kernel(got, out):
    total = jnp.sum(got[...], axis=0)
    sums = jnp.sum(total, axis=1, keepdims=True)
    packed = jnp.sum(jnp.where(iota(total.shape, 0) == iota(total.shape, 1), sums, 0.0), axis=0, keepdims=True)
    out[...] = jnp.broadcast_to(packed, out.shape)


def returned_rows(x):
    pairs = x.reshape(-1, 2, LANE, TILE)
    return jnp.concatenate([pairs[:, 0, HALF:, :], pairs[:, 1, HALF:, :]], axis=1).reshape(-1, TILE)


def final_kernel(
    total, got, vector, asked_row, asked_col, first_row, second_row, first_col, second_col,
    out, alpha, rest, near, sems,
):
    sums = jnp.sum(got[...], axis=0, keepdims=True)
    lane = iota((1, TILE), 1)

    def value(k):
        return jnp.sum(jnp.where(lane == k, sums, 0.0), axis=1, keepdims=True)

    vv, vi, ii, vw, iw, ww = [value(k) for k in range(6)]
    share = 1.0 / total
    g = lax.rsqrt(vv * (share / (SCALE * SCALE)) + 1e-06) * (1.0 / SCALE)
    c0 = g * (g * vi * share)
    square = g * (g * (ii - 2.0 * c0 * vi + c0 * c0 * vv) * share)
    square = jnp.maximum(square, 0.0) + 1e-06
    root = lax.rsqrt(square)
    b0 = square * root
    h = g * root
    c10 = h * (g * (vw - c0 * vi) * share)
    c11 = h * (h * (iw - c0 * ii - c0 * vw + c0 * c0 * vi) * share)
    a = c0 + c11
    b = c11 * c0 - c10 * b0
    square = h * (h * (ww + a * a * ii + b * b * vv - 2.0 * a * iw + 2.0 * b * vw - 2.0 * a * b * vi) * share)
    square = jnp.maximum(square, 0.0) + 1e-06
    root = lax.rsqrt(square)
    b1 = square * root
    f = h * root
    parts = sems.shape[0]
    step = vector.shape[0] // parts
    asked = [asked_row[...], returned_rows(asked_col[...])]
    lanes = jnp.concatenate([x.astype(F32).T[0:1, :].astype(jnp.int32) for x in asked], axis=1)
    image = jnp.concatenate([first_row[...], returned_rows(first_col[...])], axis=0)
    second = jnp.concatenate([second_row[...], returned_rows(second_col[...])], axis=0)
    high, low = halves(jnp.concatenate([image, second], axis=1))
    copies = []
    for k in range(parts):
        v = vector[pl.ds(k * step, step), :]
        place = iota((step, lanes.shape[1]), 0) + k * step
        select = jnp.where(place == lanes, 1.0, 0.0).astype(BF16)
        both = dot(select, high) + dot(select, low)
        i, w = both[:, :TILE], both[:, TILE:]
        near[pl.ds(2 * k * step, step, 2), :] = h * i - (h * c0 * SCALE) * v
        near[pl.ds(2 * k * step + 1, step, 2), :] = f * w - (f * a) * i + (f * b * SCALE) * v
        done = pl.ds(2 * k * step, 2 * step)
        copies.append(pltpu.make_async_copy(near.at[done], out.at[done], sems.at[k]))
        copies[-1].start()
    alpha[0] = c0[0, 0]
    rest[0] = b0[0, 0]
    rest[1] = c11[0, 0]
    rest[2] = b1[0, 0]
    for copy in copies:
        copy.wait()


def shape(*dims, dtype=F32):
    return jax.ShapeDtypeStruct(dims, dtype)


def call(kernel, outs, *args, ins=VMEM, out_specs=VMEM, scratch=(), limit=16):
    if isinstance(outs, tuple) and not isinstance(out_specs, tuple):
        out_specs = tuple([out_specs] * len(outs))
    return pl.pallas_call(
        kernel,
        out_shape=outs,
        in_specs=ins if isinstance(ins, list) else [ins] * len(args),
        out_specs=out_specs,
        scratch_shapes=scratch,
        compiler_params=pltpu.CompilerParams(vmem_limit_bytes=limit * 1024 * 1024),
    )(*args)


def exchange(x, axis, count):
    sent = x.reshape(count, -1, TILE)
    got = lax.all_to_all(sent, axis, split_axis=0, concat_axis=0, tiled=True)
    return got.reshape(x.shape)


def per_device(start_vector, tile_blocks, row_owner, row_block, col_owner, col_block, tile_counts):
    tiles = tile_blocks[0, 0]
    count = tiles.shape[0]
    vector = start_vector.reshape(-1, TILE)
    pieces = vector.shape[0]
    n_row, n_col = lax.axis_size("row"), lax.axis_size("col")
    wide_r, wide_c = n_row * LANE, n_col * LANE
    every = wide_r + wide_c
    total = float(pieces * TILE * n_row * n_col)

    def over_row(x):
        return exchange(x, "row", n_row)

    def over_col(x):
        return exchange(x, "col", n_col)

    bits = (pieces - 1).bit_length()
    n_y = n_row // 2
    n_x = n_col // n_y
    n_z = n_col // n_x
    planes = [[2 * y * n_col + c for c in range(n_col)] for y in range(n_y)]
    planes += [[(2 * y + 1) * n_col + x * n_z + z for y in range(n_y) for x in range(n_x)] for z in range(n_z)]
    chips = [[2 * y, 2 * y + 1] for y in range(n_y)]

    def over_chip(x):
        return lax.all_gather(x, "row", axis_index_groups=chips, tiled=True)

    slots = [row_owner, row_block, col_owner, col_block, tile_counts] + [jnp.zeros((), jnp.int32)] * 3
    slots = jnp.concatenate([jnp.broadcast_to(x.reshape(1, -1), (1, count)) for x in slots], axis=0)
    both = over_chip(slots)
    me, col = lax.axis_index("row").reshape(1), lax.axis_index("col").reshape(1)
    ask = call(
        functools.partial(request_kernel, bits, (n_x, n_z)),
        shape(n_col, TILE, dtype=jnp.int32),
        both,
        me,
        col,
        ins=[VMEM] + [SMEM] * 2,
    )
    ask = lax.all_to_all(
        ask.reshape(n_col, 1, TILE),
        ("row", "col"),
        split_axis=0,
        concat_axis=0,
        axis_index_groups=planes,
        tiled=True,
    ).reshape(n_col, TILE)
    pick_row, put_row, pick_col, put_col, pick_pair, mine, squares, turned = call(
        functools.partial(local_kernel, bits),
        (
            shape(count, wide_r, dtype=BF16),
            shape(wide_r, count, dtype=BF16),
            shape(count, wide_c, dtype=BF16),
            shape(wide_c, count, dtype=BF16),
            shape(count, 2 * wide_r, dtype=BF16),
            shape(count, TILE, dtype=jnp.int32),
            shape(8, TILE),
            shape(*tiles.shape, dtype=BF16),
        ),
        both,
        me,
        vector,
        tiles,
        ins=[VMEM, SMEM] + [VMEM] * 2,
    )
    asked_row, asked_col, riders, v_row, energy = call(
        functools.partial(served_kernel, n_x, bits),
        (
            shape(wide_r, TILE, dtype=jnp.int32),
            shape(wide_c, TILE, dtype=jnp.int32),
            shape(n_y, TILE, dtype=jnp.int32),
            shape(wide_r, TILE),
            shape(1, TILE),
        ),
        me,
        over_chip(ask),
        vector,
        squares,
        ins=[SMEM] + [VMEM] * 3,
    )
    x_col = over_row(v_row)
    first_col, v_col, meet, link, link_col, owned = call(
        functools.partial(direct_kernel, bits),
        (
            shape(wide_c, TILE),
            shape(wide_c, TILE),
            shape(every, every, dtype=BF16),
            shape(count, n_row * count, dtype=BF16),
            shape(wide_c, n_row * count, dtype=BF16),
            shape(wide_r, n_row * count, dtype=BF16),
        ),
        me,
        x_col,
        pick_row,
        turned,
        put_col,
        asked_row,
        asked_col,
        mine,
        riders,
        vector,
        ins=[SMEM] + [VMEM] * 9,
    )
    first_col = over_col(first_col)
    packed = call(
        mirror_kernel,
        shape(n_row, count + 2 * LANE, TILE, dtype=BF16),
        first_col,
        pick_col,
        tiles,
        put_row,
        meet,
    )
    second_col, first_row = call(
        second_direct_kernel,
        (shape(wide_c, TILE), shape(wide_r, TILE)),
        over_row(packed),
        link,
        link_col,
        owned,
        pick_pair,
        meet,
        first_col,
        turned,
        put_col,
    )
    second_col = over_col(second_col)
    second_row = over_row(
        call(second_mirror_kernel, shape(wide_r, TILE), second_col, pick_col, tiles, put_row)
    )
    products = (first_row, second_row, first_col, second_col)
    inner = call(inner_kernel, shape(n_row, 8, TILE), meet, energy, v_row, v_col, *products)
    inner = over_row(inner)
    inner = over_col(call(partial_kernel, shape(n_col, TILE), inner))

    def finish(*refs):
        final_kernel(total, *refs)

    out, alpha, rest = call(
        finish,
        (shape(2 * pieces, TILE), shape(1), shape(3)),
        inner,
        vector,
        asked_row,
        asked_col,
        *products,
        out_specs=(HBM, SMEM, SMEM),
        scratch=[pltpu.VMEM((2 * pieces, TILE), F32), pltpu.SemaphoreType.DMA((8,))],
    )
    basis = out.reshape(pieces, 2, TILE).transpose(1, 0, 2).reshape(2, pieces * TILE)
    return (basis, alpha, rest)


def solution(mesh):
    return jax.shard_map(
        per_device,
        mesh=mesh,
        in_specs=(
            P(("row", "col")),
            P("row", "col", None, None, None),
            P("row", "col", None, None),
            P("row", "col", None),
            P("row", "col", None, None),
            P("row", "col", None),
            P("row", "col"),
        ),
        out_specs=(P(None, ("row", "col")), P(), P()),
        check_vma=False,
    )
```

```python
import functools

import jax
import jax.numpy as jnp
from jax import lax
from jax.experimental import pallas as pl
from jax.experimental.pallas import tpu as pltpu
from jax.sharding import PartitionSpec as P

TILE = 128
LANE = 8
LOW = LANE - 1
BITS = 3
HALF = 4
SCALE = 1024.0
F32 = jnp.float32
BF16 = jnp.bfloat16
VMEM = pl.BlockSpec(memory_space=pltpu.VMEM)
SMEM = pl.BlockSpec(memory_space=pltpu.SMEM)
HBM = pl.BlockSpec(memory_space=pltpu.HBM)


def iota(shape, axis):
    return lax.broadcasted_iota(jnp.int32, shape, axis)


def halves(x):
    high = x.astype(BF16)
    low = (x - high.astype(F32)).astype(BF16)
    return high, low


def dot(a, b):
    return jnp.dot(a, b, preferred_element_type=F32)


def exact_dot(select, x):
    high, low = halves(x)
    return dot(select, high) + dot(select, low)


def place_of(owner, column):
    count = owner.shape[1]
    shape = (count, count)
    down, across = iota(shape, 0), iota(shape, 1)
    same = column == owner
    rank_row = jnp.sum(jnp.where(same & (down < across), 1, 0), axis=0, keepdims=True)
    rank_column = jnp.sum(jnp.where(same & (across < down), 1, 0), axis=1, keepdims=True)
    return owner * LANE + rank_row, column * LANE + rank_column


def columns_of(rows):
    rows = rows + [jnp.zeros_like(rows[0])] * (8 - len(rows))
    return jnp.concatenate(rows, axis=0).astype(F32).T.astype(jnp.int32)


def request_kernel(bits, planes, both, me, col, ask):
    n_x, n_z = planes
    first = (jnp.full((1, 1), me[0], jnp.int32) & 1) == 0
    x = col[0] // n_z
    count = both.shape[1]
    width = ask.shape[0]
    lane = iota((1, TILE), 1)
    core = jnp.where(lane < count, 0, 1)

    owner_r, block_r, owner_c, block_c, filled = [
        jnp.concatenate([both[k : k + 1, :], both[8 + k : 9 + k, :]], axis=1) for k in range(5)
    ]
    alive = lane - core * count < filled
    tags = [owner_r + core * count, owner_c + core * count]
    columns = columns_of(tags)
    earlier = iota((TILE, TILE), 0) < iota((TILE, TILE), 1)
    rank_r, rank_c = [
        jnp.sum(jnp.where((columns[:, k : k + 1] == tag) & earlier, 1, 0), axis=0, keepdims=True)
        for k, tag in enumerate(tags)
    ]
    packed = jnp.where(alive, (((owner_c << bits) + block_c) << BITS) + rank_c, -1)
    down = iota((width, TILE), 0)
    packed = jnp.where(down % n_x == x, packed, -9)
    slot = rank_r + core * HALF
    value = jnp.where((iota((TILE, TILE), 0) >> 4) == slot, jnp.where(alive, block_r + 1, 0), 0)
    there = jnp.where(down == owner_r, 1.0, 0.0).astype(BF16)
    rest = value & 15
    dims = (((1,), (1,)), ((), ()))
    total = sum(
        lax.dot_general(there, part.astype(F32).astype(BF16), dims, preferred_element_type=F32)
        for part in (value - rest, rest)
    )
    ask[...] = jnp.where(first, total.astype(jnp.int32) - 1, packed)


def local_kernel(
    bits, both, me, vector, tiles,
    pick_row, put_row, pick_col, put_col, pick_pair, mine, energy, turned,
):
    first = (jnp.full((1, 1), me[0], jnp.int32) & 1) == 0
    count = both.shape[1]
    slots = [jnp.where(first, both[k : k + 1, :], both[8 + k : 9 + k, :]) for k in (0, 2, 3)]
    live = jnp.where(first, both[4:5, 0:1], both[12:13, 0:1])
    columns = columns_of([jnp.concatenate([row, row], axis=1) for row in slots])[:count, :]
    for k, pick, put, shift in ((1, pick_row, put_row, 0), (0, pick_col, put_col, HALF)):
        width = put.shape[0]
        across, down = place_of(slots[k], columns[:, k : k + 1])
        pick[...] = jnp.where(iota((count, width), 1) == down, 1.0, 0.0).astype(BF16)
        put[...] = jnp.where(iota((width, count), 0) == across + shift, 1.0, 0.0).astype(BF16)
    ident = jnp.where(iota((count, 1), 0) < live, (columns[:, 1:2] << bits) + columns[:, 2:3], -2)
    mine[...] = jnp.broadcast_to(ident, mine.shape)
    place = place_of(slots[1], columns[:, 1:2])[1]
    high = place + (place & ~LOW) + (me[0] & 1) * LANE
    pick_pair[...] = jnp.where(iota(pick_pair.shape, 1) == high, 1.0, 0.0).astype(BF16)
    v = vector[...] * SCALE
    energy[...] = jnp.sum((v * v).reshape(-1, 8, TILE), axis=0)
    for t in range(tiles.shape[0]):
        turned[t] = tiles[t].T


def gather(asked, vector):
    pieces = vector.shape[0]
    rows = asked.shape[0]
    lanes = iota((rows, TILE), 1)
    select = jnp.concatenate(
        [jnp.where(asked == lanes + k * TILE, 1.0, 0.0).astype(BF16) for k in range(pieces // TILE)], axis=1
    )
    return exact_dot(select, vector)


def served_kernel(n_x, bits, me, pair, vector, squares, asked_row, asked_col, riders, out, energy):
    first = (jnp.full((1, 1), me[0], jnp.int32) & 1) == 0
    peers = pair.shape[0] // 2
    col = pair[:peers, :]
    for k in range(HALF):
        sides = [jnp.broadcast_to(col[:, 16 * j : 16 * j + 1], col.shape) for j in (k, k + HALF)]
        value = jnp.where(first, sides[0], sides[1])
        asked_col[pl.ds(k, peers, LANE), :] = value
        asked_col[pl.ds(k + HALF, peers, LANE), :] = value
    chips = peers // n_x
    row = pair[pl.ds(peers, chips, n_x), :]
    for x in range(1, n_x):
        row = jnp.maximum(row, pair[pl.ds(peers + x, chips, n_x), :])
    riders[...] = row
    down = iota((2 * LANE, TILE), 0)
    side = jnp.where(iota((2 * LANE, TILE), 1) < TILE // 2, 0, 1) == (down >> BITS)
    parts = []
    for k in range(chips):
        rider = row[k : k + 1, :]
        here = ((rider >> (bits + BITS)) == me[0]) & ((rider & LOW) == (down & LOW)) & side
        value = jnp.where(here, ((rider >> BITS) & ((1 << bits) - 1)) + 1, 0).astype(F32)
        parts.append(jnp.sum(value, axis=1, keepdims=True))
    asked = jnp.broadcast_to(jnp.concatenate(parts, axis=0), asked_row.shape).astype(jnp.int32) - 1
    asked_row[...] = asked
    out[...] = gather(asked, vector[...] * SCALE)
    energy[...] = jnp.sum(squares[...], axis=0, keepdims=True)


def product_lane(asked_row, asked_col):
    rows = [asked_row[...].astype(F32).T[0:1, :]]
    width = asked_col.shape[0]
    for k in range(width // TILE):
        part = asked_col[k * TILE : (k + 1) * TILE, :].astype(F32).T[0:1, :]
        lane = iota((1, TILE), 1)
        rows.append(jnp.where((lane & LOW) >= HALF, part, -2.0))
    return [row.astype(jnp.int32) for row in rows]


def meet_tables(bits, asked_row, asked_col, mine, riders, me, meet, link, link_col, owned):
    lanes = product_lane(asked_row, asked_col)
    base = 0
    served_row, served_col = asked_row[...], asked_col[...]
    for served in (served_row, served_col):
        for k, lane in enumerate(lanes):
            hit = (served == lane) & (served >= 0)
            meet[base : base + served.shape[0], k * TILE : (k + 1) * TILE] = jnp.where(hit, 1.0, 0.0).astype(BF16)
        base += served.shape[0]
    ident = jnp.where(served_col < 0, -3, served_col + (me[0] << bits))
    slot = iota(owned.shape[:1] + (TILE,), 0)
    half = jnp.where(iota(owned.shape[:1] + (TILE,), 1) < mine.shape[0], 0, 1)
    for k in range(riders.shape[0]):
        rider = riders[k : k + 1, :]
        ids = rider >> BITS
        cols = slice(k * TILE, (k + 1) * TILE)
        link[:, cols] = jnp.where(mine[...] == ids, 1.0, 0.0).astype(BF16)
        link_col[:, cols] = jnp.where(ident == ids, 1.0, 0.0).astype(BF16)
        sent = ((rider >> (bits + BITS)) == me[0]) & ((rider & LOW) == (slot & LOW))
        sent = sent & ((slot >> BITS) == 2 * k + half)
        owned[:, cols] = jnp.where(sent, 1.0, 0.0).astype(BF16)


def multiply(x, tiles):
    count = x.shape[0]
    row = iota((16, TILE), 0) & 7
    groups = []
    for g in range(count // 8):
        part = x[g * 8 : (g + 1) * 8, :]
        high = part.astype(BF16).astype(F32)
        both = jnp.concatenate([high, part - high], axis=0)
        apart = jnp.concatenate([jnp.where(row == j, both, 0.0).astype(BF16) for j in range(8)], axis=1)
        y = dot(apart, tiles[g * 8 : (g + 1) * 8].reshape(8 * TILE, TILE))
        groups.append(y[0:8] + y[8:16])
    return jnp.concatenate(groups, axis=0)


def direct_kernel(
    bits, me, got, pick, tiles, put, asked_row, asked_col, mine, riders, vector,
    out, v_col, meet, link, link_col, owned,
):
    y = multiply(exact_dot(pick[...], got[...]), tiles)
    v = gather(asked_col[...], vector[...] * SCALE)
    v_col[...] = v
    forward = (iota(v.shape, 0) & LOW) < HALF
    out[...] = exact_dot(put[...], y) + jnp.where(forward, v, 0.0)
    meet_tables(bits, asked_row, asked_col, mine, riders, me, meet, link, link_col, owned)


def mirror_kernel(got, pick, tiles, put, meet, out):
    y = multiply(exact_dot(pick[...], got[...]), tiles)
    high, low = halves(y)
    width = put.shape[0]
    total = exact_dot(meet[:width, width:], got[...])
    total, low = total.astype(BF16), dot(put[...], low).astype(BF16)
    count = y.shape[0]
    for k in range(out.shape[0]):
        rows = slice(2 * k * LANE, 2 * (k + 1) * LANE)
        out[k, :count, :] = high
        out[k, count : count + 2 * LANE, :] = total[rows]
        out[k, count + 2 * LANE :, :] = low[rows]


def second_direct_kernel(me, got, link, link_col, owned, pick, meet, first_col, tiles, put, out, first_row):
    count = link.shape[0]
    chips = got.shape[0] // 2
    peers = [core * chips + chip for chip in range(chips) for core in range(2)]
    middle = count + 2 * LANE
    mirrors = jnp.concatenate([got[k, :count, :] for k in peers], axis=0)
    sums = jnp.concatenate([got[k, count:middle, :] for k in peers], axis=0)
    lows = jnp.concatenate([got[k, middle:, :] for k in peers], axis=0)
    y = multiply(dot(link[...], mirrors) + dot(pick[...], sums), tiles)
    width = got.shape[0] * LANE
    image = dot(link_col[...], mirrors) + exact_dot(meet[width:, width:], first_col[...])
    forward = (iota(image.shape, 0) & LOW) < HALF
    out[...] = exact_dot(put[...], y) + jnp.where(forward, image, 0.0)
    slot = iota((width, 2 * width), 0)
    low = iota((width, 2 * width), 1) == slot + (slot & ~LOW) + (me[0] & 1) * LANE
    first_row[...] = dot(owned[...], mirrors) + dot(jnp.where(low, 1.0, 0.0).astype(BF16), lows)


def second_mirror_kernel(got, pick, tiles, put, out):
    out[...] = exact_dot(put[...], multiply(exact_dot(pick[...], got[...]), tiles))


def inner_kernel(meet, energy, v_row, v_col, first_row, second_row, first_col, second_col, out):
    first_r, second_r = first_row[...], second_row[...]
    first = jnp.concatenate([first_r, first_col[...]], axis=0)
    second = jnp.concatenate([second_r, second_col[...]], axis=0)
    both = exact_dot(meet[...], jnp.concatenate([first, second], axis=1))
    image, total = both[:, :TILE], both[:, TILE:]
    width = v_row.shape[0]
    returned = (iota(v_col.shape, 0) & LOW) >= HALF
    first_c = jnp.where(returned, first_col[...], 0.0)
    second_c = jnp.where(returned, second_col[...], 0.0)

    def inner(a_r, b_r, a_c, b_c):
        return jnp.sum(a_r * b_r, axis=0, keepdims=True) + jnp.sum(a_c * b_c, axis=0, keepdims=True)

    values = [
        energy[...],
        inner(v_row[...], first_r, v_col[...], first_c),
        inner(image[:width], first_r, image[width:], first_c),
        inner(v_row[...], second_r, v_col[...], second_c),
        inner(image[:width], second_r, image[width:], second_c),
        inner(total[:width], second_r, total[width:], second_c),
    ]
    packed = jnp.concatenate(values + [jnp.zeros((2, TILE), F32)], axis=0)
    for k in range(out.shape[0]):
        out[k] = packed


def partial_kernel(got, out):
    total = jnp.sum(got[...], axis=0)
    sums = jnp.sum(total, axis=1, keepdims=True)
    packed = jnp.sum(jnp.where(iota(total.shape, 0) == iota(total.shape, 1), sums, 0.0), axis=0, keepdims=True)
    out[...] = jnp.broadcast_to(packed, out.shape)


def returned_rows(x):
    pairs = x.reshape(-1, 2, LANE, TILE)
    return jnp.concatenate([pairs[:, 0, HALF:, :], pairs[:, 1, HALF:, :]], axis=1).reshape(-1, TILE)


def final_kernel(
    total, got, vector, asked_row, asked_col, first_row, second_row, first_col, second_col,
    out, alpha, rest, near, sems,
):
    sums = jnp.sum(got[...], axis=0, keepdims=True)
    lane = iota((1, TILE), 1)

    def value(k):
        return jnp.sum(jnp.where(lane == k, sums, 0.0), axis=1, keepdims=True)

    vv, vi, ii, vw, iw, ww = [value(k) for k in range(6)]
    share = 1.0 / total
    g = lax.rsqrt(vv * (share / (SCALE * SCALE)) + 1e-06) * (1.0 / SCALE)
    c0 = g * (g * vi * share)
    square = g * (g * (ii - 2.0 * c0 * vi + c0 * c0 * vv) * share)
    square = jnp.maximum(square, 0.0) + 1e-06
    root = lax.rsqrt(square)
    b0 = square * root
    h = g * root
    c10 = h * (g * (vw - c0 * vi) * share)
    c11 = h * (h * (iw - c0 * ii - c0 * vw + c0 * c0 * vi) * share)
    a = c0 + c11
    b = c11 * c0 - c10 * b0
    square = h * (h * (ww + a * a * ii + b * b * vv - 2.0 * a * iw + 2.0 * b * vw - 2.0 * a * b * vi) * share)
    square = jnp.maximum(square, 0.0) + 1e-06
    root = lax.rsqrt(square)
    b1 = square * root
    f = h * root
    parts = sems.shape[0]
    step = vector.shape[0] // parts
    asked = [asked_row[...], returned_rows(asked_col[...])]
    lanes = jnp.concatenate([x.astype(F32).T[0:1, :].astype(jnp.int32) for x in asked], axis=1)
    image = jnp.concatenate([first_row[...], returned_rows(first_col[...])], axis=0)
    second = jnp.concatenate([second_row[...], returned_rows(second_col[...])], axis=0)
    high, low = halves(jnp.concatenate([image, second], axis=1))
    copies = []
    for k in range(parts):
        v = vector[pl.ds(k * step, step), :]
        place = iota((step, lanes.shape[1]), 0) + k * step
        select = jnp.where(place == lanes, 1.0, 0.0).astype(BF16)
        both = dot(select, high) + dot(select, low)
        i, w = both[:, :TILE], both[:, TILE:]
        near[pl.ds(2 * k * step, step, 2), :] = h * i - (h * c0 * SCALE) * v
        near[pl.ds(2 * k * step + 1, step, 2), :] = f * w - (f * a) * i + (f * b * SCALE) * v
        done = pl.ds(2 * k * step, 2 * step)
        copies.append(pltpu.make_async_copy(near.at[done], out.at[done], sems.at[k]))
        copies[-1].start()
    alpha[0] = c0[0, 0]
    rest[0] = b0[0, 0]
    rest[1] = c11[0, 0]
    rest[2] = b1[0, 0]
    for copy in copies:
        copy.wait()


def shape(*dims, dtype=F32):
    return jax.ShapeDtypeStruct(dims, dtype)


def call(kernel, outs, *args, ins=VMEM, out_specs=VMEM, scratch=(), limit=16):
    if isinstance(outs, tuple) and not isinstance(out_specs, tuple):
        out_specs = tuple([out_specs] * len(outs))
    return pl.pallas_call(
        kernel,
        out_shape=outs,
        in_specs=ins if isinstance(ins, list) else [ins] * len(args),
        out_specs=out_specs,
        scratch_shapes=scratch,
        compiler_params=pltpu.CompilerParams(vmem_limit_bytes=limit * 1024 * 1024),
    )(*args)


def exchange(x, axis, count):
    sent = x.reshape(count, -1, TILE)
    got = lax.all_to_all(sent, axis, split_axis=0, concat_axis=0, tiled=True)
    return got.reshape(x.shape)


def per_device(start_vector, tile_blocks, row_owner, row_block, col_owner, col_block, tile_counts):
    tiles = tile_blocks[0, 0]
    count = tiles.shape[0]
    vector = start_vector.reshape(-1, TILE)
    pieces = vector.shape[0]
    n_row, n_col = lax.axis_size("row"), lax.axis_size("col")
    wide_r, wide_c = n_row * LANE, n_col * LANE
    every = wide_r + wide_c
    total = float(pieces * TILE * n_row * n_col)

    def over_row(x):
        return exchange(x, "row", n_row)

    def over_col(x):
        return exchange(x, "col", n_col)

    bits = (pieces - 1).bit_length()
    n_y = n_row // 2
    n_x = n_col // n_y
    n_z = n_col // n_x
    planes = [[2 * y * n_col + c for c in range(n_col)] for y in range(n_y)]
    planes += [[(2 * y + 1) * n_col + x * n_z + z for y in range(n_y) for x in range(n_x)] for z in range(n_z)]
    chips = [[2 * y, 2 * y + 1] for y in range(n_y)]

    def over_chip(x):
        return lax.all_gather(x, "row", axis_index_groups=chips, tiled=True)

    slots = [row_owner, row_block, col_owner, col_block, tile_counts] + [jnp.zeros((), jnp.int32)] * 3
    slots = jnp.concatenate([jnp.broadcast_to(x.reshape(1, -1), (1, count)) for x in slots], axis=0)
    both = over_chip(slots)
    me, col = lax.axis_index("row").reshape(1), lax.axis_index("col").reshape(1)
    ask = call(
        functools.partial(request_kernel, bits, (n_x, n_z)),
        shape(n_col, TILE, dtype=jnp.int32),
        both,
        me,
        col,
        ins=[VMEM] + [SMEM] * 2,
    )
    ask = lax.all_to_all(
        ask.reshape(n_col, 1, TILE),
        ("row", "col"),
        split_axis=0,
        concat_axis=0,
        axis_index_groups=planes,
        tiled=True,
    ).reshape(n_col, TILE)
    pick_row, put_row, pick_col, put_col, pick_pair, mine, squares, turned = call(
        functools.partial(local_kernel, bits),
        (
            shape(count, wide_r, dtype=BF16),
            shape(wide_r, count, dtype=BF16),
            shape(count, wide_c, dtype=BF16),
            shape(wide_c, count, dtype=BF16),
            shape(count, 2 * wide_r, dtype=BF16),
            shape(count, TILE, dtype=jnp.int32),
            shape(8, TILE),
            shape(*tiles.shape, dtype=BF16),
        ),
        both,
        me,
        vector,
        tiles,
        ins=[VMEM, SMEM] + [VMEM] * 2,
    )
    asked_row, asked_col, riders, v_row, energy = call(
        functools.partial(served_kernel, n_x, bits),
        (
            shape(wide_r, TILE, dtype=jnp.int32),
            shape(wide_c, TILE, dtype=jnp.int32),
            shape(n_y, TILE, dtype=jnp.int32),
            shape(wide_r, TILE),
            shape(1, TILE),
        ),
        me,
        over_chip(ask),
        vector,
        squares,
        ins=[SMEM] + [VMEM] * 3,
    )
    x_col = over_row(v_row)
    first_col, v_col, meet, link, link_col, owned = call(
        functools.partial(direct_kernel, bits),
        (
            shape(wide_c, TILE),
            shape(wide_c, TILE),
            shape(every, every, dtype=BF16),
            shape(count, n_row * count, dtype=BF16),
            shape(wide_c, n_row * count, dtype=BF16),
            shape(wide_r, n_row * count, dtype=BF16),
        ),
        me,
        x_col,
        pick_row,
        turned,
        put_col,
        asked_row,
        asked_col,
        mine,
        riders,
        vector,
        ins=[SMEM] + [VMEM] * 9,
    )
    first_col = over_col(first_col)
    packed = call(
        mirror_kernel,
        shape(n_y, count + 4 * LANE, TILE, dtype=BF16),
        first_col,
        pick_col,
        tiles,
        put_row,
        meet,
    )
    cores = [[2 * y + core for y in range(n_y)] for core in range(2)]
    packed = lax.all_to_all(packed, "row", split_axis=0, concat_axis=0, axis_index_groups=cores, tiled=True)
    second_col, first_row = call(
        second_direct_kernel,
        (shape(wide_c, TILE), shape(wide_r, TILE)),
        me,
        over_chip(packed),
        link,
        link_col,
        owned,
        pick_pair,
        meet,
        first_col,
        turned,
        put_col,
        ins=[SMEM] + [VMEM] * 9,
    )
    second_col = over_col(second_col)
    second_row = over_row(
        call(second_mirror_kernel, shape(wide_r, TILE), second_col, pick_col, tiles, put_row)
    )
    products = (first_row, second_row, first_col, second_col)
    inner = call(inner_kernel, shape(n_row, 8, TILE), meet, energy, v_row, v_col, *products)
    inner = over_row(inner)
    inner = over_col(call(partial_kernel, shape(n_col, TILE), inner))

    def finish(*refs):
        final_kernel(total, *refs)

    out, alpha, rest = call(
        finish,
        (shape(2 * pieces, TILE), shape(1), shape(3)),
        inner,
        vector,
        asked_row,
        asked_col,
        *products,
        out_specs=(HBM, SMEM, SMEM),
        scratch=[pltpu.VMEM((2 * pieces, TILE), F32), pltpu.SemaphoreType.DMA((8,))],
    )
    basis = out.reshape(pieces, 2, TILE).transpose(1, 0, 2).reshape(2, pieces * TILE)
    return (basis, alpha, rest)


def solution(mesh):
    return jax.shard_map(
        per_device,
        mesh=mesh,
        in_specs=(
            P(("row", "col")),
            P("row", "col", None, None, None),
            P("row", "col", None, None),
            P("row", "col", None),
            P("row", "col", None, None),
            P("row", "col", None),
            P("row", "col"),
        ),
        out_specs=(P(None, ("row", "col")), P(), P()),
        check_vma=False,
    )
```

```python
import functools

import jax
import jax.numpy as jnp
from jax import lax
from jax.experimental import pallas as pl
from jax.experimental.pallas import tpu as pltpu
from jax.sharding import PartitionSpec as P

TILE = 128
LANE = 8
LOW = LANE - 1
BITS = 3
HALF = 4
SCALE = 1024.0
F32 = jnp.float32
BF16 = jnp.bfloat16
VMEM = pl.BlockSpec(memory_space=pltpu.VMEM)
SMEM = pl.BlockSpec(memory_space=pltpu.SMEM)
HBM = pl.BlockSpec(memory_space=pltpu.HBM)


def iota(shape, axis):
    return lax.broadcasted_iota(jnp.int32, shape, axis)


def halves(x):
    high = x.astype(BF16)
    low = (x - high.astype(F32)).astype(BF16)
    return high, low


def dot(a, b):
    return jnp.dot(a, b, preferred_element_type=F32)


def exact_dot(select, x):
    high, low = halves(x)
    return dot(select, high) + dot(select, low)


def place_of(owner, column):
    count = owner.shape[1]
    shape = (count, count)
    down, across = iota(shape, 0), iota(shape, 1)
    same = column == owner
    rank_row = jnp.sum(jnp.where(same & (down < across), 1, 0), axis=0, keepdims=True)
    rank_column = jnp.sum(jnp.where(same & (across < down), 1, 0), axis=1, keepdims=True)
    return owner * LANE + rank_row, column * LANE + rank_column


def columns_of(rows):
    rows = rows + [jnp.zeros_like(rows[0])] * (8 - len(rows))
    return jnp.concatenate(rows, axis=0).astype(F32).T.astype(jnp.int32)


def request_kernel(bits, planes, both, me, col, ask):
    n_x, n_z = planes
    first = (jnp.full((1, 1), me[0], jnp.int32) & 1) == 0
    x = col[0] // n_z
    count = both.shape[1]
    width = ask.shape[0]
    lane = iota((1, TILE), 1)
    core = jnp.where(lane < count, 0, 1)

    owner_r, block_r, owner_c, block_c, filled = [
        jnp.concatenate([both[k : k + 1, :], both[8 + k : 9 + k, :]], axis=1) for k in range(5)
    ]
    alive = lane - core * count < filled
    tags = [owner_r + core * count, owner_c + core * count]
    columns = columns_of(tags)
    earlier = iota((TILE, TILE), 0) < iota((TILE, TILE), 1)
    rank_r, rank_c = [
        jnp.sum(jnp.where((columns[:, k : k + 1] == tag) & earlier, 1, 0), axis=0, keepdims=True)
        for k, tag in enumerate(tags)
    ]
    packed = jnp.where(alive, (((owner_c << bits) + block_c) << BITS) + rank_c, -1)
    down = iota((width, TILE), 0)
    packed = jnp.where(down % n_x == x, packed, -9)
    slot = rank_r + core * HALF
    value = jnp.where((iota((TILE, TILE), 0) >> 4) == slot, jnp.where(alive, block_r + 1, 0), 0)
    there = jnp.where(down == owner_r, 1.0, 0.0).astype(BF16)
    rest = value & 15
    dims = (((1,), (1,)), ((), ()))
    total = sum(
        lax.dot_general(there, part.astype(F32).astype(BF16), dims, preferred_element_type=F32)
        for part in (value - rest, rest)
    )
    ask[...] = jnp.where(first, total.astype(jnp.int32) - 1, packed)


def local_kernel(
    bits, both, me, vector, tiles,
    pick_row, put_row, pick_col, put_col, pick_pair, mine, energy, turned,
):
    first = (jnp.full((1, 1), me[0], jnp.int32) & 1) == 0
    count = both.shape[1]
    slots = [jnp.where(first, both[k : k + 1, :], both[8 + k : 9 + k, :]) for k in (0, 2, 3)]
    live = jnp.where(first, both[4:5, 0:1], both[12:13, 0:1])
    columns = columns_of([jnp.concatenate([row, row], axis=1) for row in slots])[:count, :]
    for k, pick, put, shift in ((1, pick_row, put_row, 0), (0, pick_col, put_col, HALF)):
        width = put.shape[0]
        across, down = place_of(slots[k], columns[:, k : k + 1])
        pick[...] = jnp.where(iota((count, width), 1) == down, 1.0, 0.0).astype(BF16)
        put[...] = jnp.where(iota((width, count), 0) == across + shift, 1.0, 0.0).astype(BF16)
    ident = jnp.where(iota((count, 1), 0) < live, (columns[:, 1:2] << bits) + columns[:, 2:3], -2)
    mine[...] = jnp.broadcast_to(ident, mine.shape)
    place = place_of(slots[1], columns[:, 1:2])[1]
    high = place + (place & ~LOW) + (me[0] & 1) * LANE
    pick_pair[...] = jnp.where(iota(pick_pair.shape, 1) == high, 1.0, 0.0).astype(BF16)
    v = vector[...] * SCALE
    energy[...] = jnp.sum((v * v).reshape(-1, 8, TILE), axis=0)
    for t in range(tiles.shape[0]):
        turned[t] = tiles[t].T


def gather(asked, vector):
    pieces = vector.shape[0]
    rows = asked.shape[0]
    lanes = iota((rows, TILE), 1)
    select = jnp.concatenate(
        [jnp.where(asked == lanes + k * TILE, 1.0, 0.0).astype(BF16) for k in range(pieces // TILE)], axis=1
    )
    return exact_dot(select, vector)


def served_kernel(n_x, bits, me, pair, vector, squares, asked_row, asked_col, riders, out, energy):
    first = (jnp.full((1, 1), me[0], jnp.int32) & 1) == 0
    peers = pair.shape[0] // 2
    col = pair[:peers, :]
    for k in range(HALF):
        sides = [jnp.broadcast_to(col[:, 16 * j : 16 * j + 1], col.shape) for j in (k, k + HALF)]
        value = jnp.where(first, sides[0], sides[1])
        asked_col[pl.ds(k, peers, LANE), :] = value
        asked_col[pl.ds(k + HALF, peers, LANE), :] = value
    chips = peers // n_x
    row = pair[pl.ds(peers, chips, n_x), :]
    for x in range(1, n_x):
        row = jnp.maximum(row, pair[pl.ds(peers + x, chips, n_x), :])
    riders[...] = row
    down = iota((2 * LANE, TILE), 0)
    side = jnp.where(iota((2 * LANE, TILE), 1) < TILE // 2, 0, 1) == (down >> BITS)
    parts = []
    for k in range(chips):
        rider = row[k : k + 1, :]
        here = ((rider >> (bits + BITS)) == me[0]) & ((rider & LOW) == (down & LOW)) & side
        value = jnp.where(here, ((rider >> BITS) & ((1 << bits) - 1)) + 1, 0).astype(F32)
        parts.append(jnp.sum(value, axis=1, keepdims=True))
    asked = jnp.broadcast_to(jnp.concatenate(parts, axis=0), asked_row.shape).astype(jnp.int32) - 1
    asked_row[...] = asked
    out[...] = gather(asked, vector[...] * SCALE)
    energy[...] = jnp.sum(squares[...], axis=0, keepdims=True)


def returned_rows(x):
    pairs = x.reshape(-1, 2, LANE, TILE)
    return jnp.concatenate([pairs[:, 0, HALF:, :], pairs[:, 1, HALF:, :]], axis=1).reshape(-1, TILE)


def laid_twice(x):
    halves_of = [x.reshape(-1, LANE, TILE)[:, k : k + HALF, :] for k in (0, HALF)]
    pairs = [jnp.concatenate([half, half], axis=1) for half in halves_of]
    return jnp.stack(pairs, axis=1).reshape(-1, TILE)


def product_lane(asked_row, asked_col):
    rows = [asked_row[...].astype(F32).T[0:1, :]]
    width = asked_col.shape[0]
    for k in range(width // TILE):
        part = asked_col[k * TILE : (k + 1) * TILE, :].astype(F32).T[0:1, :]
        lane = iota((1, TILE), 1)
        rows.append(jnp.where((lane & LOW) >= HALF, part, -2.0))
    return [row.astype(jnp.int32) for row in rows]


def meet_tables(bits, asked_row, asked_col, mine, riders, me, meet, link, link_col, owned):
    lanes = product_lane(asked_row, asked_col)
    base = 0
    served_row, served_col = asked_row[...], asked_col[...]
    for served in (served_row, served_col):
        for k, lane in enumerate(lanes):
            hit = (served == lane) & (served >= 0)
            meet[base : base + served.shape[0], k * TILE : (k + 1) * TILE] = jnp.where(hit, 1.0, 0.0).astype(BF16)
        base += served.shape[0]
    ident = returned_rows(served_col)
    ident = jnp.where(ident < 0, -3, ident + (me[0] << bits))
    slot = iota(owned.shape[:1] + (TILE,), 0)
    half = jnp.where(iota(owned.shape[:1] + (TILE,), 1) < mine.shape[0], 0, 1)
    for k in range(riders.shape[0]):
        rider = riders[k : k + 1, :]
        ids = rider >> BITS
        cols = slice(k * TILE, (k + 1) * TILE)
        link[:, cols] = jnp.where(mine[...] == ids, 1.0, 0.0).astype(BF16)
        link_col[:, cols] = jnp.where(ident == ids, 1.0, 0.0).astype(BF16)
        sent = ((rider >> (bits + BITS)) == me[0]) & ((rider & LOW) == (slot & LOW))
        sent = sent & ((slot >> BITS) == 2 * k + half)
        owned[:, cols] = jnp.where(sent, 1.0, 0.0).astype(BF16)


def multiply(x, tiles):
    count = x.shape[0]
    row = iota((16, TILE), 0) & 7
    groups = []
    for g in range(count // 8):
        part = x[g * 8 : (g + 1) * 8, :]
        high = part.astype(BF16).astype(F32)
        both = jnp.concatenate([high, part - high], axis=0)
        apart = jnp.concatenate([jnp.where(row == j, both, 0.0).astype(BF16) for j in range(8)], axis=1)
        y = dot(apart, tiles[g * 8 : (g + 1) * 8].reshape(8 * TILE, TILE))
        groups.append(y[0:8] + y[8:16])
    return jnp.concatenate(groups, axis=0)


def direct_kernel(
    bits, me, got, pick, tiles, put, asked_row, asked_col, mine, riders, vector,
    out, v_col, meet, link, link_col, owned,
):
    y = multiply(exact_dot(pick[...], got[...]), tiles)
    v = laid_twice(gather(returned_rows(asked_col[...]), vector[...] * SCALE))
    v_col[...] = v
    forward = (iota(v.shape, 0) & LOW) < HALF
    out[...] = exact_dot(put[...], y) + jnp.where(forward, v, 0.0)
    meet_tables(bits, asked_row, asked_col, mine, riders, me, meet, link, link_col, owned)


def mirror_kernel(got, pick, tiles, put, meet, out):
    y = multiply(exact_dot(pick[...], got[...]), tiles)
    high, low = halves(y)
    width = put.shape[0]
    total = exact_dot(meet[:width, width:], got[...])
    total, low = total.astype(BF16), dot(put[...], low).astype(BF16)
    count = y.shape[0]
    for k in range(out.shape[0]):
        rows = slice(2 * k * LANE, 2 * (k + 1) * LANE)
        out[k, :count, :] = high
        out[k, count : count + 2 * LANE, :] = total[rows]
        out[k, count + 2 * LANE :, :] = low[rows]


def second_direct_kernel(me, got, link, link_col, owned, pick, meet, first_col, tiles, put, out, first_row):
    count = link.shape[0]
    chips = got.shape[0] // 2
    peers = [core * chips + chip for chip in range(chips) for core in range(2)]
    middle = count + 2 * LANE
    mirrors = jnp.concatenate([got[k, :count, :] for k in peers], axis=0)
    sums = jnp.concatenate([got[k, count:middle, :] for k in peers], axis=0)
    lows = jnp.concatenate([got[k, middle:, :] for k in peers], axis=0)
    y = multiply(dot(link[...], mirrors) + dot(pick[...], sums), tiles)
    width = got.shape[0] * LANE
    image = laid_twice(dot(link_col[...], mirrors)) + exact_dot(meet[width:, width:], first_col[...])
    forward = (iota(image.shape, 0) & LOW) < HALF
    out[...] = exact_dot(put[...], y) + jnp.where(forward, image, 0.0)
    slot = iota((width, 2 * width), 0)
    low = iota((width, 2 * width), 1) == slot + (slot & ~LOW) + (me[0] & 1) * LANE
    first_row[...] = dot(owned[...], mirrors) + dot(jnp.where(low, 1.0, 0.0).astype(BF16), lows)


def second_mirror_kernel(got, pick, tiles, put, out):
    out[...] = exact_dot(put[...], multiply(exact_dot(pick[...], got[...]), tiles))


def inner_kernel(meet, energy, v_row, v_col, first_row, second_row, first_col, second_col, out):
    first_r, second_r = first_row[...], second_row[...]
    first = jnp.concatenate([first_r, first_col[...]], axis=0)
    second = jnp.concatenate([second_r, second_col[...]], axis=0)
    both = exact_dot(meet[...], jnp.concatenate([first, second], axis=1))
    image, total = both[:, :TILE], both[:, TILE:]
    width = v_row.shape[0]
    returned = (iota(v_col.shape, 0) & LOW) >= HALF
    first_c = jnp.where(returned, first_col[...], 0.0)
    second_c = jnp.where(returned, second_col[...], 0.0)

    def inner(a_r, b_r, a_c, b_c):
        return jnp.sum(a_r * b_r, axis=0, keepdims=True) + jnp.sum(a_c * b_c, axis=0, keepdims=True)

    values = [
        energy[...],
        inner(v_row[...], first_r, v_col[...], first_c),
        inner(image[:width], first_r, image[width:], first_c),
        inner(v_row[...], second_r, v_col[...], second_c),
        inner(image[:width], second_r, image[width:], second_c),
        inner(total[:width], second_r, total[width:], second_c),
    ]
    packed = jnp.concatenate(values + [jnp.zeros((2, TILE), F32)], axis=0)
    for k in range(out.shape[0]):
        out[k] = packed


def partial_kernel(got, out):
    total = jnp.sum(got[...], axis=0)
    sums = jnp.sum(total, axis=1, keepdims=True)
    packed = jnp.sum(jnp.where(iota(total.shape, 0) == iota(total.shape, 1), sums, 0.0), axis=0, keepdims=True)
    out[...] = jnp.broadcast_to(packed, out.shape)


def final_kernel(
    total, got, vector, asked_row, asked_col, first_row, second_row, first_col, second_col,
    out, alpha, rest, near, sems,
):
    sums = jnp.sum(got[...], axis=0, keepdims=True)
    lane = iota((1, TILE), 1)

    def value(k):
        return jnp.sum(jnp.where(lane == k, sums, 0.0), axis=1, keepdims=True)

    vv, vi, ii, vw, iw, ww = [value(k) for k in range(6)]
    share = 1.0 / total
    g = lax.rsqrt(vv * (share / (SCALE * SCALE)) + 1e-06) * (1.0 / SCALE)
    c0 = g * (g * vi * share)
    square = g * (g * (ii - 2.0 * c0 * vi + c0 * c0 * vv) * share)
    square = jnp.maximum(square, 0.0) + 1e-06
    root = lax.rsqrt(square)
    b0 = square * root
    h = g * root
    c10 = h * (g * (vw - c0 * vi) * share)
    c11 = h * (h * (iw - c0 * ii - c0 * vw + c0 * c0 * vi) * share)
    a = c0 + c11
    b = c11 * c0 - c10 * b0
    square = h * (h * (ww + a * a * ii + b * b * vv - 2.0 * a * iw + 2.0 * b * vw - 2.0 * a * b * vi) * share)
    square = jnp.maximum(square, 0.0) + 1e-06
    root = lax.rsqrt(square)
    b1 = square * root
    f = h * root
    parts = sems.shape[0]
    step = vector.shape[0] // parts
    asked = [asked_row[...], returned_rows(asked_col[...])]
    lanes = jnp.concatenate([x.astype(F32).T[0:1, :].astype(jnp.int32) for x in asked], axis=1)
    image = jnp.concatenate([first_row[...], returned_rows(first_col[...])], axis=0)
    second = jnp.concatenate([second_row[...], returned_rows(second_col[...])], axis=0)
    high, low = halves(jnp.concatenate([image, second], axis=1))
    copies = []
    for k in range(parts):
        v = vector[pl.ds(k * step, step), :]
        place = iota((step, lanes.shape[1]), 0) + k * step
        select = jnp.where(place == lanes, 1.0, 0.0).astype(BF16)
        both = dot(select, high) + dot(select, low)
        i, w = both[:, :TILE], both[:, TILE:]
        near[pl.ds(2 * k * step, step, 2), :] = h * i - (h * c0 * SCALE) * v
        near[pl.ds(2 * k * step + 1, step, 2), :] = f * w - (f * a) * i + (f * b * SCALE) * v
        done = pl.ds(2 * k * step, 2 * step)
        copies.append(pltpu.make_async_copy(near.at[done], out.at[done], sems.at[k]))
        copies[-1].start()
    alpha[0] = c0[0, 0]
    rest[0] = b0[0, 0]
    rest[1] = c11[0, 0]
    rest[2] = b1[0, 0]
    for copy in copies:
        copy.wait()


def shape(*dims, dtype=F32):
    return jax.ShapeDtypeStruct(dims, dtype)


def call(kernel, outs, *args, ins=VMEM, out_specs=VMEM, scratch=(), limit=16):
    if isinstance(outs, tuple) and not isinstance(out_specs, tuple):
        out_specs = tuple([out_specs] * len(outs))
    return pl.pallas_call(
        kernel,
        out_shape=outs,
        in_specs=ins if isinstance(ins, list) else [ins] * len(args),
        out_specs=out_specs,
        scratch_shapes=scratch,
        compiler_params=pltpu.CompilerParams(vmem_limit_bytes=limit * 1024 * 1024),
    )(*args)


def exchange(x, axis, count):
    sent = x.reshape(count, -1, TILE)
    got = lax.all_to_all(sent, axis, split_axis=0, concat_axis=0, tiled=True)
    return got.reshape(x.shape)


def per_device(start_vector, tile_blocks, row_owner, row_block, col_owner, col_block, tile_counts):
    tiles = tile_blocks[0, 0]
    count = tiles.shape[0]
    vector = start_vector.reshape(-1, TILE)
    pieces = vector.shape[0]
    n_row, n_col = lax.axis_size("row"), lax.axis_size("col")
    wide_r, wide_c = n_row * LANE, n_col * LANE
    every = wide_r + wide_c
    total = float(pieces * TILE * n_row * n_col)

    def over_row(x):
        return exchange(x, "row", n_row)

    def over_col(x):
        return exchange(x, "col", n_col)

    bits = (pieces - 1).bit_length()
    n_y = n_row // 2
    n_x = n_col // n_y
    n_z = n_col // n_x
    planes = [[2 * y * n_col + c for c in range(n_col)] for y in range(n_y)]
    planes += [[(2 * y + 1) * n_col + x * n_z + z for y in range(n_y) for x in range(n_x)] for z in range(n_z)]
    chips = [[2 * y, 2 * y + 1] for y in range(n_y)]

    def over_chip(x):
        return lax.all_gather(x, "row", axis_index_groups=chips, tiled=True)

    slots = [row_owner, row_block, col_owner, col_block, tile_counts] + [jnp.zeros((), jnp.int32)] * 3
    slots = jnp.concatenate([jnp.broadcast_to(x.reshape(1, -1), (1, count)) for x in slots], axis=0)
    both = over_chip(slots)
    me, col = lax.axis_index("row").reshape(1), lax.axis_index("col").reshape(1)
    ask = call(
        functools.partial(request_kernel, bits, (n_x, n_z)),
        shape(n_col, TILE, dtype=jnp.int32),
        both,
        me,
        col,
        ins=[VMEM] + [SMEM] * 2,
    )
    ask = lax.all_to_all(
        ask.reshape(n_col, 1, TILE),
        ("row", "col"),
        split_axis=0,
        concat_axis=0,
        axis_index_groups=planes,
        tiled=True,
    ).reshape(n_col, TILE)
    pick_row, put_row, pick_col, put_col, pick_pair, mine, squares, turned = call(
        functools.partial(local_kernel, bits),
        (
            shape(count, wide_r, dtype=BF16),
            shape(wide_r, count, dtype=BF16),
            shape(count, wide_c, dtype=BF16),
            shape(wide_c, count, dtype=BF16),
            shape(count, 2 * wide_r, dtype=BF16),
            shape(count, TILE, dtype=jnp.int32),
            shape(8, TILE),
            shape(*tiles.shape, dtype=BF16),
        ),
        both,
        me,
        vector,
        tiles,
        ins=[VMEM, SMEM] + [VMEM] * 2,
    )
    asked_row, asked_col, riders, v_row, energy = call(
        functools.partial(served_kernel, n_x, bits),
        (
            shape(wide_r, TILE, dtype=jnp.int32),
            shape(wide_c, TILE, dtype=jnp.int32),
            shape(n_y, TILE, dtype=jnp.int32),
            shape(wide_r, TILE),
            shape(1, TILE),
        ),
        me,
        over_chip(ask),
        vector,
        squares,
        ins=[SMEM] + [VMEM] * 3,
    )
    x_col = over_row(v_row)
    first_col, v_col, meet, link, link_col, owned = call(
        functools.partial(direct_kernel, bits),
        (
            shape(wide_c, TILE),
            shape(wide_c, TILE),
            shape(every, every, dtype=BF16),
            shape(count, n_row * count, dtype=BF16),
            shape(wide_c // 2, n_row * count, dtype=BF16),
            shape(wide_r, n_row * count, dtype=BF16),
        ),
        me,
        x_col,
        pick_row,
        turned,
        put_col,
        asked_row,
        asked_col,
        mine,
        riders,
        vector,
        ins=[SMEM] + [VMEM] * 9,
    )
    first_col = over_col(first_col)
    packed = call(
        mirror_kernel,
        shape(n_y, count + 4 * LANE, TILE, dtype=BF16),
        first_col,
        pick_col,
        tiles,
        put_row,
        meet,
    )
    cores = [[2 * y + core for y in range(n_y)] for core in range(2)]
    packed = lax.all_to_all(packed, "row", split_axis=0, concat_axis=0, axis_index_groups=cores, tiled=True)
    second_col, first_row = call(
        second_direct_kernel,
        (shape(wide_c, TILE), shape(wide_r, TILE)),
        me,
        over_chip(packed),
        link,
        link_col,
        owned,
        pick_pair,
        meet,
        first_col,
        turned,
        put_col,
        ins=[SMEM] + [VMEM] * 9,
    )
    second_col = over_col(second_col)
    second_row = over_row(
        call(second_mirror_kernel, shape(wide_r, TILE), second_col, pick_col, tiles, put_row)
    )
    products = (first_row, second_row, first_col, second_col)
    inner = call(inner_kernel, shape(n_row, 8, TILE), meet, energy, v_row, v_col, *products)
    inner = over_row(inner)
    inner = over_col(call(partial_kernel, shape(n_col, TILE), inner))

    def finish(*refs):
        final_kernel(total, *refs)

    out, alpha, rest = call(
        finish,
        (shape(2 * pieces, TILE), shape(1), shape(3)),
        inner,
        vector,
        asked_row,
        asked_col,
        *products,
        out_specs=(HBM, SMEM, SMEM),
        scratch=[pltpu.VMEM((2 * pieces, TILE), F32), pltpu.SemaphoreType.DMA((8,))],
    )
    basis = out.reshape(pieces, 2, TILE).transpose(1, 0, 2).reshape(2, pieces * TILE)
    return (basis, alpha, rest)


def solution(mesh):
    return jax.shard_map(
        per_device,
        mesh=mesh,
        in_specs=(
            P(("row", "col")),
            P("row", "col", None, None, None),
            P("row", "col", None, None),
            P("row", "col", None),
            P("row", "col", None, None),
            P("row", "col", None),
            P("row", "col"),
        ),
        out_specs=(P(None, ("row", "col")), P(), P()),
        check_vma=False,
    )
```

```python
import functools

import jax
import jax.numpy as jnp
from jax import lax
from jax.experimental import pallas as pl
from jax.experimental.pallas import tpu as pltpu
from jax.sharding import PartitionSpec as P

TILE = 128
LANE = 8
LOW = LANE - 1
BITS = 3
HALF = 4
SCALE = 1024.0
F32 = jnp.float32
BF16 = jnp.bfloat16
VMEM = pl.BlockSpec(memory_space=pltpu.VMEM)
SMEM = pl.BlockSpec(memory_space=pltpu.SMEM)
HBM = pl.BlockSpec(memory_space=pltpu.HBM)


def iota(shape, axis):
    return lax.broadcasted_iota(jnp.int32, shape, axis)


def halves(x):
    high = x.astype(BF16)
    low = (x - high.astype(F32)).astype(BF16)
    return high, low


def dot(a, b):
    return jnp.dot(a, b, preferred_element_type=F32)


def exact_dot(select, x):
    high, low = halves(x)
    return dot(select, high) + dot(select, low)


def place_of(owner, column):
    count = owner.shape[1]
    shape = (count, count)
    down, across = iota(shape, 0), iota(shape, 1)
    same = column == owner
    rank_row = jnp.sum(jnp.where(same & (down < across), 1, 0), axis=0, keepdims=True)
    rank_column = jnp.sum(jnp.where(same & (across < down), 1, 0), axis=1, keepdims=True)
    return owner * LANE + rank_row, column * LANE + rank_column


def columns_of(rows):
    rows = rows + [jnp.zeros_like(rows[0])] * (8 - len(rows))
    return jnp.concatenate(rows, axis=0).astype(F32).T.astype(jnp.int32)


def request_kernel(bits, planes, both, me, col, ask):
    n_x, n_z = planes
    first = (jnp.full((1, 1), me[0], jnp.int32) & 1) == 1
    x = col[0] // n_z
    count = both.shape[1]
    width = ask.shape[0]
    lane = iota((1, TILE), 1)
    core = jnp.where(lane < count, 0, 1)

    owner_r, block_r, owner_c, block_c, filled = [
        jnp.concatenate([both[k : k + 1, :], both[8 + k : 9 + k, :]], axis=1) for k in range(5)
    ]
    alive = lane - core * count < filled
    tags = [owner_r + core * count, owner_c + core * count]
    columns = columns_of(tags)
    earlier = iota((TILE, TILE), 0) < iota((TILE, TILE), 1)
    rank_r, rank_c = [
        jnp.sum(jnp.where((columns[:, k : k + 1] == tag) & earlier, 1, 0), axis=0, keepdims=True)
        for k, tag in enumerate(tags)
    ]
    packed = jnp.where(alive, (((owner_c << bits) + block_c) << BITS) + rank_c, -1)
    down = iota((width, TILE), 0)
    packed = jnp.where(down % n_x == x, packed, -9)
    slot = rank_r + core * HALF
    value = jnp.where((iota((TILE, TILE), 0) >> 4) == slot, jnp.where(alive, block_r + 1, 0), 0)
    there = jnp.where(down == owner_r, 1.0, 0.0).astype(BF16)
    rest = value & 15
    dims = (((1,), (1,)), ((), ()))
    total = sum(
        lax.dot_general(there, part.astype(F32).astype(BF16), dims, preferred_element_type=F32)
        for part in (value - rest, rest)
    )
    ask[...] = jnp.where(first, total.astype(jnp.int32) - 1, packed)


def local_kernel(
    bits, both, me, vector, tiles,
    pick_row, put_row, pick_col, put_col, pick_pair, mine, energy, turned,
):
    first = (jnp.full((1, 1), me[0], jnp.int32) & 1) == 0
    count = both.shape[1]
    slots = [jnp.where(first, both[k : k + 1, :], both[8 + k : 9 + k, :]) for k in (0, 2, 3)]
    live = jnp.where(first, both[4:5, 0:1], both[12:13, 0:1])
    columns = columns_of([jnp.concatenate([row, row], axis=1) for row in slots])[:count, :]
    for k, pick, put, shift in ((1, pick_row, put_row, 0), (0, pick_col, put_col, HALF)):
        width = put.shape[0]
        across, down = place_of(slots[k], columns[:, k : k + 1])
        pick[...] = jnp.where(iota((count, width), 1) == down, 1.0, 0.0).astype(BF16)
        put[...] = jnp.where(iota((width, count), 0) == across + shift, 1.0, 0.0).astype(BF16)
    ident = jnp.where(iota((count, 1), 0) < live, (columns[:, 1:2] << bits) + columns[:, 2:3], -2)
    mine[...] = jnp.broadcast_to(ident, mine.shape)
    place = place_of(slots[1], columns[:, 1:2])[1]
    high = place + (place & ~LOW) + (me[0] & 1) * LANE
    pick_pair[...] = jnp.where(iota(pick_pair.shape, 1) == high, 1.0, 0.0).astype(BF16)
    v = vector[...] * SCALE
    energy[...] = jnp.sum((v * v).reshape(-1, 8, TILE), axis=0)
    for t in range(tiles.shape[0]):
        turned[t] = tiles[t].T


def gather(asked, vector):
    pieces = vector.shape[0]
    rows = asked.shape[0]
    lanes = iota((rows, TILE), 1)
    select = jnp.concatenate(
        [jnp.where(asked == lanes + k * TILE, 1.0, 0.0).astype(BF16) for k in range(pieces // TILE)], axis=1
    )
    return exact_dot(select, vector)


def served_kernel(n_x, bits, me, pair, vector, squares, asked_row, asked_col, riders, out, energy):
    first = (jnp.full((1, 1), me[0], jnp.int32) & 1) == 0
    peers = pair.shape[0] // 2
    col = pair[peers:, :]
    for k in range(HALF):
        sides = [jnp.broadcast_to(col[:, 16 * j : 16 * j + 1], col.shape) for j in (k, k + HALF)]
        value = jnp.where(first, sides[0], sides[1])
        asked_col[pl.ds(k, peers, LANE), :] = value
        asked_col[pl.ds(k + HALF, peers, LANE), :] = value
    chips = peers // n_x
    row = pair[pl.ds(0, chips, n_x), :]
    for x in range(1, n_x):
        row = jnp.maximum(row, pair[pl.ds(x, chips, n_x), :])
    riders[...] = row
    down = iota((2 * LANE, TILE), 0)
    side = jnp.where(iota((2 * LANE, TILE), 1) < TILE // 2, 0, 1) == (down >> BITS)
    parts = []
    for k in range(chips):
        rider = row[k : k + 1, :]
        here = ((rider >> (bits + BITS)) == me[0]) & ((rider & LOW) == (down & LOW)) & side
        value = jnp.where(here, ((rider >> BITS) & ((1 << bits) - 1)) + 1, 0).astype(F32)
        parts.append(jnp.sum(value, axis=1, keepdims=True))
    asked = jnp.broadcast_to(jnp.concatenate(parts, axis=0), asked_row.shape).astype(jnp.int32) - 1
    asked_row[...] = asked
    out[...] = gather(asked, vector[...] * SCALE)
    energy[...] = jnp.sum(squares[...], axis=0, keepdims=True)


def returned_rows(x):
    pairs = x.reshape(-1, 2, LANE, TILE)
    return jnp.concatenate([pairs[:, 0, HALF:, :], pairs[:, 1, HALF:, :]], axis=1).reshape(-1, TILE)


def laid_twice(x):
    halves_of = [x.reshape(-1, LANE, TILE)[:, k : k + HALF, :] for k in (0, HALF)]
    pairs = [jnp.concatenate([half, half], axis=1) for half in halves_of]
    return jnp.stack(pairs, axis=1).reshape(-1, TILE)


def product_lane(asked_row, asked_col):
    rows = [asked_row[...].astype(F32).T[0:1, :]]
    width = asked_col.shape[0]
    for k in range(width // TILE):
        part = asked_col[k * TILE : (k + 1) * TILE, :].astype(F32).T[0:1, :]
        lane = iota((1, TILE), 1)
        rows.append(jnp.where((lane & LOW) >= HALF, part, -2.0))
    return [row.astype(jnp.int32) for row in rows]


def meet_tables(bits, asked_row, asked_col, mine, riders, me, meet, link, link_col, owned):
    lanes = product_lane(asked_row, asked_col)
    base = 0
    served_row, served_col = asked_row[...], asked_col[...]
    for served in (served_row, served_col):
        for k, lane in enumerate(lanes):
            hit = (served == lane) & (served >= 0)
            meet[base : base + served.shape[0], k * TILE : (k + 1) * TILE] = jnp.where(hit, 1.0, 0.0).astype(BF16)
        base += served.shape[0]
    ident = returned_rows(served_col)
    ident = jnp.where(ident < 0, -3, ident + (me[0] << bits))
    slot = iota(owned.shape[:1] + (TILE,), 0)
    half = jnp.where(iota(owned.shape[:1] + (TILE,), 1) < mine.shape[0], 0, 1)
    for k in range(riders.shape[0]):
        rider = riders[k : k + 1, :]
        ids = rider >> BITS
        cols = slice(k * TILE, (k + 1) * TILE)
        link[:, cols] = jnp.where(mine[...] == ids, 1.0, 0.0).astype(BF16)
        link_col[:, cols] = jnp.where(ident == ids, 1.0, 0.0).astype(BF16)
        sent = ((rider >> (bits + BITS)) == me[0]) & ((rider & LOW) == (slot & LOW))
        sent = sent & ((slot >> BITS) == 2 * k + half)
        owned[:, cols] = jnp.where(sent, 1.0, 0.0).astype(BF16)


def multiply(x, tiles):
    count = x.shape[0]
    row = iota((16, TILE), 0) & 7
    groups = []
    for g in range(count // 8):
        part = x[g * 8 : (g + 1) * 8, :]
        high = part.astype(BF16).astype(F32)
        both = jnp.concatenate([high, part - high], axis=0)
        apart = jnp.concatenate([jnp.where(row == j, both, 0.0).astype(BF16) for j in range(8)], axis=1)
        y = dot(apart, tiles[g * 8 : (g + 1) * 8].reshape(8 * TILE, TILE))
        groups.append(y[0:8] + y[8:16])
    return jnp.concatenate(groups, axis=0)


def direct_kernel(
    bits, me, got, pick, tiles, put, asked_row, asked_col, mine, riders, vector,
    out, v_col, meet, link, link_col, owned,
):
    y = multiply(exact_dot(pick[...], got[...]), tiles)
    v = laid_twice(gather(returned_rows(asked_col[...]), vector[...] * SCALE))
    v_col[...] = v
    forward = (iota(v.shape, 0) & LOW) < HALF
    out[...] = exact_dot(put[...], y) + jnp.where(forward, v, 0.0)
    meet_tables(bits, asked_row, asked_col, mine, riders, me, meet, link, link_col, owned)


def mirror_kernel(got, pick, tiles, put, meet, out):
    y = multiply(exact_dot(pick[...], got[...]), tiles)
    high, low = halves(y)
    width = put.shape[0]
    total = exact_dot(meet[:width, width:], got[...])
    total, low = total.astype(BF16), dot(put[...], low).astype(BF16)
    count = y.shape[0]
    for k in range(out.shape[0]):
        rows = slice(2 * k * LANE, 2 * (k + 1) * LANE)
        out[k, :count, :] = high
        out[k, count : count + 2 * LANE, :] = total[rows]
        out[k, count + 2 * LANE :, :] = low[rows]


def second_direct_kernel(me, got, link, link_col, owned, pick, meet, first_col, tiles, put, out, first_row):
    count = link.shape[0]
    chips = got.shape[0] // 2
    peers = [core * chips + chip for chip in range(chips) for core in range(2)]
    middle = count + 2 * LANE
    mirrors = jnp.concatenate([got[k, :count, :] for k in peers], axis=0)
    sums = jnp.concatenate([got[k, count:middle, :] for k in peers], axis=0)
    lows = jnp.concatenate([got[k, middle:, :] for k in peers], axis=0)
    y = multiply(dot(link[...], mirrors) + dot(pick[...], sums), tiles)
    width = got.shape[0] * LANE
    image = laid_twice(dot(link_col[...], mirrors)) + exact_dot(meet[width:, width:], first_col[...])
    forward = (iota(image.shape, 0) & LOW) < HALF
    out[...] = exact_dot(put[...], y) + jnp.where(forward, image, 0.0)
    slot = iota((width, 2 * width), 0)
    low = iota((width, 2 * width), 1) == slot + (slot & ~LOW) + (me[0] & 1) * LANE
    first_row[...] = dot(owned[...], mirrors) + dot(jnp.where(low, 1.0, 0.0).astype(BF16), lows)


def second_mirror_kernel(got, pick, tiles, put, out):
    out[...] = exact_dot(put[...], multiply(exact_dot(pick[...], got[...]), tiles))


def inner_kernel(meet, energy, v_row, v_col, first_row, second_row, first_col, second_col, out):
    first_r, second_r = first_row[...], second_row[...]
    first = jnp.concatenate([first_r, first_col[...]], axis=0)
    second = jnp.concatenate([second_r, second_col[...]], axis=0)
    both = exact_dot(meet[...], jnp.concatenate([first, second], axis=1))
    image, total = both[:, :TILE], both[:, TILE:]
    width = v_row.shape[0]
    returned = (iota(v_col.shape, 0) & LOW) >= HALF
    first_c = jnp.where(returned, first_col[...], 0.0)
    second_c = jnp.where(returned, second_col[...], 0.0)

    def inner(a_r, b_r, a_c, b_c):
        return jnp.sum(a_r * b_r, axis=0, keepdims=True) + jnp.sum(a_c * b_c, axis=0, keepdims=True)

    values = [
        energy[...],
        inner(v_row[...], first_r, v_col[...], first_c),
        inner(image[:width], first_r, image[width:], first_c),
        inner(v_row[...], second_r, v_col[...], second_c),
        inner(image[:width], second_r, image[width:], second_c),
        inner(total[:width], second_r, total[width:], second_c),
    ]
    packed = jnp.concatenate(values + [jnp.zeros((2, TILE), F32)], axis=0)
    for k in range(out.shape[0]):
        out[k] = packed


def partial_kernel(got, out):
    total = jnp.sum(got[...], axis=0)
    sums = jnp.sum(total, axis=1, keepdims=True)
    packed = jnp.sum(jnp.where(iota(total.shape, 0) == iota(total.shape, 1), sums, 0.0), axis=0, keepdims=True)
    out[...] = jnp.broadcast_to(packed, out.shape)


def final_kernel(
    total, got, vector, asked_row, asked_col, first_row, second_row, first_col, second_col,
    out, alpha, rest, near, sems,
):
    sums = jnp.sum(got[...], axis=0, keepdims=True)
    lane = iota((1, TILE), 1)

    def value(k):
        return jnp.sum(jnp.where(lane == k, sums, 0.0), axis=1, keepdims=True)

    vv, vi, ii, vw, iw, ww = [value(k) for k in range(6)]
    share = 1.0 / total
    g = lax.rsqrt(vv * (share / (SCALE * SCALE)) + 1e-06) * (1.0 / SCALE)
    c0 = g * (g * vi * share)
    square = g * (g * (ii - 2.0 * c0 * vi + c0 * c0 * vv) * share)
    square = jnp.maximum(square, 0.0) + 1e-06
    root = lax.rsqrt(square)
    b0 = square * root
    h = g * root
    c10 = h * (g * (vw - c0 * vi) * share)
    c11 = h * (h * (iw - c0 * ii - c0 * vw + c0 * c0 * vi) * share)
    a = c0 + c11
    b = c11 * c0 - c10 * b0
    square = h * (h * (ww + a * a * ii + b * b * vv - 2.0 * a * iw + 2.0 * b * vw - 2.0 * a * b * vi) * share)
    square = jnp.maximum(square, 0.0) + 1e-06
    root = lax.rsqrt(square)
    b1 = square * root
    f = h * root
    parts = sems.shape[0]
    step = vector.shape[0] // parts
    asked = [asked_row[...], returned_rows(asked_col[...])]
    lanes = jnp.concatenate([x.astype(F32).T[0:1, :].astype(jnp.int32) for x in asked], axis=1)
    image = jnp.concatenate([first_row[...], returned_rows(first_col[...])], axis=0)
    second = jnp.concatenate([second_row[...], returned_rows(second_col[...])], axis=0)
    high, low = halves(jnp.concatenate([image, second], axis=1))
    copies = []
    for k in range(parts):
        v = vector[pl.ds(k * step, step), :]
        place = iota((step, lanes.shape[1]), 0) + k * step
        select = jnp.where(place == lanes, 1.0, 0.0).astype(BF16)
        both = dot(select, high) + dot(select, low)
        i, w = both[:, :TILE], both[:, TILE:]
        near[pl.ds(2 * k * step, step, 2), :] = h * i - (h * c0 * SCALE) * v
        near[pl.ds(2 * k * step + 1, step, 2), :] = f * w - (f * a) * i + (f * b * SCALE) * v
        done = pl.ds(2 * k * step, 2 * step)
        copies.append(pltpu.make_async_copy(near.at[done], out.at[done], sems.at[k]))
        copies[-1].start()
    alpha[0] = c0[0, 0]
    rest[0] = b0[0, 0]
    rest[1] = c11[0, 0]
    rest[2] = b1[0, 0]
    for copy in copies:
        copy.wait()


def shape(*dims, dtype=F32):
    return jax.ShapeDtypeStruct(dims, dtype)


def call(kernel, outs, *args, ins=VMEM, out_specs=VMEM, scratch=(), limit=16):
    if isinstance(outs, tuple) and not isinstance(out_specs, tuple):
        out_specs = tuple([out_specs] * len(outs))
    return pl.pallas_call(
        kernel,
        out_shape=outs,
        in_specs=ins if isinstance(ins, list) else [ins] * len(args),
        out_specs=out_specs,
        scratch_shapes=scratch,
        compiler_params=pltpu.CompilerParams(vmem_limit_bytes=limit * 1024 * 1024),
    )(*args)


def exchange(x, axis, count):
    sent = x.reshape(count, -1, TILE)
    got = lax.all_to_all(sent, axis, split_axis=0, concat_axis=0, tiled=True)
    return got.reshape(x.shape)


def per_device(start_vector, tile_blocks, row_owner, row_block, col_owner, col_block, tile_counts):
    tiles = tile_blocks[0, 0]
    count = tiles.shape[0]
    vector = start_vector.reshape(-1, TILE)
    pieces = vector.shape[0]
    n_row, n_col = lax.axis_size("row"), lax.axis_size("col")
    wide_r, wide_c = n_row * LANE, n_col * LANE
    every = wide_r + wide_c
    total = float(pieces * TILE * n_row * n_col)

    def over_row(x):
        return exchange(x, "row", n_row)

    def over_col(x):
        return exchange(x, "col", n_col)

    bits = (pieces - 1).bit_length()
    n_y = n_row // 2
    n_x = n_col // n_y
    n_z = n_col // n_x
    planes = [[(2 * y + 1) * n_col + c for c in range(n_col)] for y in range(n_y)]
    planes += [[2 * y * n_col + x * n_z + z for y in range(n_y) for x in range(n_x)] for z in range(n_z)]
    chips = [[2 * y, 2 * y + 1] for y in range(n_y)]

    def over_chip(x):
        return lax.all_gather(x, "row", axis_index_groups=chips, tiled=True)

    slots = [row_owner, row_block, col_owner, col_block, tile_counts] + [jnp.zeros((), jnp.int32)] * 3
    slots = jnp.concatenate([jnp.broadcast_to(x.reshape(1, -1), (1, count)) for x in slots], axis=0)
    both = over_chip(slots)
    me, col = lax.axis_index("row").reshape(1), lax.axis_index("col").reshape(1)
    ask = call(
        functools.partial(request_kernel, bits, (n_x, n_z)),
        shape(n_col, TILE, dtype=jnp.int32),
        both,
        me,
        col,
        ins=[VMEM] + [SMEM] * 2,
    )
    ask = lax.all_to_all(
        ask.reshape(n_col, 1, TILE),
        ("row", "col"),
        split_axis=0,
        concat_axis=0,
        axis_index_groups=planes,
        tiled=True,
    ).reshape(n_col, TILE)
    pick_row, put_row, pick_col, put_col, pick_pair, mine, squares, turned = call(
        functools.partial(local_kernel, bits),
        (
            shape(count, wide_r, dtype=BF16),
            shape(wide_r, count, dtype=BF16),
            shape(count, wide_c, dtype=BF16),
            shape(wide_c, count, dtype=BF16),
            shape(count, 2 * wide_r, dtype=BF16),
            shape(count, TILE, dtype=jnp.int32),
            shape(8, TILE),
            shape(*tiles.shape, dtype=BF16),
        ),
        both,
        me,
        vector,
        tiles,
        ins=[VMEM, SMEM] + [VMEM] * 2,
    )
    asked_row, asked_col, riders, v_row, energy = call(
        functools.partial(served_kernel, n_x, bits),
        (
            shape(wide_r, TILE, dtype=jnp.int32),
            shape(wide_c, TILE, dtype=jnp.int32),
            shape(n_y, TILE, dtype=jnp.int32),
            shape(wide_r, TILE),
            shape(1, TILE),
        ),
        me,
        over_chip(ask),
        vector,
        squares,
        ins=[SMEM] + [VMEM] * 3,
    )
    x_col = over_row(v_row)
    first_col, v_col, meet, link, link_col, owned = call(
        functools.partial(direct_kernel, bits),
        (
            shape(wide_c, TILE),
            shape(wide_c, TILE),
            shape(every, every, dtype=BF16),
            shape(count, n_row * count, dtype=BF16),
            shape(wide_c // 2, n_row * count, dtype=BF16),
            shape(wide_r, n_row * count, dtype=BF16),
        ),
        me,
        x_col,
        pick_row,
        turned,
        put_col,
        asked_row,
        asked_col,
        mine,
        riders,
        vector,
        ins=[SMEM] + [VMEM] * 9,
    )
    first_col = over_col(first_col)
    packed = call(
        mirror_kernel,
        shape(n_y, count + 4 * LANE, TILE, dtype=BF16),
        first_col,
        pick_col,
        tiles,
        put_row,
        meet,
    )
    cores = [[2 * y + core for y in range(n_y)] for core in range(2)]
    packed = lax.all_to_all(packed, "row", split_axis=0, concat_axis=0, axis_index_groups=cores, tiled=True)
    second_col, first_row = call(
        second_direct_kernel,
        (shape(wide_c, TILE), shape(wide_r, TILE)),
        me,
        over_chip(packed),
        link,
        link_col,
        owned,
        pick_pair,
        meet,
        first_col,
        turned,
        put_col,
        ins=[SMEM] + [VMEM] * 9,
    )
    second_col = over_col(second_col)
    second_row = over_row(
        call(second_mirror_kernel, shape(wide_r, TILE), second_col, pick_col, tiles, put_row)
    )
    products = (first_row, second_row, first_col, second_col)
    inner = call(inner_kernel, shape(n_row, 8, TILE), meet, energy, v_row, v_col, *products)
    inner = over_row(inner)
    inner = over_col(call(partial_kernel, shape(n_col, TILE), inner))

    def finish(*refs):
        final_kernel(total, *refs)

    out, alpha, rest = call(
        finish,
        (shape(2 * pieces, TILE), shape(1), shape(3)),
        inner,
        vector,
        asked_row,
        asked_col,
        *products,
        out_specs=(HBM, SMEM, SMEM),
        scratch=[pltpu.VMEM((2 * pieces, TILE), F32), pltpu.SemaphoreType.DMA((8,))],
    )
    basis = out.reshape(pieces, 2, TILE).transpose(1, 0, 2).reshape(2, pieces * TILE)
    return (basis, alpha, rest)


def solution(mesh):
    return jax.shard_map(
        per_device,
        mesh=mesh,
        in_specs=(
            P(("row", "col")),
            P("row", "col", None, None, None),
            P("row", "col", None, None),
            P("row", "col", None),
            P("row", "col", None, None),
            P("row", "col", None),
            P("row", "col"),
        ),
        out_specs=(P(None, ("row", "col")), P(), P()),
        check_vma=False,
    )
```
